32 devices in a mesh: dp: 16 (over z, y, core), tensor: 2 (over x).
Axes of the slice: x: 2, y: 2, z: 4, core: 2. Of those that a mesh axis runs over, the one named last changes fastest.
Arguments:
- tokens: bfloat16 [20480, 768], P(('dp', 'tensor')), may hold values from -6 to 6
- conditioning: bfloat16 [80, 768], P('dp'), may hold values from -6 to 6
- segment_ids: int32 [20480], P('dp'), may hold values from 0 to 4, as said below
- kept_rows: int32 [10240], P('dp'), may hold values from 0 to 1279, as said below
- cotangent: bfloat16 [20480, 768], P(('dp', 'tensor')), may hold values from -6 to 6
- mod_first: bfloat16 [768, 4608], replicated, may hold values from -0.21875 to 0.21875
- qkv_first: bfloat16 [768, 3, 768], P(None, None, 'tensor'), may hold values from -0.21875 to 0.21875
- proj_first: bfloat16 [768, 768], P('tensor'), may hold values from -3 to 3
- up_first: bfloat16 [768, 3072], P(None, 'tensor'), may hold values from -0.21875 to 0.21875
- down_first: bfloat16 [3072, 768], P('tensor'), may hold values from -0.109375 to 0.109375
- mod_second: bfloat16 [768, 4608], replicated, may hold values from -0.21875 to 0.21875
- qkv_second: bfloat16 [768, 3, 768], P(None, None, 'tensor'), may hold values from -0.21875 to 0.21875
- proj_second: bfloat16 [768, 768], P('tensor'), may hold values from -3 to 3
- up_second: bfloat16 [768, 3072], P(None, 'tensor'), may hold values from -0.21875 to 0.21875
- down_second: bfloat16 [3072, 768], P('tensor'), may hold values from -0.109375 to 0.109375
Outputs:
- first_out: bfloat16 [20480, 768], P(('dp', 'tensor'))
- routed_out: bfloat16 [20480, 768], P(('dp', 'tensor'))
- input_grad: float32 [20480, 768], P(('dp', 'tensor'))
- grad_mod_first: float32 [768, 4608], P(('dp', 'tensor'))
- grad_qkv_first: float32 [768, 3, 768], P('dp', None, 'tensor')
- grad_proj_first: float32 [768, 768], P('tensor', 'dp')
- grad_up_first: float32 [768, 3072], P('dp', 'tensor')
- grad_down_first: float32 [3072, 768], P('tensor', 'dp')
- grad_mod_second: float32 [768, 4608], P(('dp', 'tensor'))
- grad_qkv_second: float32 [768, 3, 768], P('dp', None, 'tensor')
- grad_proj_second: float32 [768, 768], P('tensor', 'dp')
- grad_up_second: float32 [768, 3072], P('dp', 'tensor')
- grad_down_second: float32 [3072, 768], P('tensor', 'dp')
The draws below stay inside these ranges and needn't reach their ends.
Inputs may be any that keep to these rules, and one draw needn't show every extreme that they name: `segment_ids`: in each aligned block of 1280 tokens (one packed group) the ids number its sequences from 0 and never fall; a group is either one sequence of 1024 and one of 256 tokens, in either order, or five sequences of 256 tokens. `kept_rows`: each aligned block of 640 entries lists, in ascending order, distinct positions within one packed group: exactly half of the positions of each of its sequences.
All inputs are finite; a program needn't handle non-finite values.
Results may differ from the reference program's by a relative error of at most 0.035.
Values may be sent and summed in bfloat16 or wider, within the bound.
No kernel may reach another device: no remote copies, remote signals or barrier semaphores. Data moves between devices by JAX's collectives and lax.ppermute only.
A program may use at most 320 MiB of HBM per device.

```python
import jax
import jax.numpy as jnp
from jax import lax

D = 768
HEADS = 12
HEAD_DIM = 64
FF = 3072
SLOTS = 5
SHORT = 256
GROUPS_DEV = 1
LONG = 1024
GROUP = 1280
KEEP = 640
TOKENS = 20480
CONDS = 80
N_DP = 16
N_TENSOR = 2


def group_kinds(key):
    group_count = N_DP * GROUPS_DEV
    kind_ids = jax.random.randint(jax.random.fold_in(key, 1), (group_count,), 0, 3)
    pick_order = jax.random.permutation(jax.random.fold_in(key, 2), group_count)
    return kind_ids.at[pick_order[:3]].set(jnp.arange(3, dtype=jnp.int32))


def segment_table(kind_ids):
    positions = jnp.arange(GROUP, dtype=jnp.int32)[None, :]
    kinds_col = kind_ids[:, None]
    long_first = (positions >= LONG).astype(jnp.int32)
    short_first = (positions >= SHORT).astype(jnp.int32)
    all_short = positions // SHORT
    return jnp.where(kinds_col == 0, long_first, jnp.where(kinds_col == 1, short_first, all_short)).astype(jnp.int32)


def draw_segment_ids(key, part):
    segment_index = segment_table(group_kinds(key))
    return segment_index.reshape(-1)


def draw_kept_rows(key, part):
    segment_index = segment_table(group_kinds(key))
    key = jax.random.fold_in(key, 17)
    group_count = segment_index.shape[0]
    noise_rank = jax.vmap(lambda sub_key: jax.random.permutation(sub_key, GROUP))(jax.random.split(key, group_count)).astype(jnp.int32)
    sort_order = jnp.argsort(segment_index * GROUP + noise_rank, axis=1).astype(jnp.int32)
    sorted_seg = jnp.take_along_axis(segment_index, sort_order, axis=1)
    slot_ids = jnp.arange(SLOTS, dtype=jnp.int32)
    starts = jnp.sum((segment_index[:, None, :] < slot_ids[None, :, None]).astype(jnp.int32), axis=2)
    lengths = jnp.sum((segment_index[:, None, :] == slot_ids[None, :, None]).astype(jnp.int32), axis=2)
    within = jnp.arange(GROUP, dtype=jnp.int32)[None, :] - jnp.take_along_axis(starts, sorted_seg, axis=1)
    chosen_sorted = (within < jnp.take_along_axis(lengths, sorted_seg, axis=1) // 2).astype(jnp.int32)
    inverse = jnp.argsort(sort_order, axis=1).astype(jnp.int32)
    chosen = jnp.take_along_axis(chosen_sorted, inverse, axis=1)
    positions = jnp.arange(GROUP, dtype=jnp.int32)[None, :]
    picked = jnp.argsort((1 - chosen) * GROUP + positions, axis=1)[:, :KEEP]
    return picked.astype(jnp.int32).reshape(-1)


def block_scale(key, dims, cuts, least, largest):
    factor_of, own = 1.0, jax.random.fold_in(key, 6)
    for dim, blocks in cuts:
        steps = jnp.exp(jax.random.uniform(jax.random.fold_in(own, dim), (blocks,), jnp.float32, least / len(cuts), largest / len(cuts)))
        factor_of = factor_of * jnp.repeat(steps, dims[dim] // blocks).reshape([-1 if axis == dim else 1 for axis in range(len(dims))])
    return factor_of


def centred(rng, dims, scale, most, cuts=(), kind=jnp.bfloat16):
    loudness = block_scale(rng, dims, cuts, -0.22, 0.18) if cuts else 1.0
    values = jax.random.normal(rng, dims, jnp.float32) * scale * loudness
    return jnp.minimum(jnp.maximum(values, -most), most).astype(kind)


def setup_inputs(seed: int = 0) -> dict:
    arg_keys = jax.random.split(jax.random.key(seed), 16)
    tokens = centred(arg_keys[0], (TOKENS, D), 1.0, 6.0, ((0, 32),))
    conditioning = centred(arg_keys[1], (CONDS, D), 1.0, 6.0, ((0, 16),))
    segment_ids = draw_segment_ids(jax.random.fold_in(arg_keys[15], 71), 0)
    kept_rows = draw_kept_rows(jax.random.fold_in(arg_keys[15], 71), 0)
    cotangent = centred(arg_keys[4], (TOKENS, D), 1.0, 6.0, ((0, 32),))
    mod_first = centred(arg_keys[5], (D, 6 * D), D ** -0.5, 0.21875)
    qkv_first = centred(arg_keys[6], (D, 3, D), D ** -0.5, 0.21875, ((2, 2),))
    proj_first = centred(arg_keys[7], (D, D), 4 ** -0.5, 3.0, ((0, 2),))
    up_first = centred(arg_keys[8], (D, FF), D ** -0.5, 0.21875, ((1, 2),))
    down_first = centred(arg_keys[9], (FF, D), FF ** -0.5, 0.109375, ((0, 2),))
    mod_second = centred(arg_keys[10], (D, 6 * D), D ** -0.5, 0.21875)
    qkv_second = centred(arg_keys[11], (D, 3, D), D ** -0.5, 0.21875, ((2, 2),))
    proj_second = centred(arg_keys[12], (D, D), 4 ** -0.5, 3.0, ((0, 2),))
    up_second = centred(arg_keys[13], (D, FF), D ** -0.5, 0.21875, ((1, 2),))
    down_second = centred(arg_keys[14], (FF, D), FF ** -0.5, 0.109375, ((0, 2),))
    return {"tokens": tokens, "conditioning": conditioning, "segment_ids": segment_ids, "kept_rows": kept_rows, "cotangent": cotangent, "mod_first": mod_first, "qkv_first": qkv_first, "proj_first": proj_first, "up_first": up_first, "down_first": down_first, "mod_second": mod_second, "qkv_second": qkv_second, "proj_second": proj_second, "up_second": up_second, "down_second": down_second}


NORM_EPS = 1e-06
HIGHEST = lax.Precision.HIGHEST

@jax.custom_vjp
def low(v):
    return lax.optimization_barrier(v.astype(jnp.bfloat16)).astype(jnp.float32)

@jax.custom_vjp
def low_back(v):
    return v

def low_keep(v):
    return (low(v), None)

def low_pass(kept, grad):
    return (grad,)

def back_keep(v):
    return (v, None)

def back_low(kept, grad):
    return (low(grad),)
low.defvjp(low_keep, low_pass)
low_back.defvjp(back_keep, back_low)

def modulate(value_rows, shift_rows, scale_rows):
    centre = value_rows - lax.optimization_barrier(jnp.mean(value_rows, axis=-1, keepdims=True))
    spread_sq = lax.optimization_barrier(jnp.mean(centre * centre, axis=-1, keepdims=True))
    return centre * lax.rsqrt(spread_sq + NORM_EPS) * (1.0 + scale_rows) + shift_rows

def matmul(left, right):
    return jnp.dot(left, right, precision=HIGHEST)

def halves_sum(left, weight):
    width = left.shape[1] // N_TENSOR
    total = jnp.zeros((left.shape[0], weight.shape[1]), jnp.float32)
    for index in range(N_TENSOR):
        total = total + low(matmul(left[:, index * width:(index + 1) * width], weight[index * width:(index + 1) * width]))
    return total

def diffusion_block(value_rows, segment_index, slot_embedding, weight_set):
    w_mod, w_qkv, w_proj, w_up, w_down = weight_set
    mod_table = matmul(low(jax.nn.silu(slot_embedding)), w_mod).reshape(SLOTS, 6, D)
    per_token = mod_table[segment_index]
    normed = low(modulate(value_rows, per_token[:, 0], per_token[:, 1]))
    width = D // N_TENSOR
    head_part = HEADS // N_TENSOR
    pieces = []
    for index in range(N_TENSOR):
        weight_part = w_qkv[:, :, index * width:(index + 1) * width].reshape(D, 3 * width)
        piece = low_back(low(matmul(low_back(normed), weight_part)))
        pieces.append(piece.reshape(-1, 3, head_part, HEAD_DIM))
    projected = jnp.concatenate(pieces, axis=2)
    scores = jnp.einsum('qhd,khd->hqk', projected[:, 0], projected[:, 1], precision=HIGHEST) * HEAD_DIM ** (-0.5)
    scores = low_back(scores)
    same_seq = segment_index[:, None] == segment_index[None, :]
    scores = jnp.where(same_seq[None], scores, -1e+30)
    shifted = jnp.exp(scores - lax.optimization_barrier(jnp.max(scores, axis=-1, keepdims=True)))
    att_weights = low(shifted / lax.optimization_barrier(jnp.sum(shifted, axis=-1, keepdims=True)))
    mixed_rows = jnp.einsum('hqk,khd->qhd', att_weights, projected[:, 2], precision=HIGHEST).reshape(-1, D)
    mixed_rows = low_back(low(mixed_rows))
    attn_out = low_back(halves_sum(mixed_rows, w_proj))
    middle = value_rows + per_token[:, 2] * attn_out
    normed_two = low(modulate(middle, per_token[:, 3], per_token[:, 4]))
    hidden_part = FF // N_TENSOR
    up_pieces = []
    for index in range(N_TENSOR):
        up_pieces.append(low_back(matmul(low_back(normed_two), w_up[:, index * hidden_part:(index + 1) * hidden_part])))
    up_proj = jnp.concatenate(up_pieces, axis=1)
    activated = low(jax.nn.gelu(up_proj, approximate=True))
    mlp_out = low_back(halves_sum(activated, w_down))
    return middle + per_token[:, 5] * mlp_out

def two_blocks(parameters, value_rows, segment_index, retained_positions, slot_embedding):
    leading_rows = diffusion_block(value_rows, segment_index, slot_embedding, parameters[:5])
    routed_tokens = low(leading_rows)
    second_block = diffusion_block(routed_tokens[retained_positions], segment_index[retained_positions], slot_embedding, parameters[5:])
    return (routed_tokens.at[retained_positions].set(second_block), leading_rows)

def reference(tokens, conditioning, segment_ids, kept_rows, cotangent, mod_first, qkv_first, proj_first, up_first, down_first, mod_second, qkv_second, proj_second, up_second, down_second):
    parameters = tuple((weight.astype(jnp.float32) for weight in (mod_first, qkv_first, proj_first, up_first, down_first, mod_second, qkv_second, proj_second, up_second, down_second)))
    groups = N_DP * GROUPS_DEV
    group_items = (tokens.astype(jnp.float32).reshape(groups, GROUP, D), segment_ids.reshape(groups, GROUP), kept_rows.reshape(groups, KEEP), conditioning.astype(jnp.float32).reshape(groups, SLOTS, D), cotangent.astype(jnp.float32).reshape(groups, GROUP, D))

    def group_step(totals, group_item):
        value_rows, segment_index, retained_positions, slot_embedding, grad_rows = group_item
        routed_rows, pullback, leading_rows = jax.vjp(lambda weight_set, inputs: two_blocks(weight_set, inputs, segment_index, retained_positions, slot_embedding), parameters, value_rows, has_aux=True)
        grad_params, grad_values = pullback(grad_rows)
        totals = tuple((summed + addend for summed, addend in zip(totals, grad_params)))
        return (totals, (leading_rows.astype(jnp.bfloat16), routed_rows.astype(jnp.bfloat16), grad_values))
    start_totals = tuple((jnp.zeros(weight.shape, jnp.float32) for weight in parameters))
    totals, rows_out = lax.scan(group_step, start_totals, group_items)
    first_out = rows_out[0].reshape(TOKENS, D)
    routed_out = rows_out[1].reshape(TOKENS, D)
    input_grad = rows_out[2].reshape(TOKENS, D)
    return (first_out, routed_out, input_grad, totals[0], totals[1], totals[2], totals[3], totals[4], totals[5], totals[6], totals[7], totals[8], totals[9])
```

```python
import functools

import jax
import jax.numpy as jnp
from jax import lax
from jax.experimental import pallas as pl
from jax.experimental.pallas import tpu as pltpu
from jax.sharding import PartitionSpec as P

D = 768
HEAD_DIM = 64
SLOTS = 5
GROUP = 1280
KEEP = 640
BLOCKS = 5
SPAN = GROUP // BLOCKS
HALF = D // 2
TILE = 768
NORM_EPS = 1e-06
f32 = jnp.float32
bf16 = jnp.bfloat16
ALL = ("dp", "tensor")
VMEM_BYTES = 60 * 1024 * 1024


def dot(left, right):
    return jnp.dot(left, right, preferred_element_type=f32)


def dot_cols(left, right):
    return lax.dot_general(left, right, (((1,), (1,)), ((), ())), preferred_element_type=f32)


def dot_rows(left, right):
    return lax.dot_general(left, right, (((0,), (0,)), ((), ())), preferred_element_type=f32)


def unit_rows(rows):
    centre = rows - jnp.mean(rows, axis=-1, keepdims=True)
    inverse = lax.rsqrt(jnp.mean(centre * centre, axis=-1, keepdims=True) + NORM_EPS)
    return centre * inverse, inverse


def norm_back(d_normed, unit, inverse, scale_row):
    e = d_normed * (1.0 + scale_row)
    return inverse * (
        e
        - jnp.mean(e, axis=-1, keepdims=True)
        - unit * jnp.mean(e * unit, axis=-1, keepdims=True)
    )


def col_sum(rows):
    return jnp.sum(rows, axis=0, keepdims=True)


def flat(ref):
    value = ref[...]
    return value.reshape(-1, value.shape[-1])


def whole(shape):
    return pl.BlockSpec(shape, lambda *_: (0,) * len(shape))


def run(body, grid, ins, outs, scratch=(), scalars=(), flops=0):
    in_specs = [whole(a.shape) if s is None else s for a, s in ins]
    out_specs = [whole(sh) if s is None else s for sh, _, s in outs]
    moved = sum(a.size * a.dtype.itemsize for a, _ in ins)
    moved += sum(jnp.dtype(d).itemsize * functools.reduce(lambda p, q: p * q, sh, 1) for sh, d, _ in outs)
    return pl.pallas_call(
        body,
        grid_spec=pltpu.PrefetchScalarGridSpec(
            num_scalar_prefetch=len(scalars),
            grid=grid,
            in_specs=in_specs,
            out_specs=out_specs,
            scratch_shapes=list(scratch),
        ),
        out_shape=[jax.ShapeDtypeStruct(sh, d) for sh, d, _ in outs],
        compiler_params=pltpu.CompilerParams(
            vmem_limit_bytes=VMEM_BYTES, dimension_semantics=("arbitrary",) * len(grid)
        ),
        cost_estimate=pl.CostEstimate(flops=int(flops), bytes_accessed=int(moved), transcendentals=0),
    )(*scalars, *[a for a, _ in ins])


def qkv_body(own, oth, tab, w, normed, q, k, v):
    rows = own.shape[1]
    step = pl.program_id(0)

    @pl.when(step == 0)
    def _():
        for side, src in ((0, own), (1, oth)):
            for i in range(BLOCKS):
                unit, _ = unit_rows(src[i].astype(f32))
                normed[side, i] = (unit * (1.0 + tab[i, 1:2]) + tab[i, 0:1]).astype(bf16)

    qkv_steps(step, normed, w, q, k, v, rows)


def qkv_next_body(normed, w, q, k, v):
    qkv_steps(pl.program_id(0), normed, w, q, k, v, normed.shape[2])


def qkv_steps(step, normed, w, q, k, v, rows):
    @pl.when(step == 0)
    def _():
        mine = normed[0].reshape(BLOCKS * rows, D)
        q[...] = dot(mine, w[0]).astype(bf16).reshape(q.shape)

    for index, out in ((1, k), (2, v)):

        @pl.when(step == index)
        def _(out=out):
            out[...] = dot(flat(normed), w[0]).astype(bf16).reshape(out.shape)


def project_qkv(first, own, oth, tab, normed, w):
    if first:
        rows = own.shape[1]
        ins = [(own, None), (oth, None), (tab, None)]
        outs = [((2, BLOCKS, rows, D), bf16, None)]
        body = qkv_body
    else:
        rows = normed.shape[2]
        ins = [(normed, None)]
        outs = []
        body = qkv_next_body
    ins += [(w, pl.BlockSpec((1, D, HALF), lambda j: (j, 0, 0)))]
    outs += [
        ((BLOCKS, rows, HALF), bf16, None),
        ((2, BLOCKS, rows, HALF), bf16, None),
        ((2, BLOCKS, rows, HALF), bf16, None),
    ]
    return run(body, (3,), ins, outs, flops=2 * 25 * rows * D * HALF)


def by_sequence(kind, one_sequence, long_tiles):
    @pl.when(kind < 2)
    def _():
        one_sequence(kind, 4, long_tiles)
        one_sequence(jnp.where(kind == 0, 4, 0), 1, 1)

    @pl.when(kind == 2)
    def _():
        def short(i, carry):
            one_sequence(i, 1, 1)
            return carry

        lax.fori_loop(0, BLOCKS, short, 0)


def two_heads(rows, low):
    zero = jnp.zeros_like(rows)
    return jnp.concatenate([jnp.where(low, rows, zero), jnp.where(low, zero, rows)], axis=0)


def attend_body(kind, q, k, v, out):
    rows = q.shape[1]
    low = lax.broadcasted_iota(jnp.int32, (1, 128), 1) < HEAD_DIM
    scaling = HEAD_DIM ** (-0.5)

    def one_sequence(start, count, tiles):
        keys = k[:, pl.ds(start, count)].reshape(2 * count * rows, 128)
        values = v[:, pl.ds(start, count)].reshape(2 * count * rows, 128)
        size = tiles * rows
        for part in range(count // tiles):
            at = pl.ds(start + part * tiles, tiles)
            pair = two_heads((q[at].reshape(size, 128) * scaling).astype(bf16), low)
            scores = dot_cols(pair, keys)
            shifted = jnp.exp(scores - jnp.max(scores, axis=-1, keepdims=True))
            total = jnp.sum(shifted, axis=-1, keepdims=True)
            mixed = dot(shifted.astype(bf16), values) * (1.0 / total)
            out[at] = jnp.where(low, mixed[:size], mixed[size:]).astype(bf16).reshape(tiles, rows, 128)

    by_sequence(kind[0], one_sequence, 128 // rows)


def attend(kind, q, k, v):
    rows = q.shape[1]
    own = pl.BlockSpec((BLOCKS, rows, 128), lambda p, *_: (0, 0, p))
    every = pl.BlockSpec((2, BLOCKS, rows, 128), lambda p, *_: (0, 0, 0, p))
    return run(
        attend_body,
        (HALF // 128,),
        [(q, own), (k, every), (v, every)],
        [(q.shape, bf16, own)],
        scalars=(kind,),
        flops=16 * BLOCKS * rows * 8 * rows * HALF,
    )[0]


def attend_back_body(kind, q, k, v, d_out, dq, dk, dv, acc_k, acc_v):
    rows = q.shape[1]
    low = lax.broadcasted_iota(jnp.int32, (1, 128), 1) < HEAD_DIM
    scaling = HEAD_DIM ** (-0.5)

    def one_sequence(start, count, tiles):
        key_rows = 2 * count * rows
        keys = k[:, pl.ds(start, count)].reshape(key_rows, 128)
        values = v[:, pl.ds(start, count)].reshape(key_rows, 128)
        size = tiles * rows
        for part in range(count // tiles):
            at = pl.ds(start + part * tiles, tiles)
            pair = two_heads((q[at].reshape(size, 128) * scaling).astype(bf16), low)
            d_pair = two_heads(d_out[at].reshape(size, 128), low)
            scores = dot_cols(keys, pair)
            shifted = jnp.exp(scores - jnp.max(scores, axis=0, keepdims=True))
            probs = shifted * (1.0 / jnp.sum(shifted, axis=0, keepdims=True))
            d_probs = dot_cols(values, d_pair)
            row_sum = jnp.sum(probs * d_probs, axis=0, keepdims=True)
            d_scores = (probs * (d_probs - row_sum)).astype(bf16)
            add_v = dot(probs.astype(bf16), d_pair)
            add_k = dot(d_scores, pair)
            if part == 0:
                acc_v[:key_rows] = add_v
                acc_k[:key_rows] = add_k
            else:
                acc_v[:key_rows] += add_v
                acc_k[:key_rows] += add_k
            both = dot_rows(d_scores, keys) * scaling
            dq[at] = jnp.where(low, both[:size], both[size:]).astype(bf16).reshape(tiles, rows, 128)
        dk[:, pl.ds(start, count)] = acc_k[:key_rows].astype(bf16).reshape(2, count, rows, 128)
        dv[:, pl.ds(start, count)] = acc_v[:key_rows].astype(bf16).reshape(2, count, rows, 128)

    by_sequence(kind[0], one_sequence, 128 // rows)


def attend_back(kind, q, k, v, d_out):
    rows = q.shape[1]
    own = pl.BlockSpec((BLOCKS, rows, 128), lambda p, *_: (0, 0, p))
    every = pl.BlockSpec((2, BLOCKS, rows, 128), lambda p, *_: (0, 0, 0, p))
    return run(
        attend_back_body,
        (HALF // 128,),
        [(q, own), (k, every), (v, every), (d_out, own)],
        [(q.shape, bf16, own), (k.shape, bf16, every), (v.shape, bf16, every)],
        scratch=[pltpu.VMEM((8 * rows, 128), f32), pltpu.VMEM((8 * rows, 128), f32)],
        scalars=(kind,),
        flops=40 * BLOCKS * rows * 8 * rows * HALF,
    )


def gelu_parts(u):
    rate = 0.7978845608028654
    inner = rate * (u + 0.044715 * (u * u * u))
    return jnp.tanh(inner), rate


def mlp_body(
    mixed_n, mixed_r, proj_n, proj_r, own, tab, up_n, down_n, up_a, down_a, up_b, down_b,
    attn_out, middle, normed, u, mlp_out, out, acc,
):
    rows = own.shape[1]
    step = pl.program_id(0)

    @pl.when(step == 0)
    def _():
        acc[...] = dot(flat(mixed_n), proj_n[...]) + dot(flat(mixed_r), proj_r[...])
        for i in range(BLOCKS):
            attn = acc[i * rows : (i + 1) * rows]
            attn_out[i] = attn.astype(bf16)
            mid = own[i].astype(f32) + tab[i, 2:3] * attn
            middle[i] = mid
            unit, _ = unit_rows(mid)
            normed[i] = (unit * (1.0 + tab[i, 4:5]) + tab[i, 3:4]).astype(bf16)

    def hidden(up, down, first):
        pre = dot(flat(normed), up[...])
        u[0] = pre.astype(bf16)
        tanh, _ = gelu_parts(pre)
        term = dot((0.5 * pre * (1.0 + tanh)).astype(bf16), down[...])
        if first:
            acc[...] = term
        else:
            acc[...] += term

    @pl.when(step == 0)
    def _():
        hidden(up_n, down_n, True)

    @pl.when(step == 1)
    def _():
        hidden(up_n, down_n, False)

    @pl.when(step == 2)
    def _():
        hidden(up_a, down_a, False)

    @pl.when(step == 3)
    def _():
        hidden(up_b, down_b, False)
        for i in range(BLOCKS):
            term = acc[i * rows : (i + 1) * rows]
            mlp_out[i] = term.astype(bf16)
            out[i] = (middle[i] + tab[i, 5:6] * term).astype(bf16)


def halves(weights, rows_of_down):
    up, down, (up_a, down_a, at_a), (up_b, down_b, at_b) = weights
    here = lambda j: jnp.minimum(j, 1)
    return [
        (up, pl.BlockSpec((D, TILE), lambda j, *_: (0, here(j)))),
        (down, pl.BlockSpec((TILE, D), lambda j, *_: (here(j), 0))),
        (up_a, pl.BlockSpec((D, TILE), lambda j, *_: (0, at_a))),
        (down_a, pl.BlockSpec((TILE, D), lambda j, *_: (at_a, 0))),
        (up_b, pl.BlockSpec((D, TILE), lambda j, *_: (0, at_b))),
        (down_b, pl.BlockSpec((TILE, D), lambda j, *_: (at_b, 0))),
    ]


def feed_forward(mixed_n, mixed_r, proj_n, proj_r, own, tab, weights):
    rows = own.shape[1]
    total = BLOCKS * rows
    return run(
        mlp_body,
        (4,),
        [(mixed_n, None), (mixed_r, None), (proj_n, None), (proj_r, None), (own, None), (tab, None)]
        + halves(weights, None),
        [
            (own.shape, bf16, None),
            (own.shape, f32, None),
            (own.shape, bf16, None),
            ((4, total, TILE), bf16, pl.BlockSpec((1, total, TILE), lambda j: (j, 0, 0))),
            (own.shape, bf16, None),
            (own.shape, bf16, None),
        ],
        scratch=[pltpu.VMEM((total, D), f32)],
        flops=2 * total * D * (D + 8 * D),
    )


def mlp_back_body(
    part, d_out, tab, mlp_out, normed, u, up_n, down_n, up_a, down_a, up_b, down_b,
    middle, attn_out, proj_n, proj_r, mixed_n, mixed_r, order,
    g_keep, g_send, p_keep, p_send, d_middle, d_mix_n, d_mix_r, d_mod,
    d_mlp, d_mlp_t, normed_t, acc,
):
    rows = d_out.shape[1]
    step = pl.program_id(0)

    @pl.when(step == 0)
    def _():
        for i in range(BLOCKS):
            grad = d_out[i].astype(f32)
            d_mlp[i * rows : (i + 1) * rows] = (grad * tab[i, 5:6]).astype(bf16)
            d_mod[i, 3:4] = col_sum(grad * mlp_out[i].astype(f32))
        d_mlp_t[...] = dot_cols(order[...], d_mlp[...]).astype(bf16)
        normed_t[...] = dot_cols(order[...], flat(normed)).astype(bf16)

    def hidden(up, down, first):
        pre = u[0].astype(f32)
        tanh, rate = gelu_parts(pre)
        act = (0.5 * pre * (1.0 + tanh)).astype(bf16)
        slope = 0.5 * (1.0 + tanh) + (0.5 * rate) * pre * (1.0 - tanh * tanh) * (
            1.0 + (3.0 * 0.044715) * (pre * pre)
        )
        g_down = dot(d_mlp_t[...], act).astype(bf16)
        g_keep[0, :, TILE:] = g_down[:HALF]
        g_send[0, :, TILE:] = g_down[HALF:]
        d_up = (slope * dot_cols(d_mlp[...], down[...])).astype(bf16)
        g_up = dot(normed_t[...], d_up).astype(bf16)
        g_keep[0, :, :TILE] = g_up[:HALF]
        g_send[0, :, :TILE] = g_up[HALF:]
        term = dot_cols(d_up, up[...])
        if first:
            acc[...] = term
        else:
            acc[...] += term

    @pl.when(step == 0)
    def _():
        hidden(up_n, down_n, True)

    @pl.when(step == 1)
    def _():
        hidden(up_n, down_n, False)

    @pl.when(step == 2)
    def _():
        hidden(up_a, down_a, False)

    @pl.when(step == 3)
    def _():
        hidden(up_b, down_b, False)
        for i in range(BLOCKS):
            at = slice(i * rows, (i + 1) * rows)
            d_normed = acc[at]
            unit, inverse = unit_rows(middle[i])
            grad = d_out[i].astype(f32) + norm_back(d_normed, unit, inverse, tab[i, 4:5])
            d_middle[i] = grad
            d_mod[i, 0:1] = col_sum(grad * attn_out[i].astype(f32))
            d_mod[i, 1:2] = col_sum(d_normed)
            d_mod[i, 2:3] = col_sum(d_normed * unit)
            d_mlp[at] = (grad * tab[i, 2:3]).astype(bf16)
        d_mlp_t[...] = dot_cols(order[...], d_mlp[...]).astype(bf16)
        for side, mixed, proj, d_mix in (
            (0, mixed_n, proj_n, d_mix_n),
            (1, mixed_r, proj_r, d_mix_r),
        ):
            d_mix[...] = dot_cols(d_mlp[...], proj[...]).astype(bf16).reshape(d_mix.shape)
            g_proj = dot(d_mlp_t[...], flat(mixed)).astype(bf16)
            p_keep[side] = g_proj[:HALF]
            p_send[side] = g_proj[HALF:]


def feed_back(part, d_out, tab, saved, weights, proj_n, proj_r, mixed_n, mixed_r, order):
    attn_out, middle, normed, u, mlp_out = saved
    rows = d_out.shape[1]
    total = BLOCKS * rows

    def tile_of(j, part_ref):
        local = jnp.where(part_ref[0] == 0, j % 2, 1 - j % 2)
        return (j // 2, 0, jnp.where(j < 2, j % 2, local))

    grads = ((2, HALF, 4 * TILE), bf16, pl.BlockSpec((1, HALF, 2 * TILE), tile_of))
    return run(
        mlp_back_body,
        (4,),
        [
            (d_out, None),
            (tab, None),
            (mlp_out, None),
            (normed, None),
            (u, pl.BlockSpec((1, total, TILE), lambda j, *_: (j, 0, 0))),
        ]
        + halves(weights, None)
        + [
            (middle, None),
            (attn_out, None),
            (proj_n, None),
            (proj_r, None),
            (mixed_n, None),
            (mixed_r, None),
            (order, None),
        ],
        [
            grads,
            grads,
            ((2, HALF, HALF), bf16, None),
            ((2, HALF, HALF), bf16, None),
            (d_out.shape, f32, None),
            (mixed_n.shape, bf16, None),
            (mixed_n.shape, bf16, None),
            ((BLOCKS, 4, D), f32, None),
        ],
        scratch=[
            pltpu.VMEM((total, D), bf16),
            pltpu.VMEM((D, total), bf16),
            pltpu.VMEM((D, total), bf16),
            pltpu.VMEM((total, D), f32),
        ],
        scalars=(part,),
        flops=2 * total * D * (16 * D + 4 * D),
    )


def qkv_back_body(
    dq_n, dk_n, dv_n, dq_r, dk_r, dv_r, w_n, w_r, normed, order,
    g_keep, g_send, d_own, d_oth, normed_t, acc,
):
    rows = dq_n.shape[1]
    total = BLOCKS * rows
    step = pl.program_id(0)

    @pl.when(step == 0)
    def _():
        normed_t[...] = dot_cols(order[...], flat(normed)).astype(bf16)

    for index, (grad, w) in enumerate(
        ((dq_n, w_n), (dk_n, w_n), (dv_n, w_n), (dq_r, w_r), (dk_r, w_r), (dv_r, w_r))
    ):

        @pl.when(step == index)
        def _(index=index, grad=grad, w=w):
            value = flat(grad)
            term = dot_cols(value, w[0])
            if index == 0:
                acc[:total] = term
                acc[total:] = jnp.zeros((total, D), f32)
                g_w = dot(normed_t[:, :total], value).astype(bf16)
            elif index == 3:
                acc[:total] += term
                g_w = dot(normed_t[:, :total], value).astype(bf16)
            else:
                acc[...] += term
                g_w = dot(normed_t[...], value).astype(bf16)
            g_keep[0] = g_w[:HALF]
            g_send[0] = g_w[HALF:]
            if index == 5:
                d_own[...] = acc[:total]
                d_oth[...] = acc[total:].astype(bf16)


def qkv_back(grads_n, grads_r, w_n, w_r, normed, order):
    rows = normed.shape[2]
    total = BLOCKS * rows
    grads = ((2, HALF, 3 * HALF), bf16, pl.BlockSpec((1, HALF, HALF), lambda j: (j // 3, 0, j % 3)))
    return run(
        qkv_back_body,
        (6,),
        [(g, None) for g in grads_n]
        + [(g, None) for g in grads_r]
        + [
            (w_n, pl.BlockSpec((1, D, HALF), lambda j: (jnp.minimum(j, 2), 0, 0))),
            (w_r, pl.BlockSpec((1, D, HALF), lambda j: (jnp.maximum(j - 3, 0), 0, 0))),
            (normed, None),
            (order, None),
        ],
        [grads, grads, ((total, D), f32, None), ((total, D), bf16, None)],
        scratch=[pltpu.VMEM((D, 2 * total), bf16), pltpu.VMEM((2 * total, D), f32)],
        flops=2 * total * D * (20 * HALF + 2 * D),
    )


def finish_body(d_own, d_got, own, tab, d_middle, d_rows, d_mod):
    rows = own.shape[1]
    for i in range(BLOCKS):
        at = slice(i * rows, (i + 1) * rows)
        d_normed = d_own[at] + d_got[at].astype(f32)
        unit, inverse = unit_rows(own[i].astype(f32))
        grad = d_middle[i] + norm_back(d_normed, unit, inverse, tab[i, 1:2])
        d_rows[i] = grad.astype(bf16)
        d_mod[i, 0:1] = col_sum(d_normed)
        d_mod[i, 1:2] = col_sum(d_normed * unit)


def finish(d_own, d_got, own, tab, d_middle):
    return run(
        finish_body,
        (1,),
        [(d_own, None), (d_got, None), (own, None), (tab, None), (d_middle, None)],
        [(own.shape, bf16, None), ((BLOCKS, 2, D), f32, None)],
    )


def pick_body(index, own, oth, out):
    spot = lax.broadcasted_iota(jnp.int32, (1, own.shape[0]), 1)
    here = (index[...] == spot).astype(bf16)
    there = (index[...] - own.shape[0] == spot).astype(bf16)
    out[...] = (dot(here, own[...]) + dot(there, oth[...])).astype(bf16)


def pick(index, own, oth):
    count = index.shape[0]
    return run(
        pick_body,
        (1,),
        [(index, None), (own, None), (oth, None)],
        [((count, D), bf16, None)],
        flops=2 * count * GROUP * D,
    )[0]


def put_body(index_own, index_oth, own, oth, base, out):
    spot = lax.broadcasted_iota(jnp.int32, (base.shape[0], 1), 0)
    here = (index_own[...] == spot).astype(f32)
    there = (index_oth[...] == spot).astype(f32)
    hit = jnp.sum(here, axis=1, keepdims=True) + jnp.sum(there, axis=1, keepdims=True)
    put = dot(here.astype(bf16), own[...]) + dot(there.astype(bf16), oth[...])
    out[...] = jnp.where(hit > 0.5, put, base[...].astype(f32)).astype(bf16)


def put(index_own, index_oth, own, oth, base):
    return run(
        put_body,
        (1,),
        [(index_own, None), (index_oth, None), (own, None), (oth, None), (base, None)],
        [(base.shape, bf16, None)],
        flops=2 * base.shape[0] * KEEP * D,
    )[0]


def on_device(
    n_dp,
    tokens,
    conditioning,
    segment_ids,
    kept_rows,
    cotangent,
    mod_first,
    qkv_first,
    proj_first,
    up_first,
    down_first,
    mod_second,
    qkv_second,
    proj_second,
    up_second,
    down_second,
):
    dp_pos = lax.axis_index("dp")
    side = lax.axis_index("tensor")
    core = dp_pos % 2
    bits = n_dp.bit_length() - 1

    def moves(where):
        pairs = []
        for dp in range(n_dp):
            for t in range(2):
                to_dp, to_t = where(dp, t)
                pairs.append((dp * 2 + t, to_dp * 2 + to_t))
        return pairs

    across = moves(lambda dp, t: (dp, 1 - t))
    core_swap = moves(lambda dp, t: (dp ^ 1, t))
    turn = moves(lambda dp, t: (dp // 2 * 2 + t, dp % 2))
    deal = moves(lambda dp, t: (dp // 2 * 2 + 1 - t, dp % 2))
    undeal = moves(lambda dp, t: (dp // 2 * 2 + t, 1 - dp % 2))

    def send(value, pairs):
        return lax.ppermute(value, ALL, pairs)

    def to_owner(rows):
        tiles = rows.reshape(BLOCKS, SPAN // 2, D)
        even = send(tiles[0::2], turn)
        odd = send(tiles[1::2], deal)
        return jnp.where(core == 0, jnp.concatenate([even, odd]), jnp.concatenate([odd, even]))

    def from_owner(rows):
        even = send(lax.dynamic_slice_in_dim(rows, 2 * core, 3), turn)
        odd = send(lax.dynamic_slice_in_dim(rows, 3 * (1 - core), 2), undeal)
        return jnp.concatenate([even[0:1], odd[0:1], even[1:2], odd[1:2], even[2:3]]).reshape(-1, D)

    def halves_of(value, axis):
        size = value.shape[axis] // 2
        near = send(lax.dynamic_slice_in_dim(value, core * size, size, axis), across)
        return near, send(near, core_swap)

    def joined(value, axis):
        near, far = halves_of(value, axis)
        return jnp.where(
            core == 0, jnp.concatenate([near, far], axis), jnp.concatenate([far, near], axis)
        )

    def gathered(value):
        size = value.shape[0] // n_dp
        piece = send(lax.dynamic_slice_in_dim(value, dp_pos * size, size), across)
        return lax.all_gather(piece, "dp", axis=0, tiled=True)

    own = to_owner(tokens)
    oth = send(own, core_swap)
    numbers = send(jnp.concatenate([kept_rows, segment_ids[::SPAN]]), turn)
    kept, segs = numbers[:KEEP], numbers[KEEP:]
    kind = jnp.where(segs[3] == segs[0], 0, jnp.where(segs[4] == segs[1], 1, 2)).reshape(1)
    cond = send(jax.nn.silu(conditioning.astype(f32)).astype(bf16), turn)
    slot_hot = segs[:, None] == jnp.arange(SLOTS, dtype=jnp.int32)[None, :]
    cond_rows = jnp.dot(slot_hot.astype(bf16), cond, preferred_element_type=f32).astype(bf16)

    def table(mod):
        return jnp.dot(cond_rows, mod, preferred_element_type=f32).reshape(BLOCKS, 6, D)

    tab_one, tab_two = table(mod_first), table(mod_second)

    wq_one = jnp.transpose(qkv_first, (1, 0, 2))
    wq_two = jnp.transpose(qkv_second, (1, 0, 2))
    wq_one_far = joined(wq_one, 1)
    proj_one_far = joined(proj_first, 0)
    up_near, up_far = halves_of(up_first, 1)
    down_near, down_far = halves_of(down_first, 0)
    mlp_one = (up_first, down_first, (up_near, down_near, 0), (up_far, down_far, 0))
    wq_two_far = gathered(wq_two.reshape(3 * D, HALF)).reshape(3, D, HALF)
    proj_two_far = joined(proj_second, 0)
    up_two_far, down_two_far = gathered(up_second), gathered(down_second)
    mlp_two = (up_second, down_second, (up_two_far, down_two_far, 0), (up_two_far, down_two_far, 1))
    cot_own = to_owner(cotangent)
    cot_oth = send(cot_own, core_swap)

    block_of, inside = kept // SPAN, kept % SPAN
    spot = (
        jnp.where(inside // (SPAN // 2) == core, 0, GROUP // 2)
        + block_of * (SPAN // 2)
        + inside % (SPAN // 2)
    ).reshape(BLOCKS, 2, KEEP // (2 * BLOCKS))
    spot_own = lax.dynamic_slice_in_dim(spot, core, 1, 1).reshape(-1)
    spot_oth = lax.dynamic_slice_in_dim(spot, 1 - core, 1, 1).reshape(-1)
    spot_all = jnp.concatenate([spot_own, spot_oth])

    stages = [0, 1] + list(range(bits - 1, 1, -1))
    piece = D // n_dp
    row = jnp.arange(D, dtype=jnp.int32)
    turned = jnp.zeros_like(row)
    for place, bit in enumerate(stages):
        turned = turned + (((row // piece) // 2 ** (bits - 1 - place)) % 2) * 2**bit
    source = jnp.bitwise_xor(turned, dp_pos) * piece + row % piece
    order = (source[:, None] == row[None, :]).astype(bf16)

    def forward(own, oth, tab, wq, wq_far, proj, proj_far, weights):
        normed, *near = project_qkv(True, own, oth, tab, None, wq)
        mixed_n = attend(kind, *near)
        far = project_qkv(False, None, None, None, normed, wq_far)
        mixed_r = attend(kind, *far)
        *saved, out = feed_forward(mixed_n, mixed_r, proj, proj_far, own, tab, weights)
        return out, (normed, near, far, mixed_n, mixed_r, saved)

    def backward(d_out, own, tab, wq, wq_far, proj, proj_far, weights, kept_of, part):
        normed, near, far, mixed_n, mixed_r, saved = kept_of
        g_keep, g_send, p_keep, p_send, d_middle, d_mix_n, d_mix_r, d_mod = feed_back(
            part, d_out, tab, saved, weights, proj, proj_far, mixed_n, mixed_r, order
        )
        total_mlp = total(g_keep, g_send)
        total_proj = total(p_keep, p_send)
        grads_n = attend_back(kind, *near, d_mix_n)
        grads_r = attend_back(kind, *far, d_mix_r)
        q_keep, q_send, d_own, d_oth = qkv_back(grads_n, grads_r, wq, wq_far, normed, order)
        d_got = send(d_oth, core_swap)
        total_qkv = total(q_keep, q_send)
        d_rows, d_mod_a = finish(d_own, d_got, own, tab, d_middle)
        per_block = jnp.concatenate([d_mod_a, d_mod], axis=1).reshape(BLOCKS, 6 * D)
        d_table = lax.dot_general(
            slot_hot.astype(f32),
            per_block,
            (((0,), (0,)), ((), ())),
            precision=lax.Precision.HIGHEST,
        )
        return d_rows, (total_qkv, total_proj, total_mlp), d_table.astype(bf16)

    def total(keep, away):
        got = send(away, core_swap)
        other = (keep[1].astype(f32) + got[1].astype(f32)).astype(bf16)
        got_x = send(other, across)
        acc = keep[0].astype(f32) + got[0].astype(f32) + got_x.astype(f32)
        for bit in stages[1:]:
            size = acc.shape[0] // 2
            got = send(acc[size:].astype(bf16), moves(lambda dp, t, bit=bit: (dp ^ 2**bit, t)))
            acc = acc[:size] + got.astype(f32)
        return acc

    out_one, kept_one = forward(
        own, oth, tab_one, wq_one, wq_one_far, proj_first, proj_one_far, mlp_one
    )
    first_own = out_one.reshape(-1, D)
    first_oth = send(first_own, core_swap)
    first_out = from_owner(out_one)

    routed = pick(spot_all[:, None], first_own, first_oth)
    routed_own, routed_oth = routed.reshape(2, BLOCKS, KEEP // (2 * BLOCKS), D)
    cot_routed = pick(spot_own[:, None], cot_own.reshape(-1, D), cot_oth.reshape(-1, D)).reshape(
        routed_own.shape
    )
    out_two, kept_two = forward(
        routed_own, routed_oth, tab_two, wq_two, wq_two_far, proj_second, proj_two_far, mlp_two
    )
    second_own = out_two.reshape(-1, D)
    second_oth = send(second_own, core_swap)
    routed_rows = put(spot_own[None], spot_oth[None], second_own, second_oth, first_own)
    routed_out = from_owner(routed_rows.reshape(own.shape))

    d_two, grads_two, d_table_two = backward(
        cot_routed, routed_own, tab_two, wq_two, wq_two_far, proj_second, proj_two_far, mlp_two,
        kept_two, jnp.zeros((1,), jnp.int32),
    )
    d_two_own = d_two.reshape(-1, D)
    d_two_oth = send(d_two_own, core_swap)
    d_first = put(spot_own[None], spot_oth[None], d_two_own, d_two_oth, cot_own.reshape(-1, D))
    d_one, grads_one, d_table_one = backward(
        d_first.reshape(own.shape), own, tab_one, wq_one, wq_one_far, proj_first, proj_one_far,
        mlp_one, kept_one, core.reshape(1).astype(jnp.int32),
    )
    input_grad = from_owner(d_one).astype(f32)

    mod_rows = D // (n_dp * 2)
    cond_every = lax.all_gather(cond, ALL, axis=0, tiled=True)
    cond_cols = lax.dynamic_slice_in_dim(cond_every, (dp_pos * 2 + side) * mod_rows, mod_rows, 1)

    def mod_grad(d_table):
        every = lax.all_gather(d_table, ALL, axis=0, tiled=True)
        return dot_rows(cond_cols, every)

    def placed(grads):
        qkv, proj, mlp = grads
        parts = mlp.reshape(piece, 2, 2, TILE)
        up = parts[:, :, 0].reshape(piece, 2 * TILE)
        down = parts[:, :, 1].reshape(piece, 2 * TILE)
        return qkv.reshape(piece, 3, HALF), proj.T, up, down.T

    return (
        first_out,
        routed_out,
        input_grad,
        mod_grad(d_table_one),
        *placed(grads_one),
        mod_grad(d_table_two),
        *placed(grads_two),
    )


def solution(mesh):
    n_dp = mesh.shape["dp"]
    return jax.shard_map(
        functools.partial(on_device, n_dp),
        mesh=mesh,
        in_specs=(
            P(("dp", "tensor"), None),
            P("dp", None),
            P("dp"),
            P("dp"),
            P(("dp", "tensor"), None),
            P(),
            P(None, None, "tensor"),
            P("tensor", None),
            P(None, "tensor"),
            P("tensor", None),
            P(),
            P(None, None, "tensor"),
            P("tensor", None),
            P(None, "tensor"),
            P("tensor", None),
        ),
        out_specs=(
            P(("dp", "tensor"), None),
            P(("dp", "tensor"), None),
            P(("dp", "tensor"), None),
            P(("dp", "tensor"), None),
            P("dp", None, "tensor"),
            P("tensor", "dp"),
            P("dp", "tensor"),
            P("tensor", "dp"),
            P(("dp", "tensor"), None),
            P("dp", None, "tensor"),
            P("tensor", "dp"),
            P("dp", "tensor"),
            P("tensor", "dp"),
        ),
        check_vma=False,
    )
```

```python
import functools

import jax
import jax.numpy as jnp
from jax import lax
from jax.experimental import pallas as pl
from jax.experimental.pallas import tpu as pltpu
from jax.sharding import PartitionSpec as P

D = 768
HEAD_DIM = 64
SLOTS = 5
GROUP = 1280
KEEP = 640
BLOCKS = 5
SPAN = GROUP // BLOCKS
HALF = D // 2
TILE = 768
NORM_EPS = 1e-06
f32 = jnp.float32
bf16 = jnp.bfloat16
ALL = ("dp", "tensor")
VMEM_BYTES = 32 * 1024 * 1024
LIGHT = 2000


def dot(left, right):
    return jnp.dot(left, right, preferred_element_type=f32)


def dot_cols(left, right):
    return lax.dot_general(left, right, (((1,), (1,)), ((), ())), preferred_element_type=f32)


def dot_rows(left, right):
    return lax.dot_general(left, right, (((0,), (0,)), ((), ())), preferred_element_type=f32)


def unit_rows(rows):
    centre = rows - jnp.mean(rows, axis=-1, keepdims=True)
    inverse = lax.rsqrt(jnp.mean(centre * centre, axis=-1, keepdims=True) + NORM_EPS)
    return centre * inverse, inverse


def norm_back(d_normed, unit, inverse, scale_row):
    e = d_normed * (1.0 + scale_row)
    return inverse * (
        e
        - jnp.mean(e, axis=-1, keepdims=True)
        - unit * jnp.mean(e * unit, axis=-1, keepdims=True)
    )


def col_sum(rows):
    return jnp.sum(rows, axis=0, keepdims=True)


def flat(ref):
    value = ref[...]
    return value.reshape(-1, value.shape[-1])


def whole(shape):
    return pl.BlockSpec(shape, lambda *_: (0,) * len(shape), pipeline_mode=pl.Buffered(1))


def run(body, grid, ins, outs, scratch=(), scalars=(), flops=0, deps=()):
    in_specs = [whole(a.shape) if s is None else s for a, s in ins]
    in_specs += [pl.BlockSpec(memory_space=pl.ANY)] * len(deps)
    first, past = len(scalars) + len(ins), len(scalars) + len(ins) + len(deps)

    def step(*refs):
        body(*refs[:first], *refs[past:])

    out_specs = [whole(sh) if s is None else s for sh, _, s in outs]
    moved = sum(a.size * a.dtype.itemsize for a, _ in ins)
    moved += sum(jnp.dtype(d).itemsize * functools.reduce(lambda p, q: p * q, sh, 1) for sh, d, _ in outs)
    return pl.pallas_call(
        step,
        grid_spec=pltpu.PrefetchScalarGridSpec(
            num_scalar_prefetch=len(scalars),
            grid=grid,
            in_specs=in_specs,
            out_specs=out_specs,
            scratch_shapes=list(scratch),
        ),
        out_shape=[jax.ShapeDtypeStruct(sh, d) for sh, d, _ in outs],
        compiler_params=pltpu.CompilerParams(
            vmem_limit_bytes=VMEM_BYTES, dimension_semantics=("arbitrary",) * len(grid)
        ),
        cost_estimate=pl.CostEstimate(
            flops=1 + int(flops) // LIGHT, bytes_accessed=1 + int(moved) // LIGHT, transcendentals=0
        ),
    )(*scalars, *[a for a, _ in ins], *deps)


def qkv_body(own, oth, tab, w, normed, q, k, v):
    rows = own.shape[1]
    step = pl.program_id(0)

    @pl.when(step == 0)
    def _():
        for side, src in ((0, own), (1, oth)):
            for i in range(BLOCKS):
                unit, _ = unit_rows(src[i].astype(f32))
                normed[side, i] = (unit * (1.0 + tab[i, 1:2]) + tab[i, 0:1]).astype(bf16)

    qkv_steps(step, normed, w, q, k, v)


def qkv_next_body(normed, w, q, k, v):
    qkv_steps(pl.program_id(0), normed, w, q, k, v)


def qkv_parts_body(place, normed, w_0, w_1, w_2, w_3, w, q, k, v):
    for index, part in enumerate((w_0, w_1, w_2, w_3)):
        at = pl.multiple_of(((place[0] % 4) ^ index) * (D // 4), D // 4)
        w[0, pl.ds(at, D // 4)] = part[0]
    qkv_steps(pl.program_id(0), normed, w, q, k, v)


def block(w):
    return w[...].reshape(D, HALF)


def qkv_steps(step, normed, w, q, k, v):
    @pl.when(step == 0)
    def _():
        mine = normed[0].reshape(-1, D)
        q[...] = dot(mine, block(w)).astype(bf16).reshape(q.shape)

    for index, out in ((1, k), (2, v)):

        @pl.when(step == index)
        def _(out=out):
            out[...] = dot(flat(normed), block(w)).astype(bf16).reshape(out.shape)


def qkv_outs(rows):
    return [
        ((BLOCKS, rows, HALF), bf16, None),
        ((2, BLOCKS, rows, HALF), bf16, None),
        ((2, BLOCKS, rows, HALF), bf16, None),
    ]


BY_STEP = pl.BlockSpec((1, D, HALF), lambda j, *_: (j, 0, 0))


def block_at(w, index):
    if w.ndim == 3:
        return (w, pl.BlockSpec((1, D, HALF), lambda j, *_: (index(j), 0, 0)))
    pieces, _, rows, _ = w.shape
    return (w, pl.BlockSpec((pieces, 1, rows, HALF), lambda j, *_: (0, index(j), 0, 0)))


def project_first(own, oth, tab, w, deps=()):
    rows = own.shape[1]
    return run(
        qkv_body,
        (3,),
        [(own, None), (oth, None), (tab, None), (w, BY_STEP)],
        [((2, BLOCKS, rows, D), bf16, None)] + qkv_outs(rows),
        flops=2 * 25 * rows * D * HALF,
        deps=deps,
    )


def project_next(normed, w, deps=()):
    rows = normed.shape[2]
    ins = [(normed, None), block_at(w, lambda j: j)]
    return run(qkv_next_body, (3,), ins, qkv_outs(rows), flops=2 * 25 * rows * D * HALF, deps=deps)


def project_parts(place, normed, parts, deps=()):
    rows = normed.shape[2]
    by_step = pl.BlockSpec((1, D // 4, HALF), lambda j, *_: (j, 0, 0))
    return run(
        qkv_parts_body,
        (4,),
        [(normed, None)] + [(part, by_step) for part in parts],
        [((4, D, HALF), bf16, BY_STEP)] + qkv_outs(rows),
        scalars=(place,),
        flops=2 * 25 * rows * D * HALF,
        deps=deps,
    )


def by_sequence(kind, one_sequence, long_tiles):
    @pl.when(kind < 2)
    def _():
        one_sequence(kind, 4, long_tiles)
        one_sequence(jnp.where(kind == 0, 4, 0), 1, 1)

    @pl.when(kind == 2)
    def _():
        def short(i, carry):
            one_sequence(i, 1, 1)
            return carry

        lax.fori_loop(0, BLOCKS, short, 0)


def two_heads(rows, low):
    zero = jnp.zeros_like(rows)
    return jnp.concatenate([jnp.where(low, rows, zero), jnp.where(low, zero, rows)], axis=0)


def attend_body(kind, q, k, v, out):
    rows = q.shape[1]
    low = lax.broadcasted_iota(jnp.int32, (1, 128), 1) < HEAD_DIM
    scaling = HEAD_DIM ** (-0.5)

    def one_sequence(start, count, tiles):
        keys = k[:, pl.ds(start, count)].reshape(2 * count * rows, 128)
        values = v[:, pl.ds(start, count)].reshape(2 * count * rows, 128)
        size = tiles * rows
        for part in range(count // tiles):
            at = pl.ds(start + part * tiles, tiles)
            pair = two_heads((q[at].reshape(size, 128) * scaling).astype(bf16), low)
            scores = dot_cols(pair, keys)
            shifted = jnp.exp(scores - jnp.max(scores, axis=-1, keepdims=True))
            total = jnp.sum(shifted, axis=-1, keepdims=True)
            mixed = dot(shifted.astype(bf16), values) * (1.0 / total)
            out[at] = jnp.where(low, mixed[:size], mixed[size:]).astype(bf16).reshape(tiles, rows, 128)

    by_sequence(kind[0], one_sequence, 128 // rows)


def attend(kind, q, k, v, deps=()):
    rows = q.shape[1]
    own = pl.BlockSpec((BLOCKS, rows, 128), lambda p, *_: (0, 0, p))
    every = pl.BlockSpec((2, BLOCKS, rows, 128), lambda p, *_: (0, 0, 0, p))
    return run(
        attend_body,
        (HALF // 128,),
        [(q, own), (k, every), (v, every)],
        [(q.shape, bf16, own)],
        scalars=(kind,),
        flops=16 * BLOCKS * rows * 8 * rows * HALF,
        deps=deps,
    )[0]


def attend_back_body(kind, q, k, v, d_out, dq, dk, dv, acc_k, acc_v):
    rows = q.shape[1]
    low = lax.broadcasted_iota(jnp.int32, (1, 128), 1) < HEAD_DIM
    scaling = HEAD_DIM ** (-0.5)

    def one_sequence(start, count, tiles):
        key_rows = 2 * count * rows
        keys = k[:, pl.ds(start, count)].reshape(key_rows, 128)
        values = v[:, pl.ds(start, count)].reshape(key_rows, 128)
        size = tiles * rows
        for part in range(count // tiles):
            at = pl.ds(start + part * tiles, tiles)
            pair = two_heads((q[at].reshape(size, 128) * scaling).astype(bf16), low)
            d_pair = two_heads(d_out[at].reshape(size, 128), low)
            scores = dot_cols(keys, pair)
            shifted = jnp.exp(scores - jnp.max(scores, axis=0, keepdims=True))
            probs = shifted * (1.0 / jnp.sum(shifted, axis=0, keepdims=True))
            d_probs = dot_cols(values, d_pair)
            row_sum = jnp.sum(probs * d_probs, axis=0, keepdims=True)
            d_scores = (probs * (d_probs - row_sum)).astype(bf16)
            add_v = dot(probs.astype(bf16), d_pair)
            add_k = dot(d_scores, pair)
            if part == 0:
                acc_v[:key_rows] = add_v
                acc_k[:key_rows] = add_k
            else:
                acc_v[:key_rows] += add_v
                acc_k[:key_rows] += add_k
            both = dot_rows(d_scores, keys) * scaling
            dq[at] = jnp.where(low, both[:size], both[size:]).astype(bf16).reshape(tiles, rows, 128)
        dk[:, pl.ds(start, count)] = acc_k[:key_rows].astype(bf16).reshape(2, count, rows, 128)
        dv[:, pl.ds(start, count)] = acc_v[:key_rows].astype(bf16).reshape(2, count, rows, 128)

    by_sequence(kind[0], one_sequence, 128 // rows)


def attend_back(kind, q, k, v, d_out, deps=()):
    rows = q.shape[1]
    own = pl.BlockSpec((BLOCKS, rows, 128), lambda p, *_: (0, 0, p))
    every = pl.BlockSpec((2, BLOCKS, rows, 128), lambda p, *_: (0, 0, 0, p))
    return run(
        attend_back_body,
        (HALF // 128,),
        [(q, own), (k, every), (v, every), (d_out, own)],
        [(q.shape, bf16, own), (k.shape, bf16, every), (v.shape, bf16, every)],
        scratch=[pltpu.VMEM((8 * rows, 128), f32), pltpu.VMEM((8 * rows, 128), f32)],
        scalars=(kind,),
        flops=40 * BLOCKS * rows * 8 * rows * HALF,
        deps=deps,
    )


def gelu_parts(u):
    rate = 0.7978845608028654
    inner = rate * (u + 0.044715 * (u * u * u))
    return jnp.tanh(inner), rate


def hidden(normed, ups, downs, u, act):
    start = 0
    total = None
    ups = [far_up(up) for up in ups]
    for up, down in zip(ups, downs):
        at = slice(start, start + up.shape[1])
        start = start + up.shape[1]
        pre = dot(flat(normed), up)
        u[0, :, at] = pre.astype(bf16)
        tanh, _ = gelu_parts(pre)
        value = (0.5 * pre * (1.0 + tanh)).astype(bf16)
        act[0, :, at] = value
        term = dot(value, down[...])
        total = term if total is None else total + term
    return total


def mlp_near_body(
    mixed_n, mixed_r, proj_n, proj_r, own, tab, up, down,
    attn_out, middle, normed, u, act, acc,
):
    rows = own.shape[1]
    step = pl.program_id(0)

    @pl.when(step == 0)
    def _():
        for at in (slice(0, HALF), slice(HALF, D)):
            acc[:, at] = dot(flat(mixed_n), proj_n[:, at]) + dot(flat(mixed_r), block(proj_r)[at])
        for i in range(BLOCKS):
            attn = acc[i * rows : (i + 1) * rows]
            attn_out[i] = attn.astype(bf16)
            mid = own[i].astype(f32) + tab[i, 2:3] * attn
            middle[i] = mid
            unit, _ = unit_rows(mid)
            normed[i] = (unit * (1.0 + tab[i, 4:5]) + tab[i, 3:4]).astype(bf16)
        acc[...] = hidden(normed, [up], [down], u, act)

    @pl.when(step == 1)
    def _():
        acc[...] += hidden(normed, [up], [down], u, act)


def matching(place, down_0, down_1, down_2, down_3):
    refs = (down_0, down_1, down_2, down_3)
    if len(down_0.shape) > 2:
        return (lambda: far_downs(refs)[:2]), (lambda: far_downs(refs)[2:])
    same = (place[0] // 2 + place[0] // 4) % 2 == 0

    def first():
        return [
            jnp.where(same, down_0[...], down_2[...]),
            jnp.where(same, down_1[...], down_3[...]),
        ]

    def second():
        return [
            jnp.where(same, down_2[...], down_0[...]),
            jnp.where(same, down_3[...], down_1[...]),
        ]

    return first, second


def mlp_far_body(
    place, normed, start, middle, tab, up_0, up_1, up_2, up_3, down_0, down_1, down_2, down_3,
    u, act, mlp_out, out, acc,
):
    rows = middle.shape[1]
    step = pl.program_id(0)
    first, second = matching(place, down_0, down_1, down_2, down_3)

    @pl.when(step == 0)
    def _():
        acc[...] = start[...] + hidden(normed, [up_0, up_1], first(), u, act)

    @pl.when(step == 1)
    def _():
        acc[...] += hidden(normed, [up_2, up_3], second(), u, act)
        for i in range(BLOCKS):
            term = acc[i * rows : (i + 1) * rows]
            mlp_out[i] = term.astype(bf16)
            out[i] = (middle[i] + tab[i, 5:6] * term).astype(bf16)


def projection(w):
    return block_at(w, lambda j: 3)


def far_up(ref):
    return ref[...] if len(ref.shape) == 2 else block(ref)


def far_downs(downs):
    if len(downs[0].shape) == 2:
        return [down[...] for down in downs]
    wide = [
        jnp.concatenate([block(downs[index]), block(downs[index + 2])], axis=1) for index in range(2)
    ]
    return [wide[0][:HALF], wide[0][HALF:], wide[1][:HALF], wide[1][HALF:]]


def far_ins(ups, downs):
    if ups[0].ndim == 2:
        return [(part, None) for part in (*ups, *downs)]
    ins = []
    for index, part in enumerate((*ups, *downs)):
        pieces, _, rows, _ = part.shape
        at = pl.BlockSpec(
            (pieces, 1, rows, HALF),
            lambda *_, index=index: (0, 4 + index, 0, 0),
            pipeline_mode=pl.Buffered(1),
        )
        ins.append((part, at))
    return ins


def feed_near(mixed_n, mixed_r, proj_n, w_r, own, tab, up, down, deps=()):
    rows = own.shape[1]
    total = BLOCKS * rows
    tiles = ((2, total, TILE), bf16, pl.BlockSpec((1, total, TILE), lambda j: (j, 0, 0)))
    return run(
        mlp_near_body,
        (2,),
        [
            (mixed_n, None),
            (mixed_r, None),
            (proj_n, None),
            projection(w_r),
            (own, None),
            (tab, None),
            (up, pl.BlockSpec((D, TILE), lambda j: (0, j))),
            (down, pl.BlockSpec((TILE, D), lambda j: (j, 0))),
        ],
        [
            (own.shape, bf16, None),
            (own.shape, f32, None),
            (own.shape, bf16, None),
            tiles,
            tiles,
            ((total, D), f32, None),
        ],
        flops=2 * total * D * (D + 4 * D),
        deps=deps,
    )


def feed_far(place, normed, start, middle, tab, ups, downs, deps=()):
    total = BLOCKS * normed.shape[1]
    tiles = ((2, total, TILE), bf16, pl.BlockSpec((1, total, TILE), lambda j, *_: (j, 0, 0)))
    return run(
        mlp_far_body,
        (2,),
        [(normed, None), (start, None), (middle, None), (tab, None)]
        + far_ins(ups, downs),
        [tiles, tiles, (normed.shape, bf16, None), (normed.shape, bf16, None)],
        scratch=[pltpu.VMEM((total, D), f32)],
        scalars=(place,),
        flops=2 * total * D * (4 * D),
        deps=deps,
    )


def tile_of(j, place_ref):
    far = jnp.where(place_ref[0] // 2 % 2 == 0, j % 2, 1 - j % 2)
    return (j // 2, 0, jnp.where(j < 2, j % 2, far))


MLP_GRAD = ((2, HALF, 2 * TILE), bf16, pl.BlockSpec((1, HALF, TILE), tile_of))


def both_halves(near, far):
    size = near.shape[1]
    return [
        (near, pl.BlockSpec((1, size, TILE), lambda j, *_: (jnp.minimum(j, 1), 0, 0))),
        (far, pl.BlockSpec((1, size, TILE), lambda j, *_: (jnp.maximum(j - 2, 0), 0, 0))),
    ]


def store_grad(keep, away, at, size, value):
    there = pl.ds(at, size)
    keep[0, :, there] = value[:HALF]
    away[0, :, there] = value[HALF:]


def down_back_body(
    place, d_out, tab, mlp_out, order, act_n, act_r, g_keep, g_send, d_mlp, d_gate, d_mlp_t
):
    rows = d_out.shape[1]
    step = pl.program_id(0)
    core = place[0] % 2

    @pl.when(step == 0)
    def _():
        for i in range(BLOCKS):
            grad = d_out[i].astype(f32)
            d_mlp[i * rows : (i + 1) * rows] = (grad * tab[i, 5:6]).astype(bf16)
            d_gate[i] = col_sum(grad * mlp_out[i].astype(f32))
        d_mlp_t[...] = dot_cols(order[...], d_mlp[...]).astype(bf16)

    @pl.when(step < 2)
    def _():
        store_grad(g_keep, g_send, 0, TILE, dot(d_mlp_t[...], act_n[0]).astype(bf16))

    @pl.when(step >= 2)
    def _():
        for index in range(2):
            value = act_r[0, :, index * HALF : (index + 1) * HALF]
            at = pl.multiple_of((core if index == 0 else 1 - core) * HALF, 128)
            store_grad(g_keep, g_send, at, HALF, dot(d_mlp_t[...], value).astype(bf16))


def down_back(place, d_out, tab, mlp_out, order, act_n, act_r, deps=()):
    total = BLOCKS * d_out.shape[1]
    return run(
        down_back_body,
        (4,),
        [(d_out, None), (tab, None), (mlp_out, None), (order, None)] + both_halves(act_n, act_r),
        [MLP_GRAD, MLP_GRAD, ((total, D), bf16, None), ((BLOCKS, 1, D), f32, None)],
        scratch=[pltpu.VMEM((D, total), bf16)],
        scalars=(place,),
        flops=2 * total * D * 5 * D,
        deps=deps,
    )


def up_back_body(
    place, d_out, tab, d_mlp, normed, u_n, u_r,
    up_n, down_n, up_0, up_1, up_2, up_3, down_0, down_1, down_2, down_3,
    middle, attn_out, proj_n, proj_r, mixed_n, mixed_r, order,
    g_keep, g_send, p_keep, p_send, d_middle, d_mix_n, d_mix_r, d_mod,
    d_attn, turned, acc,
):
    rows = d_out.shape[1]
    step = pl.program_id(0)
    core = place[0] % 2

    @pl.when(step == 0)
    def _():
        turned[...] = dot_cols(order[...], flat(normed)).astype(bf16)

    def back(u, ups, downs, places):
        start = 0
        total = None
        ups = [far_up(up) for up in ups]
        for up, down, at in zip(ups, downs, places):
            size = up.shape[1]
            pre = u[0, :, start : start + size].astype(f32)
            start = start + size
            tanh, rate = gelu_parts(pre)
            slope = 0.5 * (1.0 + tanh) + (0.5 * rate) * pre * (1.0 - tanh * tanh) * (
                1.0 + (3.0 * 0.044715) * (pre * pre)
            )
            d_up = (slope * dot_cols(d_mlp[...], down[...])).astype(bf16)
            store_grad(g_keep, g_send, at, size, dot(turned[...], d_up).astype(bf16))
            term = dot_cols(d_up, up)
            total = term if total is None else total + term
        return total

    both = [pl.multiple_of(core * HALF, 128), pl.multiple_of((1 - core) * HALF, 128)]
    first, second = matching(place, down_0, down_1, down_2, down_3)

    @pl.when(step == 0)
    def _():
        acc[...] = back(u_n, [up_n], [down_n], [0])

    @pl.when(step == 1)
    def _():
        acc[...] += back(u_n, [up_n], [down_n], [0])

    @pl.when(step == 2)
    def _():
        acc[...] += back(u_r, [up_0, up_1], first(), both)

    @pl.when(step == 3)
    def _():
        acc[...] += back(u_r, [up_2, up_3], second(), both)
        for i in range(BLOCKS):
            at = slice(i * rows, (i + 1) * rows)
            d_normed = acc[at]
            unit, inverse = unit_rows(middle[i])
            grad = d_out[i].astype(f32) + norm_back(d_normed, unit, inverse, tab[i, 4:5])
            d_middle[i] = grad
            d_mod[i, 0:1] = col_sum(grad * attn_out[i].astype(f32))
            d_mod[i, 1:2] = col_sum(d_normed)
            d_mod[i, 2:3] = col_sum(d_normed * unit)
            d_attn[at] = (grad * tab[i, 2:3]).astype(bf16)
        turned[...] = dot_cols(order[...], d_attn[...]).astype(bf16)
        d_rows_n = dot_cols(d_attn[...], proj_n[...])
        far = block(proj_r)
        d_rows_r = dot_cols(d_attn[:, :HALF], far[:HALF]) + dot_cols(d_attn[:, HALF:], far[HALF:])
        for side, mixed, d_rows, d_mix in (
            (0, mixed_n, d_rows_n, d_mix_n),
            (1, mixed_r, d_rows_r, d_mix_r),
        ):
            d_mix[...] = d_rows.astype(bf16).reshape(d_mix.shape)
            g_proj = dot(turned[...], flat(mixed)).astype(bf16)
            p_keep[side] = g_proj[:HALF]
            p_send[side] = g_proj[HALF:]


def up_back(place, d_out, tab, d_mlp, saved, weights, proj_n, w_r, mixed_n, mixed_r, order, deps=()):
    attn_out, middle, normed, u_n, u_r = saved
    up, down, ups, downs = weights
    rows = d_out.shape[1]
    total = BLOCKS * rows
    here = lambda j: jnp.minimum(j, 1)
    return run(
        up_back_body,
        (4,),
        [(d_out, None), (tab, None), (d_mlp, None), (normed, None)]
        + both_halves(u_n, u_r)
        + [
            (up, pl.BlockSpec((D, TILE), lambda j, *_: (0, here(j)))),
            (down, pl.BlockSpec((TILE, D), lambda j, *_: (here(j), 0))),
        ]
        + far_ins(ups, downs)
        + [
            (middle, None),
            (attn_out, None),
            (proj_n, None),
            projection(w_r),
            (mixed_n, None),
            (mixed_r, None),
            (order, None),
        ],
        [
            MLP_GRAD,
            MLP_GRAD,
            ((2, HALF, HALF), bf16, None),
            ((2, HALF, HALF), bf16, None),
            (d_out.shape, f32, None),
            (mixed_n.shape, bf16, None),
            (mixed_n.shape, bf16, None),
            ((BLOCKS, 3, D), f32, None),
        ],
        scratch=[
            pltpu.VMEM((total, D), bf16),
            pltpu.VMEM((D, total), bf16),
            pltpu.VMEM((total, D), f32),
        ],
        scalars=(place,),
        flops=2 * total * D * (12 * D + 4 * D),
        deps=deps,
    )


def qkv_back_steps(step, grads, w, turned, p_keep, p_send, g_keep, g_send, acc, start):
    total = grads[0].shape[0] * grads[0].shape[1]

    for index, grad in enumerate(grads):

        @pl.when(step == index)
        def _(index=index, grad=grad):
            value = flat(grad)
            term = dot_cols(value, block(w))
            if index == 0:
                g_w = dot(turned[:, :total], value).astype(bf16)
                start(term)
            else:
                g_w = dot(turned[...], value).astype(bf16)
                acc[...] += term
            g_keep[...] = g_w[:HALF]
            g_send[...] = g_w[HALF:]

    @pl.when(step == 3)
    def _():
        g_keep[...] = p_keep[0]
        g_send[...] = p_send[0]


def qkv_back_body(
    dq, dk, dv, w, normed, order, p_keep, p_send, g_keep, g_send, turned, acc
):
    total = dq.shape[0] * dq.shape[1]
    step = pl.program_id(0)

    @pl.when(step == 0)
    def _():
        turned[...] = dot_cols(order[...], flat(normed)).astype(bf16)

    def start(term):
        acc[:total] = term
        acc[total:] = jnp.zeros((total, D), f32)

    qkv_back_steps(step, (dq, dk, dv), w, turned, p_keep, p_send, g_keep, g_send, acc, start)


def qkv_back_next_body(
    dq, dk, dv, w, turned, before, p_keep, p_send, g_keep, g_send, d_own, d_oth, acc
):
    total = dq.shape[0] * dq.shape[1]
    step = pl.program_id(0)

    def start(term):
        acc[...] = before[...]
        acc[:total] += term

    qkv_back_steps(step, (dq, dk, dv), w, turned, p_keep, p_send, g_keep, g_send, acc, start)

    @pl.when(step == 3)
    def _():
        d_own[...] = acc[:total]
        d_oth[...] = acc[total:].astype(bf16)


def qkv_back(first, side, grads, w, normed, order, turned, before, p_keep, p_send, deps=()):
    rows = normed.shape[2]
    total = BLOCKS * rows
    grad = ((HALF, 4 * HALF), bf16, pl.BlockSpec((HALF, HALF), lambda j: (0, j)))
    piece = pl.BlockSpec((1, HALF, HALF), lambda j: (side, 0, 0))
    ins = [(g, None) for g in grads]
    ins += [block_at(w, lambda j: jnp.minimum(j, 2))]
    ends = [(p_keep, piece), (p_send, piece)]
    flops = 2 * total * D * 10 * HALF
    if first:
        return run(
            qkv_back_body,
            (4,),
            ins + [(normed, None), (order, None)] + ends,
            [grad, grad, ((D, 2 * total), bf16, None), ((2 * total, D), f32, None)],
            flops=flops + 4 * total * D * D,
            deps=deps,
        )
    return run(
        qkv_back_next_body,
        (4,),
        ins + [(turned, None), (before, None)] + ends,
        [grad, grad, ((total, D), f32, None), ((total, D), bf16, None)],
        scratch=[pltpu.VMEM((2 * total, D), f32)],
        flops=flops,
        deps=deps,
    )


def finish_body(d_own, d_got, own, tab, d_middle, d_rows, d_mod):
    rows = own.shape[1]
    for i in range(BLOCKS):
        at = slice(i * rows, (i + 1) * rows)
        d_normed = d_own[at] + d_got[at].astype(f32)
        unit, inverse = unit_rows(own[i].astype(f32))
        grad = d_middle[i] + norm_back(d_normed, unit, inverse, tab[i, 1:2])
        d_rows[i] = grad.astype(bf16)
        d_mod[i, 0:1] = col_sum(d_normed)
        d_mod[i, 1:2] = col_sum(d_normed * unit)


def finish(d_own, d_got, own, tab, d_middle, deps=()):
    return run(
        finish_body,
        (1,),
        [(d_own, None), (d_got, None), (own, None), (tab, None), (d_middle, None)],
        [(own.shape, bf16, None), ((BLOCKS, 2, D), f32, None)],
        deps=deps,
    )


def pick_body(index, own, oth, out):
    spot = lax.broadcasted_iota(jnp.int32, (1, own.shape[0]), 1)
    here = (index[...] == spot).astype(bf16)
    there = (index[...] - own.shape[0] == spot).astype(bf16)
    out[...] = (dot(here, own[...]) + dot(there, oth[...])).astype(bf16)


def pick(index, own, oth, deps=()):
    count = index.shape[0]
    return run(
        pick_body,
        (1,),
        [(index, None), (own, None), (oth, None)],
        [((count, D), bf16, None)],
        flops=2 * count * GROUP * D,
        deps=deps,
    )[0]


def put_body(index_own, index_oth, own, oth, base, out):
    spot = lax.broadcasted_iota(jnp.int32, (base.shape[0], 1), 0)
    here = (index_own[...] == spot).astype(f32)
    there = (index_oth[...] == spot).astype(f32)
    hit = jnp.sum(here, axis=1, keepdims=True) + jnp.sum(there, axis=1, keepdims=True)
    put = dot(here.astype(bf16), own[...]) + dot(there.astype(bf16), oth[...])
    out[...] = jnp.where(hit > 0.5, put, base[...].astype(f32)).astype(bf16)


def put(index_own, index_oth, own, oth, base, deps=()):
    return run(
        put_body,
        (1,),
        [(index_own, None), (index_oth, None), (own, None), (oth, None), (base, None)],
        [(base.shape, bf16, None)],
        flops=2 * base.shape[0] * KEEP * D,
        deps=deps,
    )[0]


def on_device(
    n_dp,
    tokens,
    conditioning,
    segment_ids,
    kept_rows,
    cotangent,
    mod_first,
    qkv_first,
    proj_first,
    up_first,
    down_first,
    mod_second,
    qkv_second,
    proj_second,
    up_second,
    down_second,
):
    dp_pos = lax.axis_index("dp")
    side = lax.axis_index("tensor")
    core = dp_pos % 2
    bits = n_dp.bit_length() - 1

    def moves(where):
        pairs = []
        for dp in range(n_dp):
            for t in range(2):
                to_dp, to_t = where(dp, t)
                pairs.append((dp * 2 + t, to_dp * 2 + to_t))
        return pairs

    across = moves(lambda dp, t: (dp, 1 - t))
    core_swap = moves(lambda dp, t: (dp ^ 1, t))
    next_swap = moves(lambda dp, t: (dp ^ 2, t))
    turn = moves(lambda dp, t: (dp // 2 * 2 + t, dp % 2))
    deal = moves(lambda dp, t: (dp // 2 * 2 + 1 - t, dp % 2))
    undeal = moves(lambda dp, t: (dp // 2 * 2 + t, 1 - dp % 2))

    def send(value, pairs):
        return lax.ppermute(value, ALL, pairs)

    def after(value, *deps):
        return lax.optimization_barrier((value, *deps))[0]

    def to_owner(rows):
        tiles = rows.reshape(BLOCKS, SPAN // 2, D)
        return send(tiles[0::2], turn), send(tiles[1::2], deal)

    def owned(even, odd, *when):
        even, odd = after(even, *when), after(odd, *when)
        return jnp.where(core == 0, jnp.concatenate([even, odd]), jnp.concatenate([odd, even]))

    def from_owner(rows, begin=(), end=()):
        rows = after(rows.reshape(BLOCKS, SPAN // 2, D), *begin)
        even = after(send(lax.dynamic_slice_in_dim(rows, 2 * core, 3), turn), *end)
        odd = after(send(lax.dynamic_slice_in_dim(rows, 3 * (1 - core), 2), undeal), *end)
        shape = (3, 2, SPAN // 2, D)
        odd = jnp.pad(odd, ((0, 1), (0, 0), (0, 0)))
        even = jnp.broadcast_to(even[:, None], shape)
        odd = jnp.broadcast_to(odd[:, None], shape)
        second = lax.broadcasted_iota(jnp.int32, shape, 1) == 1
        both = jnp.where(second, odd, even).reshape(6 * SPAN // 2, D)
        return both[: BLOCKS * SPAN // 2]

    class Far:
        def __init__(self, near, bit, deps=()):
            self.swap = moves(lambda dp, t: (dp ^ 2**bit, t))
            self.first = send(after(near, *deps), across)

        def hop(self, *deps):
            first = after(self.first, *deps)
            self.third = send(first, self.swap)
            self.second = send(first, core_swap)

        def end(self, *deps):
            return self.first, self.second, self.third, send(after(self.third, *deps), core_swap)

    def part_of(value, axis, bit):
        size = value.shape[axis] // 4
        part = dp_pos // 2**bit % 2 * 2 + core
        return lax.dynamic_slice_in_dim(value, part * size, size, axis)

    numbers = send(jnp.concatenate([kept_rows, segment_ids[::SPAN]]), turn)
    cond = send(jax.nn.silu(conditioning.astype(f32)).astype(bf16), turn)
    wq_one = jnp.transpose(qkv_first, (1, 0, 2))
    wq_two = jnp.transpose(qkv_second, (1, 0, 2))
    place_ref = dp_pos.reshape(1).astype(jnp.int32)
    zero_ref = jnp.zeros((1,), jnp.int32)
    quarter_at = dp_pos // 2 % 2 * 2 + core
    proj_part = lax.dynamic_slice(
        proj_first, (quarter_at % 2 * (D // 4), quarter_at // 2 * HALF), (D // 4, HALF)
    )
    near_part = jnp.concatenate([part_of(wq_one, 1, 1), proj_part[None]])
    kept, segs = numbers[:KEEP], numbers[KEEP:]
    kind = jnp.where(segs[3] == segs[0], 0, jnp.where(segs[4] == segs[1], 1, 2)).reshape(1)
    slot_hot = segs[:, None] == jnp.arange(SLOTS, dtype=jnp.int32)[None, :]
    cond_rows = jnp.dot(slot_hot.astype(bf16), cond, preferred_element_type=f32).astype(bf16)

    def table(mod):
        return jnp.dot(cond_rows, mod, preferred_element_type=f32).reshape(BLOCKS, 6, D)

    arrived = to_owner(tokens)
    cond_rows = after(cond_rows, *arrived)
    tab_one, tab_two = table(mod_first), table(mod_second)

    block_of, inside = kept // SPAN, kept % SPAN
    spot = (
        jnp.where(inside // (SPAN // 2) == core, 0, GROUP // 2)
        + block_of * (SPAN // 2)
        + inside % (SPAN // 2)
    ).reshape(BLOCKS, 2, KEEP // (2 * BLOCKS))
    spot_own = lax.dynamic_slice_in_dim(spot, core, 1, 1).reshape(-1)
    spot_oth = lax.dynamic_slice_in_dim(spot, 1 - core, 1, 1).reshape(-1)
    spot_all = jnp.concatenate([spot_own, spot_oth])

    piece = D // n_dp
    row = jnp.arange(D, dtype=jnp.int32)
    turned = jnp.zeros_like(row)
    for bit in range(bits):
        turned = turned + (((row // piece) // 2 ** (bits - 1 - bit)) % 2) * 2**bit
    source = jnp.bitwise_xor(turned, dp_pos) * piece + row % piece
    order = (source[:, None] == row[None, :]).astype(bf16)
    pieces = min(n_dp, 16)
    deep = D // pieces
    which = dp_pos % pieces
    at = which * deep
    proj_piece = lax.dynamic_slice(
        proj_second, (at % HALF, at // HALF * HALF), (deep, HALF)
    )
    up_piece = lax.dynamic_slice_in_dim(up_second, at, deep).reshape(deep, 4, HALF)
    down_pieces = [
        lax.dynamic_slice_in_dim(down_second, row * D + at, deep).reshape(deep, 2, HALF)
        for row in range(2)
    ]
    pieces_two = jnp.concatenate(
        [
            lax.dynamic_slice_in_dim(wq_two, at, deep, 1),
            proj_piece[None],
            jnp.transpose(up_piece, (1, 0, 2)),
        ]
        + [down_pieces[row][None, :, column] for column in range(2) for row in range(2)]
    )
    w_one_parts = Far(near_part, 1, arrived)
    own = owned(*arrived, tab_one, tab_two, w_one_parts.first, order)
    piece_two = send(after(pieces_two, own), across)
    oth = send(own, core_swap)

    def add(*terms):
        return functools.reduce(lambda p, q: p + q, [t.astype(f32) for t in terms])

    quarter = HALF // 2

    class Total:
        def cores(self, keep, away):
            got = send(away, core_swap)
            self.keep_n, self.keep_r, self.got_n, self.got_r = keep[0], keep[1], got[0], got[1]
            return self

        def cores_far(self, keep, away):
            self.keep_r, self.got_r = keep, send(away, core_swap)
            return self

        def cores_near(self, keep, away):
            self.keep_n, self.got_n = keep, send(away, core_swap)
            return self

        def far(self, *when):
            away = add(self.keep_r, after(self.got_r, *when)).astype(bf16)
            self.got = send(away, across)
            return (away,)

        def chips(self, *when):
            return add(self.keep_n, self.got_n, after(self.got, *when)).astype(bf16)

        def near(self, *when):
            terms = (self.keep_n, self.got_n, after(self.got, *when))
            away = add(*[t[quarter:] for t in terms]).astype(bf16)
            self.got = send(away, next_swap)
            self.terms = tuple(t[:quarter] for t in terms)
            return (away,)

        def sum(self, *when):
            return add(*self.terms, after(self.got, *when))

    class Rest:
        def __init__(self, acc, bit=2):
            self.acc, self.got, self.bit = acc, None, bit

        def next(self, *when):
            if self.bit == bits:
                return ()
            acc = self.acc
            if self.got is not None:
                acc = acc + after(self.got, *when).astype(f32)
            self.acc = acc
            size = self.acc.shape[0] // 2
            away = self.acc[size:].astype(bf16)
            bit = self.bit
            self.got = send(away, moves(lambda dp, t: (dp ^ 2**bit, t)))
            self.acc = self.acc[:size]
            self.bit = bit + 1
            return (away,)

        def sum(self, *when):
            return self.acc + after(self.got, *when).astype(f32)

        def end(self, *when):
            while self.bit < bits:
                self.next(*when)
            return self.acc + after(self.got, *when).astype(f32)

    normed_one, *near_one = project_first(own, oth, tab_one, wq_one)
    ups_one = Far(part_of(up_first, 1, 1), 1, (normed_one,))
    downs_one = Far(part_of(down_first, 0, 2), 2, (normed_one,))
    w_one_parts.hop(own)
    mixed_one_n = attend(kind, *near_one)
    w_parts = w_one_parts.end(normed_one)
    w_two_far = lax.all_gather(
        after(piece_two, normed_one)[None],
        "dp",
        axis=0,
        tiled=True,
        axis_index_groups=[
            list(range(first, first + pieces)) for first in range(0, n_dp, pieces)
        ],
    )
    far_two_mlp = ([w_two_far] * 4, [w_two_far] * 4)
    w_one_far, *far_one = project_parts(
        place_ref, normed_one, w_parts, deps=(mixed_one_n, ups_one.first, downs_one.first)
    )
    ups_one.hop(w_one_far)
    downs_one.hop(w_one_far)
    mixed_one_r = attend(kind, *far_one)
    attn_one, middle_one, normed_mlp_one, u_one_n, act_one_n, acc = feed_near(
        mixed_one_n, mixed_one_r, proj_first, w_one_far, own, tab_one, up_first, down_first
    )
    ups_one, downs_one = ups_one.end(normed_mlp_one), downs_one.end(normed_mlp_one)
    mlp_one = (up_first, down_first, ups_one, downs_one)
    cot_parts = to_owner(after(cotangent, normed_mlp_one))
    u_one_r, act_one_r, mlp_out_one, out_one = feed_far(
        place_ref, normed_mlp_one, acc, middle_one, tab_one, ups_one, downs_one
    )
    first_own = out_one.reshape(-1, D)
    first_oth = send(first_own, core_swap)

    routed = pick(spot_all[:, None], first_own, first_oth)
    routed_own, routed_oth = routed.reshape(2, BLOCKS, KEEP // (2 * BLOCKS), D)
    normed_two, *near_two = project_first(routed_own, routed_oth, tab_two, wq_two)
    mixed_two_n = attend(kind, *near_two)
    far_two = project_next(normed_two, w_two_far, deps=(mixed_two_n,))
    mixed_two_r = attend(kind, *far_two)
    cot_own = owned(*cot_parts, mixed_two_r)
    cot_oth = send(cot_own, core_swap)
    attn_two, middle_two, normed_mlp_two, u_two_n, act_two_n, acc = feed_near(
        mixed_two_n, mixed_two_r, proj_second, w_two_far, routed_own, tab_two, up_second,
        down_second,
    )
    first_out = from_owner(out_one, (mixed_two_r,), (normed_mlp_two,))
    mlp_two = (up_second, down_second, *far_two_mlp)
    u_two_r, act_two_r, mlp_out_two, out_two = feed_far(
        zero_ref, normed_mlp_two, acc, middle_two, tab_two, *mlp_two[2:], deps=(first_out,)
    )
    second_own = out_two.reshape(-1, D)
    second_oth = send(second_own, core_swap)
    cot_routed = pick(
        spot_own[:, None], cot_own.reshape(-1, D), cot_oth.reshape(-1, D), deps=(second_own,)
    ).reshape(routed_own.shape)

    g_keep, g_send, d_mlp, d_gate_two = down_back(
        zero_ref, cot_routed, tab_two, mlp_out_two, order, act_two_n, act_two_r
    )
    down_two = Total().cores(g_keep, g_send)
    saved = (attn_two, middle_two, normed_mlp_two, u_two_n, u_two_r)
    g_keep, g_send, p_keep, p_send, d_middle, d_mix_n, d_mix_r, d_mod_two = up_back(
        zero_ref, cot_routed, tab_two, d_mlp, saved, mlp_two, proj_second, w_two_far, mixed_two_n,
        mixed_two_r, order,
    )
    up_two = Total().cores(g_keep, g_send)
    sent = down_two.far(d_mix_r)
    grads_r = attend_back(kind, *far_two, d_mix_r, deps=sent)
    sent = up_two.far(grads_r[0])
    qr_keep, qr_send, normed_t, acc = qkv_back(
        True, 1, grads_r, w_two_far, normed_two, order, None, None, p_keep, p_send, deps=sent
    )
    qkv_two = Total().cores_far(qr_keep, qr_send)
    grads_n = attend_back(kind, *near_two, d_mix_n, deps=(acc, down_two.got))
    sent = qkv_two.far(grads_n[0])
    qn_keep, qn_send, d_own, d_oth = qkv_back(
        False, 0, grads_n, wq_two, normed_two, None, normed_t, acc, p_keep, p_send, deps=sent
    )
    d_got = send(d_oth, core_swap)
    qkv_two.cores_near(qn_keep, qn_send)
    d_two, d_mod_two_a = finish(
        d_own, d_got, routed_own, tab_two, d_middle
    )
    d_two_own = d_two.reshape(-1, D)
    d_two_oth = send(d_two_own, core_swap)

    def slot_sums(*parts):
        per_block = jnp.concatenate(parts, axis=1).reshape(BLOCKS, -1)
        return lax.dot_general(
            slot_hot.astype(f32),
            per_block,
            (((0,), (0,)), ((), ())),
            precision=lax.Precision.HIGHEST,
        ).astype(bf16)

    routed_rows = put(
        spot_own[None], spot_oth[None], second_own, second_oth, first_own, deps=(d_two_own,)
    )
    d_first = put(
        spot_own[None], spot_oth[None], d_two_own, d_two_oth, cot_own.reshape(-1, D),
        deps=(routed_rows,),
    ).reshape(own.shape)
    g_keep, g_send, d_mlp, d_gate = down_back(
        place_ref, d_first, tab_one, mlp_out_one, order, act_one_n, act_one_r, deps=(up_two.got,)
    )
    down_one = Total().cores(g_keep, g_send)
    mlp_rest_two = Rest(jnp.concatenate([t.chips(d_mlp) for t in (down_two, up_two)], axis=1), 1)
    sent = mlp_rest_two.next()
    saved = (attn_one, middle_one, normed_mlp_one, u_one_n, u_one_r)
    g_keep, g_send, p_keep, p_send, d_middle, d_mix_n, d_mix_r, d_mod = up_back(
        place_ref, d_first, tab_one, d_mlp, saved, mlp_one, proj_first, w_one_far, mixed_one_n,
        mixed_one_r, order, deps=sent,
    )
    up_one = Total().cores(g_keep, g_send)
    qkv_rest_two = Rest(qkv_two.chips(d_mix_r), 1)
    sent = (*down_one.far(d_mix_r), *qkv_rest_two.next())
    early = lax.all_gather(
        jnp.concatenate(
            [cond, slot_sums(d_mod_two_a, d_mod_two, d_gate_two), slot_sums(d_mod, d_gate)], axis=1
        ),
        ALL,
        axis=0,
        tiled=True,
    )
    grads_r = attend_back(kind, *far_one, d_mix_r, deps=sent)
    rest_two = Rest(
        jnp.concatenate([t.sum(grads_r[0]) for t in (mlp_rest_two, qkv_rest_two)], axis=1)
    )
    sent = (*up_one.far(grads_r[0]), *rest_two.next())
    qr_keep, qr_send, normed_t, acc = qkv_back(
        True, 1, grads_r, w_one_far, normed_one, order, None, None, p_keep, p_send,
        deps=sent,
    )
    qkv_one = Total().cores_far(qr_keep, qr_send)
    sent = down_one.near(acc)
    grads_n = attend_back(kind, *near_one, d_mix_n, deps=sent)
    done = grads_n[0]
    sent = (*qkv_one.far(done), *up_one.near(done), *rest_two.next(done))
    qn_keep, qn_send, d_own, d_oth = qkv_back(
        False, 0, grads_n, wq_one, normed_one, None, normed_t, acc, p_keep, p_send, deps=sent
    )
    d_got = send(d_oth, core_swap)
    qkv_one.cores_near(qn_keep, qn_send)
    routed_out = from_owner(routed_rows, (grads_r[0],), (d_own,))
    mlp_rest = Rest(jnp.concatenate([down_one.sum(d_own), up_one.sum(d_own)], axis=1))
    sent = (*mlp_rest.next(), routed_out)
    d_one, d_mod_a = finish(d_own, d_got, own, tab_one, d_middle, deps=(*sent, qkv_one.got_n))

    last = qkv_one.near(d_one)
    late = after(jnp.pad(slot_sums(d_mod_a), ((0, 8 - SLOTS), (0, 0))), *last)
    late = (late.astype(f32) + send(late, core_swap).astype(f32)).astype(bf16)[None]
    sources = jnp.array([dp_pos * 2 + side])

    def doubled(late, sources, mask):
        pairs = moves(lambda dp, t: ((dp * 2 + t ^ mask) // 2, (t ^ mask) % 2))
        late = jnp.concatenate([late, send(late, pairs)])
        return late, jnp.concatenate([sources, jnp.bitwise_xor(sources, mask)])

    late, sources = doubled(late, sources, 1)
    qkv_rest = Rest(qkv_one.sum(late))
    last = qkv_rest.next()
    mlp_rest.next(*last)
    for bit in range(2, bits):
        late, sources = doubled(after(late, *last), sources, 2**bit)
        last = qkv_rest.next(late) or last
    late, sources = doubled(after(late, *last), sources, 2**bits)
    input_grad = from_owner(d_one, (), last).astype(f32)
    early = after(early, *last)
    mlp_total = mlp_rest.end(*last)
    total_two = rest_two.end(*last)
    qkv_total = qkv_rest.end(late)

    mod_rows = D // (n_dp * 2)
    mine = lax.dynamic_slice_in_dim(early[:, :D], (dp_pos * 2 + side) * mod_rows, mod_rows, 1)
    mine_late = jnp.pad(
        mine.reshape(-1, SLOTS, mod_rows)[sources], ((0, 0), (0, 8 - SLOTS), (0, 0))
    ).reshape(-1, mod_rows)
    mod_two_end = 7 * D
    mod_one = jnp.concatenate(
        [
            dot_rows(mine_late, late.reshape(-1, 2 * D)),
            dot_rows(mine, early[:, mod_two_end:]),
        ],
        axis=1,
    )
    mod_two = dot_rows(mine, early[:, D:mod_two_end])
    wide = 2 * TILE

    def placed(attention, down, up):
        qkv = attention[:, : 3 * HALF].reshape(piece, 3, HALF)
        return qkv, attention[:, 3 * HALF :].T, up, down.T

    return (
        first_out,
        routed_out,
        input_grad,
        mod_one,
        *placed(qkv_total, mlp_total[:, :wide], mlp_total[:, wide:]),
        mod_two,
        *placed(
            total_two[:, 2 * wide :].astype(f32),
            total_two[:, :wide].astype(f32),
            total_two[:, wide : 2 * wide].astype(f32),
        ),
    )


def solution(mesh):
    n_dp = mesh.shape["dp"]
    return jax.shard_map(
        functools.partial(on_device, n_dp),
        mesh=mesh,
        in_specs=(
            P(("dp", "tensor"), None),
            P("dp", None),
            P("dp"),
            P("dp"),
            P(("dp", "tensor"), None),
            P(),
            P(None, None, "tensor"),
            P("tensor", None),
            P(None, "tensor"),
            P("tensor", None),
            P(),
            P(None, None, "tensor"),
            P("tensor", None),
            P(None, "tensor"),
            P("tensor", None),
        ),
        out_specs=(
            P(("dp", "tensor"), None),
            P(("dp", "tensor"), None),
            P(("dp", "tensor"), None),
            P(("dp", "tensor"), None),
            P("dp", None, "tensor"),
            P("tensor", "dp"),
            P("dp", "tensor"),
            P("tensor", "dp"),
            P(("dp", "tensor"), None),
            P("dp", None, "tensor"),
            P("tensor", "dp"),
            P("dp", "tensor"),
            P("tensor", "dp"),
        ),
        check_vma=False,
    )
```

```python
import functools

import jax
import jax.numpy as jnp
from jax import lax
from jax.experimental import pallas as pl
from jax.experimental.pallas import tpu as pltpu
from jax.sharding import PartitionSpec as P

D = 768
HEAD_DIM = 64
SLOTS = 5
GROUP = 1280
KEEP = 640
BLOCKS = 5
SPAN = GROUP // BLOCKS
HALF = D // 2
TILE = 768
NORM_EPS = 1e-06
f32 = jnp.float32
bf16 = jnp.bfloat16
ALL = ("dp", "tensor")
VMEM_BYTES = 26 * 1024 * 1024
LIGHT = 2000


def dot(left, right):
    return jnp.dot(left, right, preferred_element_type=f32)


def dot_cols(left, right):
    return lax.dot_general(left, right, (((1,), (1,)), ((), ())), preferred_element_type=f32)


def dot_rows(left, right):
    return lax.dot_general(left, right, (((0,), (0,)), ((), ())), preferred_element_type=f32)


def unit_rows(rows):
    centre = rows - jnp.mean(rows, axis=-1, keepdims=True)
    inverse = lax.rsqrt(jnp.mean(centre * centre, axis=-1, keepdims=True) + NORM_EPS)
    return centre * inverse, inverse


def norm_back(d_normed, unit, inverse, scale_row):
    e = d_normed * (1.0 + scale_row)
    return inverse * (
        e
        - jnp.mean(e, axis=-1, keepdims=True)
        - unit * jnp.mean(e * unit, axis=-1, keepdims=True)
    )


def col_sum(rows):
    return jnp.sum(rows, axis=0, keepdims=True)


def flat(ref):
    value = ref[...]
    return value.reshape(-1, value.shape[-1])


def whole(shape):
    return pl.BlockSpec(shape, lambda *_: (0,) * len(shape), pipeline_mode=pl.Buffered(1))


def run(body, grid, ins, outs, scratch=(), scalars=(), flops=0, deps=()):
    in_specs = [whole(a.shape) if s is None else s for a, s in ins]
    in_specs += [pl.BlockSpec(memory_space=pl.ANY)] * len(deps)
    first, past = len(scalars) + len(ins), len(scalars) + len(ins) + len(deps)

    def step(*refs):
        body(*refs[:first], *refs[past:])

    out_specs = [whole(sh) if s is None else s for sh, _, s in outs]
    moved = sum(a.size * a.dtype.itemsize for a, _ in ins)
    moved += sum(jnp.dtype(d).itemsize * functools.reduce(lambda p, q: p * q, sh, 1) for sh, d, _ in outs)
    return pl.pallas_call(
        step,
        grid_spec=pltpu.PrefetchScalarGridSpec(
            num_scalar_prefetch=len(scalars),
            grid=grid,
            in_specs=in_specs,
            out_specs=out_specs,
            scratch_shapes=list(scratch),
        ),
        out_shape=[jax.ShapeDtypeStruct(sh, d) for sh, d, _ in outs],
        compiler_params=pltpu.CompilerParams(
            vmem_limit_bytes=VMEM_BYTES, dimension_semantics=("arbitrary",) * len(grid)
        ),
        cost_estimate=pl.CostEstimate(
            flops=1 + int(flops) // LIGHT, bytes_accessed=1 + int(moved) // LIGHT, transcendentals=0
        ),
    )(*scalars, *[a for a, _ in ins], *deps)


def qkv_body(own, oth, tab, w, normed, q, k, v):
    rows = own.shape[1]
    step = pl.program_id(0)

    @pl.when(step == 0)
    def _():
        for side, src in ((0, own), (1, oth)):
            for i in range(BLOCKS):
                unit, _ = unit_rows(src[i].astype(f32))
                normed[side, i] = (unit * (1.0 + tab[i, 1:2]) + tab[i, 0:1]).astype(bf16)

    qkv_steps(step, normed, w, q, k, v)


def qkv_next_body(normed, w, q, k, v):
    qkv_steps(pl.program_id(0), normed, w, q, k, v)


def qkv_parts_body(place, normed, w_0, w_1, w, q, k, v):
    for index, part in enumerate((w_0, w_1)):
        at = pl.multiple_of((place[0] % 2 ^ index) * HALF, HALF)
        w[0, pl.ds(at, HALF)] = part[0]
    qkv_steps(pl.program_id(0), normed, w, q, k, v)


def block(w):
    return w[...].reshape(D, HALF)


def qkv_steps(step, normed, w, q, k, v):
    @pl.when(step == 0)
    def _():
        mine = normed[0].reshape(-1, D)
        q[...] = dot(mine, block(w)).astype(bf16).reshape(q.shape)

    for index, out in ((1, k), (2, v)):

        @pl.when(step == index)
        def _(out=out):
            out[...] = dot(flat(normed), block(w)).astype(bf16).reshape(out.shape)


def qkv_outs(rows):
    return [
        ((BLOCKS, rows, HALF), bf16, None),
        ((2, BLOCKS, rows, HALF), bf16, None),
        ((2, BLOCKS, rows, HALF), bf16, None),
    ]


BY_STEP = pl.BlockSpec((1, D, HALF), lambda j, *_: (j, 0, 0))


def block_at(w, index):
    if w.ndim == 3:
        return (w, pl.BlockSpec((1, D, HALF), lambda j, *_: (index(j), 0, 0)))
    pieces, _, rows, _ = w.shape
    return (w, pl.BlockSpec((pieces, 1, rows, HALF), lambda j, *_: (0, index(j), 0, 0)))


def project_first(own, oth, tab, w, deps=()):
    rows = own.shape[1]
    return run(
        qkv_body,
        (3,),
        [(own, None), (oth, None), (tab, None), (w, BY_STEP)],
        [((2, BLOCKS, rows, D), bf16, None)] + qkv_outs(rows),
        flops=2 * 25 * rows * D * HALF,
        deps=deps,
    )


def project_next(normed, w, deps=()):
    rows = normed.shape[2]
    ins = [(normed, None), block_at(w, lambda j: j)]
    return run(qkv_next_body, (3,), ins, qkv_outs(rows), flops=2 * 25 * rows * D * HALF, deps=deps)


def project_parts(place, normed, parts, deps=()):
    rows = normed.shape[2]
    by_step = pl.BlockSpec((1, HALF, HALF), lambda j, *_: (j, 0, 0))
    return run(
        qkv_parts_body,
        (4,),
        [(normed, None)] + [(part, by_step) for part in parts],
        [((4, D, HALF), bf16, BY_STEP)] + qkv_outs(rows),
        scalars=(place,),
        flops=2 * 25 * rows * D * HALF,
        deps=deps,
    )


def by_sequence(kind, one_sequence, long_tiles):
    @pl.when(kind < 2)
    def _():
        one_sequence(kind, 4, long_tiles)
        one_sequence(jnp.where(kind == 0, 4, 0), 1, 1)

    @pl.when(kind == 2)
    def _():
        def short(i, carry):
            one_sequence(i, 1, 1)
            return carry

        lax.fori_loop(0, BLOCKS, short, 0)


def two_heads(rows, low):
    zero = jnp.zeros_like(rows)
    return jnp.concatenate([jnp.where(low, rows, zero), jnp.where(low, zero, rows)], axis=0)


def attend_body(kind, q, k, v, out):
    rows = q.shape[1]
    low = lax.broadcasted_iota(jnp.int32, (1, 128), 1) < HEAD_DIM
    scaling = HEAD_DIM ** (-0.5)

    def one_sequence(start, count, tiles):
        keys = k[:, pl.ds(start, count)].reshape(2 * count * rows, 128)
        values = v[:, pl.ds(start, count)].reshape(2 * count * rows, 128)
        size = tiles * rows
        for part in range(count // tiles):
            at = pl.ds(start + part * tiles, tiles)
            pair = two_heads((q[at].reshape(size, 128) * scaling).astype(bf16), low)
            scores = dot_cols(pair, keys)
            shifted = jnp.exp(scores - jnp.max(scores, axis=-1, keepdims=True))
            total = jnp.sum(shifted, axis=-1, keepdims=True)
            mixed = dot(shifted.astype(bf16), values) * (1.0 / total)
            out[at] = jnp.where(low, mixed[:size], mixed[size:]).astype(bf16).reshape(tiles, rows, 128)

    by_sequence(kind[0], one_sequence, 128 // rows)


def attend(kind, q, k, v, deps=()):
    rows = q.shape[1]
    own = pl.BlockSpec((BLOCKS, rows, 128), lambda p, *_: (0, 0, p))
    every = pl.BlockSpec((2, BLOCKS, rows, 128), lambda p, *_: (0, 0, 0, p))
    return run(
        attend_body,
        (HALF // 128,),
        [(q, own), (k, every), (v, every)],
        [(q.shape, bf16, own)],
        scalars=(kind,),
        flops=16 * BLOCKS * rows * 8 * rows * HALF,
        deps=deps,
    )[0]


def attend_back_body(kind, q, k, v, d_out, dq, dk, dv, acc_k, acc_v):
    rows = q.shape[1]
    low = lax.broadcasted_iota(jnp.int32, (1, 128), 1) < HEAD_DIM
    scaling = HEAD_DIM ** (-0.5)

    def one_sequence(start, count, tiles):
        key_rows = 2 * count * rows
        keys = k[:, pl.ds(start, count)].reshape(key_rows, 128)
        values = v[:, pl.ds(start, count)].reshape(key_rows, 128)
        size = tiles * rows
        for part in range(count // tiles):
            at = pl.ds(start + part * tiles, tiles)
            pair = two_heads((q[at].reshape(size, 128) * scaling).astype(bf16), low)
            d_pair = two_heads(d_out[at].reshape(size, 128), low)
            scores = dot_cols(keys, pair)
            shifted = jnp.exp(scores - jnp.max(scores, axis=0, keepdims=True))
            probs = shifted * (1.0 / jnp.sum(shifted, axis=0, keepdims=True))
            d_probs = dot_cols(values, d_pair)
            row_sum = jnp.sum(probs * d_probs, axis=0, keepdims=True)
            d_scores = (probs * (d_probs - row_sum)).astype(bf16)
            add_v = dot(probs.astype(bf16), d_pair)
            add_k = dot(d_scores, pair)
            if part == 0:
                acc_v[:key_rows] = add_v
                acc_k[:key_rows] = add_k
            else:
                acc_v[:key_rows] += add_v
                acc_k[:key_rows] += add_k
            both = dot_rows(d_scores, keys) * scaling
            dq[at] = jnp.where(low, both[:size], both[size:]).astype(bf16).reshape(tiles, rows, 128)
        dk[:, pl.ds(start, count)] = acc_k[:key_rows].astype(bf16).reshape(2, count, rows, 128)
        dv[:, pl.ds(start, count)] = acc_v[:key_rows].astype(bf16).reshape(2, count, rows, 128)

    by_sequence(kind[0], one_sequence, 128 // rows)


def attend_back(kind, q, k, v, d_out, deps=()):
    rows = q.shape[1]
    own = pl.BlockSpec((BLOCKS, rows, 128), lambda p, *_: (0, 0, p))
    every = pl.BlockSpec((2, BLOCKS, rows, 128), lambda p, *_: (0, 0, 0, p))
    return run(
        attend_back_body,
        (HALF // 128,),
        [(q, own), (k, every), (v, every), (d_out, own)],
        [(q.shape, bf16, own), (k.shape, bf16, every), (v.shape, bf16, every)],
        scratch=[pltpu.VMEM((8 * rows, 128), f32), pltpu.VMEM((8 * rows, 128), f32)],
        scalars=(kind,),
        flops=40 * BLOCKS * rows * 8 * rows * HALF,
        deps=deps,
    )


def gelu_parts(u):
    rate = 0.7978845608028654
    inner = rate * (u + 0.044715 * (u * u * u))
    return jnp.tanh(inner), rate


def hidden(normed, ups, downs, u, act):
    start = 0
    total = None
    ups = [far_up(up) for up in ups]
    for up, down in zip(ups, downs):
        at = slice(start, start + up.shape[1])
        start = start + up.shape[1]
        pre = dot(flat(normed), up)
        u[0, :, at] = pre.astype(bf16)
        tanh, _ = gelu_parts(pre)
        value = (0.5 * pre * (1.0 + tanh)).astype(bf16)
        act[0, :, at] = value
        term = dot(value, down[...])
        total = term if total is None else total + term
    return total


def mlp_near_body(
    mixed_n, mixed_r, proj_n, proj_r, own, tab, up, down,
    attn_out, middle, normed, u, act, acc,
):
    rows = own.shape[1]
    step = pl.program_id(0)

    @pl.when(step == 0)
    def _():
        for at in (slice(0, HALF), slice(HALF, D)):
            acc[:, at] = dot(flat(mixed_n), proj_n[:, at]) + dot(flat(mixed_r), block(proj_r)[at])
        for i in range(BLOCKS):
            attn = acc[i * rows : (i + 1) * rows]
            attn_out[i] = attn.astype(bf16)
            mid = own[i].astype(f32) + tab[i, 2:3] * attn
            middle[i] = mid
            unit, _ = unit_rows(mid)
            normed[i] = (unit * (1.0 + tab[i, 4:5]) + tab[i, 3:4]).astype(bf16)
        acc[...] = hidden(normed, [up], [down], u, act)

    @pl.when(step == 1)
    def _():
        acc[...] += hidden(normed, [up], [down], u, act)


def matching(place, down_0, down_1, down_2, down_3):
    refs = (down_0, down_1, down_2, down_3)
    if len(down_0.shape) > 2:
        return (lambda: far_downs(refs)[:2]), (lambda: far_downs(refs)[2:])
    same = (place[0] // 2 + place[0] // 4) % 2 == 0

    def first():
        return [
            jnp.where(same, down_0[...], down_2[...]),
            jnp.where(same, down_1[...], down_3[...]),
        ]

    def second():
        return [
            jnp.where(same, down_2[...], down_0[...]),
            jnp.where(same, down_3[...], down_1[...]),
        ]

    return first, second


def mlp_far_body(
    place, normed, start, middle, tab, up_0, up_1, up_2, up_3, down_0, down_1, down_2, down_3,
    u, act, mlp_out, out, acc,
):
    rows = middle.shape[1]
    step = pl.program_id(0)
    first, second = matching(place, down_0, down_1, down_2, down_3)

    @pl.when(step == 0)
    def _():
        acc[...] = start[...] + hidden(normed, [up_0, up_1], first(), u, act)

    @pl.when(step == 1)
    def _():
        acc[...] += hidden(normed, [up_2, up_3], second(), u, act)
        for i in range(BLOCKS):
            term = acc[i * rows : (i + 1) * rows]
            mlp_out[i] = term.astype(bf16)
            out[i] = (middle[i] + tab[i, 5:6] * term).astype(bf16)


def projection(w):
    return block_at(w, lambda j: 3)


def far_up(ref):
    return ref[...] if len(ref.shape) == 2 else block(ref)


def far_downs(downs):
    if len(downs[0].shape) == 2:
        return [down[...] for down in downs]
    wide = [
        jnp.concatenate([block(downs[index]), block(downs[index + 2])], axis=1) for index in range(2)
    ]
    return [wide[0][:HALF], wide[0][HALF:], wide[1][:HALF], wide[1][HALF:]]


def far_ins(ups, downs):
    if ups[0].ndim == 2:
        return [(part, None) for part in (*ups, *downs)]
    ins = []
    for index, part in enumerate((*ups, *downs)):
        pieces, _, rows, _ = part.shape
        at = pl.BlockSpec(
            (pieces, 1, rows, HALF),
            lambda *_, index=index: (0, 4 + index, 0, 0),
            pipeline_mode=pl.Buffered(1),
        )
        ins.append((part, at))
    return ins


def feed_near(mixed_n, mixed_r, proj_n, w_r, own, tab, up, down, deps=()):
    rows = own.shape[1]
    total = BLOCKS * rows
    tiles = ((2, total, TILE), bf16, pl.BlockSpec((1, total, TILE), lambda j: (j, 0, 0)))
    return run(
        mlp_near_body,
        (2,),
        [
            (mixed_n, None),
            (mixed_r, None),
            (proj_n, None),
            projection(w_r),
            (own, None),
            (tab, None),
            (up, pl.BlockSpec((D, TILE), lambda j: (0, j))),
            (down, pl.BlockSpec((TILE, D), lambda j: (j, 0))),
        ],
        [
            (own.shape, bf16, None),
            (own.shape, f32, None),
            (own.shape, bf16, None),
            tiles,
            tiles,
            ((total, D), f32, None),
        ],
        flops=2 * total * D * (D + 4 * D),
        deps=deps,
    )


def feed_far(place, normed, start, middle, tab, ups, downs, deps=()):
    total = BLOCKS * normed.shape[1]
    tiles = ((2, total, TILE), bf16, pl.BlockSpec((1, total, TILE), lambda j, *_: (j, 0, 0)))
    return run(
        mlp_far_body,
        (2,),
        [(normed, None), (start, None), (middle, None), (tab, None)]
        + far_ins(ups, downs),
        [tiles, tiles, (normed.shape, bf16, None), (normed.shape, bf16, None)],
        scratch=[pltpu.VMEM((total, D), f32)],
        scalars=(place,),
        flops=2 * total * D * (4 * D),
        deps=deps,
    )


def tile_of(j, place_ref):
    far = jnp.where(place_ref[0] // 2 % 2 == 0, j % 2, 1 - j % 2)
    return (j // 2, 0, jnp.where(j < 2, j % 2, far))


MLP_GRAD = ((2, HALF, 2 * TILE), bf16, pl.BlockSpec((1, HALF, TILE), tile_of))


def both_halves(near, far):
    size = near.shape[1]
    return [
        (near, pl.BlockSpec((1, size, TILE), lambda j, *_: (jnp.minimum(j, 1), 0, 0))),
        (far, pl.BlockSpec((1, size, TILE), lambda j, *_: (jnp.maximum(j - 2, 0), 0, 0))),
    ]


def store_grad(keep, away, at, size, value):
    there = pl.ds(at, size)
    keep[0, :, there] = value[:HALF]
    away[0, :, there] = value[HALF:]


def down_back_body(
    place, d_out, tab, mlp_out, order, act_n, act_r, g_keep, g_send, d_mlp, d_gate, d_mlp_t
):
    rows = d_out.shape[1]
    step = pl.program_id(0)
    core = place[0] % 2

    @pl.when(step == 0)
    def _():
        for i in range(BLOCKS):
            grad = d_out[i].astype(f32)
            d_mlp[i * rows : (i + 1) * rows] = (grad * tab[i, 5:6]).astype(bf16)
            d_gate[i] = col_sum(grad * mlp_out[i].astype(f32))
        d_mlp_t[...] = dot_cols(order[...], d_mlp[...]).astype(bf16)

    @pl.when(step < 2)
    def _():
        store_grad(g_keep, g_send, 0, TILE, dot(d_mlp_t[...], act_n[0]).astype(bf16))

    @pl.when(step >= 2)
    def _():
        for index in range(2):
            value = act_r[0, :, index * HALF : (index + 1) * HALF]
            at = pl.multiple_of((core if index == 0 else 1 - core) * HALF, 128)
            store_grad(g_keep, g_send, at, HALF, dot(d_mlp_t[...], value).astype(bf16))


def down_back(place, d_out, tab, mlp_out, order, act_n, act_r, deps=()):
    total = BLOCKS * d_out.shape[1]
    return run(
        down_back_body,
        (4,),
        [(d_out, None), (tab, None), (mlp_out, None), (order, None)] + both_halves(act_n, act_r),
        [MLP_GRAD, MLP_GRAD, ((total, D), bf16, None), ((BLOCKS, 1, D), f32, None)],
        scratch=[pltpu.VMEM((D, total), bf16)],
        scalars=(place,),
        flops=2 * total * D * 5 * D,
        deps=deps,
    )


def up_back_body(
    place, d_out, tab, d_mlp, normed, u_n, u_r,
    up_n, down_n, up_0, up_1, up_2, up_3, down_0, down_1, down_2, down_3,
    middle, attn_out, proj_n, proj_r, mixed_n, mixed_r, order,
    g_keep, g_send, p_keep, p_send, d_middle, d_mix_n, d_mix_r, d_mod,
    d_attn, turned, acc,
):
    rows = d_out.shape[1]
    step = pl.program_id(0)
    core = place[0] % 2

    @pl.when(step == 0)
    def _():
        turned[...] = dot_cols(order[...], flat(normed)).astype(bf16)

    def back(u, ups, downs, places):
        start = 0
        total = None
        ups = [far_up(up) for up in ups]
        for up, down, at in zip(ups, downs, places):
            size = up.shape[1]
            pre = u[0, :, start : start + size].astype(f32)
            start = start + size
            tanh, rate = gelu_parts(pre)
            slope = 0.5 * (1.0 + tanh) + (0.5 * rate) * pre * (1.0 - tanh * tanh) * (
                1.0 + (3.0 * 0.044715) * (pre * pre)
            )
            d_up = (slope * dot_cols(d_mlp[...], down[...])).astype(bf16)
            store_grad(g_keep, g_send, at, size, dot(turned[...], d_up).astype(bf16))
            term = dot_cols(d_up, up)
            total = term if total is None else total + term
        return total

    both = [pl.multiple_of(core * HALF, 128), pl.multiple_of((1 - core) * HALF, 128)]
    first, second = matching(place, down_0, down_1, down_2, down_3)

    @pl.when(step == 0)
    def _():
        acc[...] = back(u_n, [up_n], [down_n], [0])

    @pl.when(step == 1)
    def _():
        acc[...] += back(u_n, [up_n], [down_n], [0])

    @pl.when(step == 2)
    def _():
        acc[...] += back(u_r, [up_0, up_1], first(), both)

    @pl.when(step == 3)
    def _():
        acc[...] += back(u_r, [up_2, up_3], second(), both)
        for i in range(BLOCKS):
            at = slice(i * rows, (i + 1) * rows)
            d_normed = acc[at]
            unit, inverse = unit_rows(middle[i])
            grad = d_out[i].astype(f32) + norm_back(d_normed, unit, inverse, tab[i, 4:5])
            d_middle[i] = grad
            d_mod[i, 0:1] = col_sum(grad * attn_out[i].astype(f32))
            d_mod[i, 1:2] = col_sum(d_normed)
            d_mod[i, 2:3] = col_sum(d_normed * unit)
            d_attn[at] = (grad * tab[i, 2:3]).astype(bf16)
        turned[...] = dot_cols(order[...], d_attn[...]).astype(bf16)
        d_rows_n = dot_cols(d_attn[...], proj_n[...])
        far = block(proj_r)
        d_rows_r = dot_cols(d_attn[:, :HALF], far[:HALF]) + dot_cols(d_attn[:, HALF:], far[HALF:])
        for side, mixed, d_rows, d_mix in (
            (0, mixed_n, d_rows_n, d_mix_n),
            (1, mixed_r, d_rows_r, d_mix_r),
        ):
            d_mix[...] = d_rows.astype(bf16).reshape(d_mix.shape)
            g_proj = dot(turned[...], flat(mixed)).astype(bf16)
            p_keep[side] = g_proj[:HALF]
            p_send[side] = g_proj[HALF:]


def up_back(place, d_out, tab, d_mlp, saved, weights, proj_n, w_r, mixed_n, mixed_r, order, deps=()):
    attn_out, middle, normed, u_n, u_r = saved
    up, down, ups, downs = weights
    rows = d_out.shape[1]
    total = BLOCKS * rows
    here = lambda j: jnp.minimum(j, 1)
    return run(
        up_back_body,
        (4,),
        [(d_out, None), (tab, None), (d_mlp, None), (normed, None)]
        + both_halves(u_n, u_r)
        + [
            (up, pl.BlockSpec((D, TILE), lambda j, *_: (0, here(j)))),
            (down, pl.BlockSpec((TILE, D), lambda j, *_: (here(j), 0))),
        ]
        + far_ins(ups, downs)
        + [
            (middle, None),
            (attn_out, None),
            (proj_n, None),
            projection(w_r),
            (mixed_n, None),
            (mixed_r, None),
            (order, None),
        ],
        [
            MLP_GRAD,
            MLP_GRAD,
            ((2, HALF, HALF), bf16, None),
            ((2, HALF, HALF), bf16, None),
            (d_out.shape, f32, None),
            (mixed_n.shape, bf16, None),
            (mixed_n.shape, bf16, None),
            ((BLOCKS, 3, D), f32, None),
        ],
        scratch=[
            pltpu.VMEM((total, D), bf16),
            pltpu.VMEM((D, total), bf16),
            pltpu.VMEM((total, D), f32),
        ],
        scalars=(place,),
        flops=2 * total * D * (12 * D + 4 * D),
        deps=deps,
    )


def qkv_back_steps(step, grads, w, turned, p_keep, p_send, g_keep, g_send, acc, start):
    total = grads[0].shape[0] * grads[0].shape[1]

    for index, grad in enumerate(grads):

        @pl.when(step == index)
        def _(index=index, grad=grad):
            value = flat(grad)
            term = dot_cols(value, block(w))
            if index == 0:
                g_w = dot(turned[:, :total], value).astype(bf16)
                start(term)
            else:
                g_w = dot(turned[...], value).astype(bf16)
                acc[...] += term
            g_keep[...] = g_w[:HALF]
            g_send[...] = g_w[HALF:]

    @pl.when(step == 3)
    def _():
        g_keep[...] = p_keep[0]
        g_send[...] = p_send[0]


def qkv_back_body(
    dq, dk, dv, w, normed, order, p_keep, p_send, g_keep, g_send, turned, acc
):
    total = dq.shape[0] * dq.shape[1]
    step = pl.program_id(0)

    @pl.when(step == 0)
    def _():
        turned[...] = dot_cols(order[...], flat(normed)).astype(bf16)

    def start(term):
        acc[:total] = term
        acc[total:] = jnp.zeros((total, D), f32)

    qkv_back_steps(step, (dq, dk, dv), w, turned, p_keep, p_send, g_keep, g_send, acc, start)


def qkv_back_next_body(
    dq, dk, dv, w, turned, before, p_keep, p_send, g_keep, g_send, d_own, d_oth, acc
):
    total = dq.shape[0] * dq.shape[1]
    step = pl.program_id(0)

    def start(term):
        acc[...] = before[...]
        acc[:total] += term

    qkv_back_steps(step, (dq, dk, dv), w, turned, p_keep, p_send, g_keep, g_send, acc, start)

    @pl.when(step == 3)
    def _():
        d_own[...] = acc[:total]
        d_oth[...] = acc[total:].astype(bf16)


def qkv_back(first, side, grads, w, normed, order, turned, before, p_keep, p_send, deps=()):
    rows = normed.shape[2]
    total = BLOCKS * rows
    grad = ((HALF, 4 * HALF), bf16, pl.BlockSpec((HALF, HALF), lambda j: (0, j)))
    piece = pl.BlockSpec((1, HALF, HALF), lambda j: (side, 0, 0))
    ins = [(g, None) for g in grads]
    ins += [block_at(w, lambda j: jnp.minimum(j, 2))]
    ends = [(p_keep, piece), (p_send, piece)]
    flops = 2 * total * D * 10 * HALF
    if first:
        return run(
            qkv_back_body,
            (4,),
            ins + [(normed, None), (order, None)] + ends,
            [grad, grad, ((D, 2 * total), bf16, None), ((2 * total, D), f32, None)],
            flops=flops + 4 * total * D * D,
            deps=deps,
        )
    return run(
        qkv_back_next_body,
        (4,),
        ins + [(turned, None), (before, None)] + ends,
        [grad, grad, ((total, D), f32, None), ((total, D), bf16, None)],
        scratch=[pltpu.VMEM((2 * total, D), f32)],
        flops=flops,
        deps=deps,
    )


def finish_body(d_own, d_got, own, tab, d_middle, d_rows, d_mod):
    rows = own.shape[1]
    for i in range(BLOCKS):
        at = slice(i * rows, (i + 1) * rows)
        d_normed = d_own[at] + d_got[at].astype(f32)
        unit, inverse = unit_rows(own[i].astype(f32))
        grad = d_middle[i] + norm_back(d_normed, unit, inverse, tab[i, 1:2])
        d_rows[i] = grad.astype(bf16)
        d_mod[i, 0:1] = col_sum(d_normed)
        d_mod[i, 1:2] = col_sum(d_normed * unit)


def finish(d_own, d_got, own, tab, d_middle, deps=()):
    return run(
        finish_body,
        (1,),
        [(d_own, None), (d_got, None), (own, None), (tab, None), (d_middle, None)],
        [(own.shape, bf16, None), ((BLOCKS, 2, D), f32, None)],
        deps=deps,
    )


def pick_body(index, own, oth, out):
    spot = lax.broadcasted_iota(jnp.int32, (1, own.shape[0]), 1)
    here = (index[...] == spot).astype(bf16)
    there = (index[...] - own.shape[0] == spot).astype(bf16)
    out[...] = (dot(here, own[...]) + dot(there, oth[...])).astype(bf16)


def pick(index, own, oth, deps=()):
    count = index.shape[0]
    return run(
        pick_body,
        (1,),
        [(index, None), (own, None), (oth, None)],
        [((count, D), bf16, None)],
        flops=2 * count * GROUP * D,
        deps=deps,
    )[0]


def put_body(index_own, index_oth, own, oth, base, out):
    spot = lax.broadcasted_iota(jnp.int32, (base.shape[0], 1), 0)
    here = (index_own[...] == spot).astype(f32)
    there = (index_oth[...] == spot).astype(f32)
    hit = jnp.sum(here, axis=1, keepdims=True) + jnp.sum(there, axis=1, keepdims=True)
    put = dot(here.astype(bf16), own[...]) + dot(there.astype(bf16), oth[...])
    out[...] = jnp.where(hit > 0.5, put, base[...].astype(f32)).astype(bf16)


def put(index_own, index_oth, own, oth, base, deps=()):
    return run(
        put_body,
        (1,),
        [(index_own, None), (index_oth, None), (own, None), (oth, None), (base, None)],
        [(base.shape, bf16, None)],
        flops=2 * base.shape[0] * KEEP * D,
        deps=deps,
    )[0]


def on_device(
    n_dp,
    tokens,
    conditioning,
    segment_ids,
    kept_rows,
    cotangent,
    mod_first,
    qkv_first,
    proj_first,
    up_first,
    down_first,
    mod_second,
    qkv_second,
    proj_second,
    up_second,
    down_second,
):
    dp_pos = lax.axis_index("dp")
    side = lax.axis_index("tensor")
    core = dp_pos % 2
    bits = n_dp.bit_length() - 1

    def moves(where):
        pairs = []
        for dp in range(n_dp):
            for t in range(2):
                to_dp, to_t = where(dp, t)
                pairs.append((dp * 2 + t, to_dp * 2 + to_t))
        return pairs

    across = moves(lambda dp, t: (dp, 1 - t))
    core_swap = moves(lambda dp, t: (dp ^ 1, t))
    next_swap = moves(lambda dp, t: (dp ^ 2, t))
    turn = moves(lambda dp, t: (dp // 2 * 2 + t, dp % 2))
    deal = moves(lambda dp, t: (dp // 2 * 2 + 1 - t, dp % 2))
    undeal = moves(lambda dp, t: (dp // 2 * 2 + t, 1 - dp % 2))

    def send(value, pairs):
        return lax.ppermute(value, ALL, pairs)

    def after(value, *deps):
        return lax.optimization_barrier((value, *deps))[0]

    def to_owner(rows):
        tiles = rows.reshape(BLOCKS, SPAN // 2, D)
        return send(tiles[0::2], turn), send(tiles[1::2], deal)

    def owned(even, odd, *when):
        even, odd = after(even, *when), after(odd, *when)
        return jnp.where(core == 0, jnp.concatenate([even, odd]), jnp.concatenate([odd, even]))

    def from_owner(rows, begin=(), end=()):
        rows = after(rows.reshape(BLOCKS, SPAN // 2, D), *begin)
        even = after(send(lax.dynamic_slice_in_dim(rows, 2 * core, 3), turn), *end)
        odd = after(send(lax.dynamic_slice_in_dim(rows, 3 * (1 - core), 2), undeal), *end)
        shape = (3, 2, SPAN // 2, D)
        odd = jnp.pad(odd, ((0, 1), (0, 0), (0, 0)))
        even = jnp.broadcast_to(even[:, None], shape)
        odd = jnp.broadcast_to(odd[:, None], shape)
        second = lax.broadcasted_iota(jnp.int32, shape, 1) == 1
        both = jnp.where(second, odd, even).reshape(6 * SPAN // 2, D)
        return both[: BLOCKS * SPAN // 2]

    class Far:
        def __init__(self, near, bit, deps=()):
            self.swap = moves(lambda dp, t: (dp ^ 2**bit, t))
            self.first = send(after(near, *deps), across)

        def hop(self, *deps):
            first = after(self.first, *deps)
            self.third = send(first, self.swap)
            self.second = send(first, core_swap)

        def end(self, *deps):
            return self.first, self.second, self.third, send(after(self.third, *deps), core_swap)

    def part_of(value, axis, bit):
        size = value.shape[axis] // 4
        part = dp_pos // 2**bit % 2 * 2 + core
        return lax.dynamic_slice_in_dim(value, part * size, size, axis)

    numbers = send(jnp.concatenate([kept_rows, segment_ids[::SPAN]]), turn)
    cond = send(jax.nn.silu(conditioning.astype(f32)).astype(bf16), turn)
    wq_one = jnp.transpose(qkv_first, (1, 0, 2))
    wq_two = jnp.transpose(qkv_second, (1, 0, 2))
    place_ref = dp_pos.reshape(1).astype(jnp.int32)
    zero_ref = jnp.zeros((1,), jnp.int32)
    near_part = jnp.concatenate(
        [
            lax.dynamic_slice_in_dim(wq_one, core * HALF, HALF, 1),
            lax.dynamic_slice_in_dim(proj_first, core * HALF, HALF, 1)[None],
        ]
    )
    kept, segs = numbers[:KEEP], numbers[KEEP:]
    kind = jnp.where(segs[3] == segs[0], 0, jnp.where(segs[4] == segs[1], 1, 2)).reshape(1)
    slot_hot = segs[:, None] == jnp.arange(SLOTS, dtype=jnp.int32)[None, :]
    cond_rows = jnp.dot(slot_hot.astype(bf16), cond, preferred_element_type=f32).astype(bf16)

    def table(mod):
        return jnp.dot(cond_rows, mod, preferred_element_type=f32).reshape(BLOCKS, 6, D)

    arrived = to_owner(tokens)
    cond_rows = after(cond_rows, *arrived)
    tab_one, tab_two = table(mod_first), table(mod_second)

    block_of, inside = kept // SPAN, kept % SPAN
    spot = (
        jnp.where(inside // (SPAN // 2) == core, 0, GROUP // 2)
        + block_of * (SPAN // 2)
        + inside % (SPAN // 2)
    ).reshape(BLOCKS, 2, KEEP // (2 * BLOCKS))
    spot_own = lax.dynamic_slice_in_dim(spot, core, 1, 1).reshape(-1)
    spot_oth = lax.dynamic_slice_in_dim(spot, 1 - core, 1, 1).reshape(-1)
    spot_all = jnp.concatenate([spot_own, spot_oth])

    piece = D // n_dp
    row = jnp.arange(D, dtype=jnp.int32)
    turned = jnp.zeros_like(row)
    for bit in range(bits):
        turned = turned + (((row // piece) // 2 ** (bits - 1 - bit)) % 2) * 2**bit
    source = jnp.bitwise_xor(turned, dp_pos) * piece + row % piece
    order = (source[:, None] == row[None, :]).astype(bf16)
    pieces = min(n_dp, 16)
    deep = D // pieces
    which = dp_pos % pieces
    at = which * deep
    proj_piece = lax.dynamic_slice(
        proj_second, (at % HALF, at // HALF * HALF), (deep, HALF)
    )
    up_piece = lax.dynamic_slice_in_dim(up_second, at, deep).reshape(deep, 4, HALF)
    down_pieces = [
        lax.dynamic_slice_in_dim(down_second, row * D + at, deep).reshape(deep, 2, HALF)
        for row in range(2)
    ]
    pieces_two = jnp.concatenate(
        [
            lax.dynamic_slice_in_dim(wq_two, at, deep, 1),
            proj_piece[None],
            jnp.transpose(up_piece, (1, 0, 2)),
        ]
        + [down_pieces[row][None, :, column] for column in range(2) for row in range(2)]
    )
    piece_two = send(after(pieces_two, *arrived), across)
    w_near = send(after(near_part, *arrived), across)
    own = owned(*arrived, tab_one, tab_two, piece_two, order)
    oth = send(own, core_swap)

    def add(*terms):
        return functools.reduce(lambda p, q: p + q, [t.astype(f32) for t in terms])

    quarter = HALF // 2

    class Total:
        def cores(self, keep, away):
            got = send(away, core_swap)
            self.keep_n, self.keep_r, self.got_n, self.got_r = keep[0], keep[1], got[0], got[1]
            return self

        def cores_far(self, keep, away):
            self.keep_r, self.got_r = keep, send(away, core_swap)
            return self

        def cores_near(self, keep, away):
            self.keep_n, self.got_n = keep, send(away, core_swap)
            return self

        def far(self, *when):
            away = add(self.keep_r, after(self.got_r, *when)).astype(bf16)
            self.got = send(away, across)
            return (away,)

        def chips(self, *when):
            return add(self.keep_n, self.got_n, after(self.got, *when)).astype(bf16)

        def near(self, *when):
            terms = (self.keep_n, self.got_n, after(self.got, *when))
            away = add(*[t[quarter:] for t in terms]).astype(bf16)
            self.got = send(away, next_swap)
            self.terms = tuple(t[:quarter] for t in terms)
            return (away,)

        def sum(self, *when):
            return add(*self.terms, after(self.got, *when))

    class Rest:
        def __init__(self, acc, bit=2):
            self.acc, self.got, self.bit = acc, None, bit

        def next(self, *when):
            if self.bit == bits:
                return ()
            acc = self.acc
            if self.got is not None:
                acc = acc + after(self.got, *when).astype(f32)
            self.acc = acc
            size = self.acc.shape[0] // 2
            away = self.acc[size:].astype(bf16)
            bit = self.bit
            self.got = send(away, moves(lambda dp, t: (dp ^ 2**bit, t)))
            self.acc = self.acc[:size]
            self.bit = bit + 1
            return (away,)

        def sum(self, *when):
            return self.acc + after(self.got, *when).astype(f32)

        def end(self, *when):
            while self.bit < bits:
                self.next(*when)
            return self.acc + after(self.got, *when).astype(f32)

    normed_one, *near_one = project_first(own, oth, tab_one, wq_one)
    ups_one = Far(part_of(up_first, 1, 1), 1, (own,))
    downs_one = Far(part_of(down_first, 0, 2), 2, (own,))
    mixed_one_n = attend(kind, *near_one)
    w_parts = (w_near, send(after(w_near, mixed_one_n), core_swap))
    w_two_far = lax.all_gather(
        after(piece_two, own)[None],
        "dp",
        axis=0,
        tiled=True,
        axis_index_groups=[
            list(range(first, first + pieces)) for first in range(0, n_dp, pieces)
        ],
    )
    far_two_mlp = ([w_two_far] * 4, [w_two_far] * 4)
    w_one_far, *far_one = project_parts(
        place_ref, normed_one, w_parts, deps=(mixed_one_n,)
    )
    mixed_one_r = attend(kind, *far_one)
    ups_one.hop(mixed_one_r)
    downs_one.hop(mixed_one_r)
    attn_one, middle_one, normed_mlp_one, u_one_n, act_one_n, acc = feed_near(
        mixed_one_n, mixed_one_r, proj_first, w_one_far, own, tab_one, up_first, down_first
    )
    ups_one, downs_one = ups_one.end(normed_mlp_one), downs_one.end(normed_mlp_one)
    mlp_one = (up_first, down_first, ups_one, downs_one)
    cot_parts = to_owner(after(cotangent, normed_mlp_one))
    u_one_r, act_one_r, mlp_out_one, out_one = feed_far(
        place_ref, normed_mlp_one, acc, middle_one, tab_one, ups_one, downs_one
    )
    first_own = out_one.reshape(-1, D)
    first_oth = send(first_own, core_swap)

    routed = pick(spot_all[:, None], first_own, first_oth)
    routed_own, routed_oth = routed.reshape(2, BLOCKS, KEEP // (2 * BLOCKS), D)
    normed_two, *near_two = project_first(routed_own, routed_oth, tab_two, wq_two)
    mixed_two_n = attend(kind, *near_two)
    far_two = project_next(normed_two, w_two_far, deps=(mixed_two_n,))
    mixed_two_r = attend(kind, *far_two)
    cot_own = owned(*cot_parts, mixed_two_r)
    cot_oth = send(cot_own, core_swap)
    attn_two, middle_two, normed_mlp_two, u_two_n, act_two_n, acc = feed_near(
        mixed_two_n, mixed_two_r, proj_second, w_two_far, routed_own, tab_two, up_second,
        down_second,
    )
    first_out = from_owner(out_one, (mixed_two_r,), (normed_mlp_two,))
    mlp_two = (up_second, down_second, *far_two_mlp)
    u_two_r, act_two_r, mlp_out_two, out_two = feed_far(
        zero_ref, normed_mlp_two, acc, middle_two, tab_two, *mlp_two[2:], deps=(first_out,)
    )
    second_own = out_two.reshape(-1, D)
    second_oth = send(second_own, core_swap)
    cot_routed = pick(
        spot_own[:, None], cot_own.reshape(-1, D), cot_oth.reshape(-1, D), deps=(second_own,)
    ).reshape(routed_own.shape)

    g_keep, g_send, d_mlp, d_gate_two = down_back(
        zero_ref, cot_routed, tab_two, mlp_out_two, order, act_two_n, act_two_r
    )
    down_two = Total().cores(g_keep, g_send)
    saved = (attn_two, middle_two, normed_mlp_two, u_two_n, u_two_r)
    g_keep, g_send, p_keep, p_send, d_middle, d_mix_n, d_mix_r, d_mod_two = up_back(
        zero_ref, cot_routed, tab_two, d_mlp, saved, mlp_two, proj_second, w_two_far, mixed_two_n,
        mixed_two_r, order,
    )
    up_two = Total().cores(g_keep, g_send)
    sent = down_two.far(d_mix_r)
    grads_r = attend_back(kind, *far_two, d_mix_r, deps=sent)
    sent = up_two.far(grads_r[0])
    qr_keep, qr_send, normed_t, acc = qkv_back(
        True, 1, grads_r, w_two_far, normed_two, order, None, None, p_keep, p_send, deps=sent
    )
    qkv_two = Total().cores_far(qr_keep, qr_send)
    grads_n = attend_back(kind, *near_two, d_mix_n, deps=(acc, down_two.got))
    sent = qkv_two.far(grads_n[0])
    qn_keep, qn_send, d_own, d_oth = qkv_back(
        False, 0, grads_n, wq_two, normed_two, None, normed_t, acc, p_keep, p_send, deps=sent
    )
    d_got = send(d_oth, core_swap)
    qkv_two.cores_near(qn_keep, qn_send)
    d_two, d_mod_two_a = finish(
        d_own, d_got, routed_own, tab_two, d_middle
    )
    d_two_own = d_two.reshape(-1, D)
    d_two_oth = send(d_two_own, core_swap)

    def slot_sums(*parts):
        per_block = jnp.concatenate(parts, axis=1).reshape(BLOCKS, -1)
        return lax.dot_general(
            slot_hot.astype(f32),
            per_block,
            (((0,), (0,)), ((), ())),
            precision=lax.Precision.HIGHEST,
        ).astype(bf16)

    routed_rows = put(
        spot_own[None], spot_oth[None], second_own, second_oth, first_own, deps=(d_two_own,)
    )
    d_first = put(
        spot_own[None], spot_oth[None], d_two_own, d_two_oth, cot_own.reshape(-1, D),
        deps=(routed_rows,),
    ).reshape(own.shape)
    g_keep, g_send, d_mlp, d_gate = down_back(
        place_ref, d_first, tab_one, mlp_out_one, order, act_one_n, act_one_r, deps=(up_two.got,)
    )
    down_one = Total().cores(g_keep, g_send)
    mlp_rest_two = Rest(jnp.concatenate([t.chips(d_mlp) for t in (down_two, up_two)], axis=1), 1)
    sent = mlp_rest_two.next()
    saved = (attn_one, middle_one, normed_mlp_one, u_one_n, u_one_r)
    g_keep, g_send, p_keep, p_send, d_middle, d_mix_n, d_mix_r, d_mod = up_back(
        place_ref, d_first, tab_one, d_mlp, saved, mlp_one, proj_first, w_one_far, mixed_one_n,
        mixed_one_r, order, deps=sent,
    )
    up_one = Total().cores(g_keep, g_send)
    qkv_rest_two = Rest(qkv_two.chips(d_mix_r), 1)
    sent = (*down_one.far(d_mix_r), *qkv_rest_two.next())
    early = lax.all_gather(
        jnp.concatenate(
            [cond, slot_sums(d_mod_two_a, d_mod_two, d_gate_two), slot_sums(d_mod, d_gate)], axis=1
        ),
        ALL,
        axis=0,
        tiled=True,
    )
    grads_r = attend_back(kind, *far_one, d_mix_r, deps=sent)
    rest_two = Rest(
        jnp.concatenate([t.sum(grads_r[0]) for t in (mlp_rest_two, qkv_rest_two)], axis=1)
    )
    sent = (*up_one.far(grads_r[0]), *rest_two.next())
    qr_keep, qr_send, normed_t, acc = qkv_back(
        True, 1, grads_r, w_one_far, normed_one, order, None, None, p_keep, p_send,
        deps=sent,
    )
    qkv_one = Total().cores_far(qr_keep, qr_send)
    sent = down_one.near(acc)
    grads_n = attend_back(kind, *near_one, d_mix_n, deps=sent)
    done = grads_n[0]
    sent = (*qkv_one.far(done), *up_one.near(done), *rest_two.next(done))
    qn_keep, qn_send, d_own, d_oth = qkv_back(
        False, 0, grads_n, wq_one, normed_one, None, normed_t, acc, p_keep, p_send, deps=sent
    )
    d_got = send(d_oth, core_swap)
    qkv_one.cores_near(qn_keep, qn_send)
    routed_out = from_owner(routed_rows, (grads_r[0],), (d_own,))
    mlp_rest = Rest(jnp.concatenate([down_one.sum(d_own), up_one.sum(d_own)], axis=1))
    sent = (*mlp_rest.next(), routed_out)
    d_one, d_mod_a = finish(d_own, d_got, own, tab_one, d_middle, deps=(*sent, qkv_one.got_n))

    last = qkv_one.near(d_one)
    late = after(jnp.pad(slot_sums(d_mod_a), ((0, 8 - SLOTS), (0, 0))), *last)
    late = (late.astype(f32) + send(late, core_swap).astype(f32)).astype(bf16)[None]
    sources = jnp.array([dp_pos * 2 + side])

    def doubled(late, sources, mask):
        pairs = moves(lambda dp, t: ((dp * 2 + t ^ mask) // 2, (t ^ mask) % 2))
        late = jnp.concatenate([late, send(late, pairs)])
        return late, jnp.concatenate([sources, jnp.bitwise_xor(sources, mask)])

    late, sources = doubled(late, sources, 1)
    qkv_rest = Rest(qkv_one.sum(late))
    last = qkv_rest.next()
    mlp_rest.next(*last)
    for bit in range(2, bits):
        late, sources = doubled(after(late, *last), sources, 2**bit)
        last = qkv_rest.next(late) or last
    late, sources = doubled(after(late, *last), sources, 2**bits)
    input_grad = from_owner(d_one, (), last).astype(f32)
    early = after(early, *last)
    mlp_total = mlp_rest.end(*last)
    total_two = rest_two.end(*last)
    qkv_total = qkv_rest.end(late)

    mod_rows = D // (n_dp * 2)
    mine = lax.dynamic_slice_in_dim(early[:, :D], (dp_pos * 2 + side) * mod_rows, mod_rows, 1)
    mine_late = jnp.pad(
        mine.reshape(-1, SLOTS, mod_rows)[sources], ((0, 0), (0, 8 - SLOTS), (0, 0))
    ).reshape(-1, mod_rows)
    mod_two_end = 7 * D
    mod_one = jnp.concatenate(
        [
            dot_rows(mine_late, late.reshape(-1, 2 * D)),
            dot_rows(mine, early[:, mod_two_end:]),
        ],
        axis=1,
    )
    mod_two = dot_rows(mine, early[:, D:mod_two_end])
    wide = 2 * TILE

    def placed(attention, down, up):
        qkv = attention[:, : 3 * HALF].reshape(piece, 3, HALF)
        return qkv, attention[:, 3 * HALF :].T, up, down.T

    return (
        first_out,
        routed_out,
        input_grad,
        mod_one,
        *placed(qkv_total, mlp_total[:, :wide], mlp_total[:, wide:]),
        mod_two,
        *placed(
            total_two[:, 2 * wide :].astype(f32),
            total_two[:, :wide].astype(f32),
            total_two[:, wide : 2 * wide].astype(f32),
        ),
    )


def solution(mesh):
    n_dp = mesh.shape["dp"]
    return jax.shard_map(
        functools.partial(on_device, n_dp),
        mesh=mesh,
        in_specs=(
            P(("dp", "tensor"), None),
            P("dp", None),
            P("dp"),
            P("dp"),
            P(("dp", "tensor"), None),
            P(),
            P(None, None, "tensor"),
            P("tensor", None),
            P(None, "tensor"),
            P("tensor", None),
            P(),
            P(None, None, "tensor"),
            P("tensor", None),
            P(None, "tensor"),
            P("tensor", None),
        ),
        out_specs=(
            P(("dp", "tensor"), None),
            P(("dp", "tensor"), None),
            P(("dp", "tensor"), None),
            P(("dp", "tensor"), None),
            P("dp", None, "tensor"),
            P("tensor", "dp"),
            P("dp", "tensor"),
            P("tensor", "dp"),
            P(("dp", "tensor"), None),
            P("dp", None, "tensor"),
            P("tensor", "dp"),
            P("dp", "tensor"),
            P("tensor", "dp"),
        ),
        check_vma=False,
    )
```

```python
import functools

import jax
import jax.numpy as jnp
from jax import lax
from jax.experimental import pallas as pl
from jax.experimental.pallas import tpu as pltpu
from jax.sharding import PartitionSpec as P

D = 768
HEAD_DIM = 64
SLOTS = 5
GROUP = 1280
KEEP = 640
BLOCKS = 5
SPAN = GROUP // BLOCKS
HALF = D // 2
TILE = 768
NORM_EPS = 1e-06
f32 = jnp.float32
bf16 = jnp.bfloat16
ALL = ("dp", "tensor")
VMEM_BYTES = 24 * 1024 * 1024
CHUNK = 1024
LIGHT = 2000


def dot(left, right):
    return jnp.dot(left, right, preferred_element_type=f32)


def dot_cols(left, right):
    return lax.dot_general(left, right, (((1,), (1,)), ((), ())), preferred_element_type=f32)


def dot_rows(left, right):
    return lax.dot_general(left, right, (((0,), (0,)), ((), ())), preferred_element_type=f32)


def unit_rows(rows):
    centre = rows - jnp.mean(rows, axis=-1, keepdims=True)
    inverse = lax.rsqrt(jnp.mean(centre * centre, axis=-1, keepdims=True) + NORM_EPS)
    return centre * inverse, inverse


def norm_back(d_normed, unit, inverse, scale_row):
    e = d_normed * (1.0 + scale_row)
    return inverse * (
        e
        - jnp.mean(e, axis=-1, keepdims=True)
        - unit * jnp.mean(e * unit, axis=-1, keepdims=True)
    )


def col_sum(rows):
    return jnp.sum(rows, axis=0, keepdims=True)


def flat(ref):
    value = ref[...]
    return value.reshape(-1, value.shape[-1])


def whole(shape):
    return pl.BlockSpec(shape, lambda *_: (0,) * len(shape), pipeline_mode=pl.Buffered(1))


def run(body, grid, ins, outs, scratch=(), scalars=(), flops=0, deps=()):
    in_specs = [whole(a.shape) if s is None else s for a, s in ins]
    in_specs += [pl.BlockSpec(memory_space=pl.ANY)] * len(deps)
    first, past = len(scalars) + len(ins), len(scalars) + len(ins) + len(deps)

    def step(*refs):
        body(*refs[:first], *refs[past:])

    out_specs = [whole(sh) if s is None else s for sh, _, s in outs]
    moved = sum(a.size * a.dtype.itemsize for a, _ in ins)
    moved += sum(jnp.dtype(d).itemsize * functools.reduce(lambda p, q: p * q, sh, 1) for sh, d, _ in outs)
    return pl.pallas_call(
        step,
        grid_spec=pltpu.PrefetchScalarGridSpec(
            num_scalar_prefetch=len(scalars),
            grid=grid,
            in_specs=in_specs,
            out_specs=out_specs,
            scratch_shapes=list(scratch),
        ),
        out_shape=[jax.ShapeDtypeStruct(sh, d) for sh, d, _ in outs],
        compiler_params=pltpu.CompilerParams(
            vmem_limit_bytes=VMEM_BYTES, dimension_semantics=("arbitrary",) * len(grid)
        ),
        cost_estimate=pl.CostEstimate(
            flops=1 + int(flops) // LIGHT, bytes_accessed=1 + int(moved) // LIGHT, transcendentals=0
        ),
    )(*scalars, *[a for a, _ in ins], *deps)


def qkv_body(own, oth, tab, w, normed, q, k, v):
    rows = own.shape[1]
    step = pl.program_id(0)

    @pl.when(step == 0)
    def _():
        for side, src in ((0, own), (1, oth)):
            for i in range(BLOCKS):
                unit, _ = unit_rows(src[i].astype(f32))
                normed[side, i] = (unit * (1.0 + tab[i, 1:2]) + tab[i, 0:1]).astype(bf16)

    qkv_steps(step, normed, w, q, k, v)


def qkv_next_body(normed, w, q, k, v):
    qkv_steps(pl.program_id(0), normed, w, q, k, v)


def qkv_parts_body(place, normed, w_0, w_1, w, q, k, v):
    for index, part in enumerate((w_0, w_1)):
        at = pl.multiple_of((place[0] % 2 ^ index) * HALF, HALF)
        w[0, pl.ds(at, HALF)] = part[0]
    qkv_steps(pl.program_id(0), normed, w, q, k, v)


def block(w):
    return w[...].reshape(D, HALF)


def qkv_steps(step, normed, w, q, k, v):
    @pl.when(step == 0)
    def _():
        mine = normed[0].reshape(-1, D)
        q[...] = dot(mine, block(w)).astype(bf16).reshape(q.shape)

    for index, out in ((1, k), (2, v)):

        @pl.when(step == index)
        def _(out=out):
            out[...] = dot(flat(normed), block(w)).astype(bf16).reshape(out.shape)


def qkv_outs(rows):
    return [
        ((BLOCKS, rows, HALF), bf16, None),
        ((2, BLOCKS, rows, HALF), bf16, None),
        ((2, BLOCKS, rows, HALF), bf16, None),
    ]


BY_STEP = pl.BlockSpec((1, D, HALF), lambda j, *_: (j, 0, 0))


def block_at(w, index):
    if w.ndim == 3:
        return (w, pl.BlockSpec((1, D, HALF), lambda j, *_: (index(j), 0, 0)))
    pieces, _, rows, _ = w.shape
    return (w, pl.BlockSpec((pieces, 1, rows, HALF), lambda j, *_: (0, index(j), 0, 0)))


def project_first(own, oth, tab, w, deps=()):
    rows = own.shape[1]
    return run(
        qkv_body,
        (3,),
        [(own, None), (oth, None), (tab, None), (w, BY_STEP)],
        [((2, BLOCKS, rows, D), bf16, None)] + qkv_outs(rows),
        flops=2 * 25 * rows * D * HALF,
        deps=deps,
    )


def project_next(normed, w, deps=()):
    rows = normed.shape[2]
    ins = [(normed, None), block_at(w, lambda j: j)]
    return run(qkv_next_body, (3,), ins, qkv_outs(rows), flops=2 * 25 * rows * D * HALF, deps=deps)


def project_parts(place, normed, parts, deps=()):
    rows = normed.shape[2]
    by_step = pl.BlockSpec((1, HALF, HALF), lambda j, *_: (j, 0, 0))
    return run(
        qkv_parts_body,
        (4,),
        [(normed, None)] + [(part, by_step) for part in parts],
        [((4, D, HALF), bf16, BY_STEP)] + qkv_outs(rows),
        scalars=(place,),
        flops=2 * 25 * rows * D * HALF,
        deps=deps,
    )


def by_sequence(kind, one_sequence, long_tiles):
    @pl.when(kind < 2)
    def _():
        one_sequence(kind, 4, long_tiles)
        one_sequence(jnp.where(kind == 0, 4, 0), 1, 1)

    @pl.when(kind == 2)
    def _():
        def short(i, carry):
            one_sequence(i, 1, 1)
            return carry

        lax.fori_loop(0, BLOCKS, short, 0)


def two_heads(rows, low):
    zero = jnp.zeros_like(rows)
    return jnp.concatenate([jnp.where(low, rows, zero), jnp.where(low, zero, rows)], axis=0)


def attend_body(kind, q, k, v, out, log_total):
    rows = q.shape[1]
    low = lax.broadcasted_iota(jnp.int32, (1, 128), 1) < HEAD_DIM
    scaling = HEAD_DIM ** (-0.5)

    def one_sequence(start, count, tiles):
        keys = k[:, pl.ds(start, count)].reshape(2 * count * rows, 128)
        values = v[:, pl.ds(start, count)].reshape(2 * count * rows, 128)
        size = tiles * rows
        for part in range(count // tiles):
            at = pl.ds(start + part * tiles, tiles)
            pair = two_heads((q[at].reshape(size, 128) * scaling).astype(bf16), low)
            scores = dot_cols(pair, keys)
            highest = jnp.max(scores, axis=-1, keepdims=True)
            shifted = jnp.exp(scores - highest)
            total = jnp.sum(shifted, axis=-1, keepdims=True)
            log_rows = highest + jnp.log(total)
            log_both = jnp.where(low, log_rows[:size], log_rows[size:])
            log_total[at] = log_both.reshape(tiles, rows, 128)
            mixed = dot(shifted.astype(bf16), values) * (1.0 / total)
            out[at] = jnp.where(low, mixed[:size], mixed[size:]).astype(bf16).reshape(tiles, rows, 128)

    by_sequence(kind[0], one_sequence, 128 // rows)


def attend(kind, q, k, v, deps=()):
    rows = q.shape[1]
    own = pl.BlockSpec((BLOCKS, rows, 128), lambda p, *_: (0, 0, p))
    every = pl.BlockSpec((2, BLOCKS, rows, 128), lambda p, *_: (0, 0, 0, p))
    return run(
        attend_body,
        (HALF // 128,),
        [(q, own), (k, every), (v, every)],
        [(q.shape, bf16, own), (q.shape, f32, own)],
        scalars=(kind,),
        flops=16 * BLOCKS * rows * 8 * rows * HALF,
        deps=deps,
    )


def attend_back_body(kind, q, k, v, d_out, mixed, log_total, dq, dk, dv, acc_k, acc_v):
    rows = q.shape[1]
    low = lax.broadcasted_iota(jnp.int32, (1, 128), 1) < HEAD_DIM
    scaling = HEAD_DIM ** (-0.5)
    head = lax.broadcasted_iota(jnp.int32, (8, 128), 0)
    lane = lax.broadcasted_iota(jnp.int32, (8, 128), 1)
    first_lane = (lane == head * HEAD_DIM).astype(f32)
    own_lanes = (lane // HEAD_DIM == head).astype(f32)

    def as_row(pick_lanes, value):
        both = lax.dot_general(
            pick_lanes, value, (((1,), (1,)), ((), ())), precision=lax.Precision.HIGHEST
        )
        return jnp.concatenate([both[0:1], both[1:2]], axis=1)

    def one_sequence(start, count, tiles):
        key_rows = 2 * count * rows
        keys = k[:, pl.ds(start, count)].reshape(key_rows, 128)
        values = v[:, pl.ds(start, count)].reshape(key_rows, 128)
        size = tiles * rows
        chunk = min(key_rows, CHUNK)
        for part in range(count // tiles):
            at = pl.ds(start + part * tiles, tiles)
            pair = two_heads((q[at].reshape(size, 128) * scaling).astype(bf16), low)
            d_rows = d_out[at].reshape(size, 128)
            d_pair = two_heads(d_rows, low)
            log_row = as_row(first_lane, log_total[at].reshape(size, 128))
            product = d_rows.astype(f32) * mixed[at].reshape(size, 128).astype(f32)
            row_sum = as_row(own_lanes, product)
            both = None
            for begin in range(0, key_rows, chunk):
                here = slice(begin, begin + chunk)
                probs = jnp.exp(dot_cols(keys[here], pair) - log_row)
                d_probs = dot_cols(values[here], d_pair)
                d_scores = (probs * (d_probs - row_sum)).astype(bf16)
                add_v = dot(probs.astype(bf16), d_pair)
                add_k = dot(d_scores, pair)
                if part == 0:
                    acc_v[here] = add_v
                    acc_k[here] = add_k
                else:
                    acc_v[here] += add_v
                    acc_k[here] += add_k
                term = dot_rows(d_scores, keys[here])
                both = term if both is None else both + term
            both = both * scaling
            dq[at] = jnp.where(low, both[:size], both[size:]).astype(bf16).reshape(tiles, rows, 128)
        dk[:, pl.ds(start, count)] = acc_k[:key_rows].astype(bf16).reshape(2, count, rows, 128)
        dv[:, pl.ds(start, count)] = acc_v[:key_rows].astype(bf16).reshape(2, count, rows, 128)

    by_sequence(kind[0], one_sequence, 128 // rows)


def attend_back(kind, q, k, v, d_out, mixed, log_total, deps=()):
    rows = q.shape[1]
    own = pl.BlockSpec((BLOCKS, rows, 128), lambda p, *_: (0, 0, p))
    every = pl.BlockSpec((2, BLOCKS, rows, 128), lambda p, *_: (0, 0, 0, p))
    return run(
        attend_back_body,
        (HALF // 128,),
        [
            (q, own),
            (k, every),
            (v, every),
            (d_out, own),
            (mixed, own),
            (log_total, own),
        ],
        [(q.shape, bf16, own), (k.shape, bf16, every), (v.shape, bf16, every)],
        scratch=[pltpu.VMEM((8 * rows, 128), f32), pltpu.VMEM((8 * rows, 128), f32)],
        scalars=(kind,),
        flops=40 * BLOCKS * rows * 8 * rows * HALF,
        deps=deps,
    )


def gelu_parts(u):
    rate = 0.7978845608028654
    inner = rate * (u + 0.044715 * (u * u * u))
    return jnp.tanh(inner), rate


def hidden(normed, ups, downs, u, act):
    start = 0
    total = None
    ups = [far_up(up) for up in ups]
    for up, down in zip(ups, downs):
        at = slice(start, start + up.shape[1])
        start = start + up.shape[1]
        pre = dot(flat(normed), up)
        u[0, :, at] = pre.astype(bf16)
        tanh, _ = gelu_parts(pre)
        value = (0.5 * pre * (1.0 + tanh)).astype(bf16)
        act[0, :, at] = value
        term = dot(value, down[...])
        total = term if total is None else total + term
    return total


def mlp_near_body(
    mixed_n, mixed_r, proj_n, proj_r, own, tab, up, down,
    attn_out, middle, normed, u, act, acc,
):
    rows = own.shape[1]
    step = pl.program_id(0)

    @pl.when(step == 0)
    def _():
        for at in (slice(0, HALF), slice(HALF, D)):
            acc[:, at] = dot(flat(mixed_n), proj_n[:, at]) + dot(flat(mixed_r), block(proj_r)[at])
        for i in range(BLOCKS):
            attn = acc[i * rows : (i + 1) * rows]
            attn_out[i] = attn.astype(bf16)
            mid = own[i].astype(f32) + tab[i, 2:3] * attn
            middle[i] = mid
            unit, _ = unit_rows(mid)
            normed[i] = (unit * (1.0 + tab[i, 4:5]) + tab[i, 3:4]).astype(bf16)
        acc[...] = hidden(normed, [up], [down], u, act)

    @pl.when(step == 1)
    def _():
        acc[...] += hidden(normed, [up], [down], u, act)


def matching(place, down_0, down_1, down_2, down_3):
    refs = (down_0, down_1, down_2, down_3)
    if len(down_0.shape) > 2:
        return (lambda: far_downs(refs)[:2]), (lambda: far_downs(refs)[2:])
    same = (place[0] // 2 + place[0] // 4) % 2 == 0

    def first():
        return [
            jnp.where(same, down_0[...], down_2[...]),
            jnp.where(same, down_1[...], down_3[...]),
        ]

    def second():
        return [
            jnp.where(same, down_2[...], down_0[...]),
            jnp.where(same, down_3[...], down_1[...]),
        ]

    return first, second


def mlp_far_body(
    place, normed, start, middle, tab, up_0, up_1, up_2, up_3, down_0, down_1, down_2, down_3,
    u, act, mlp_out, out, acc,
):
    rows = middle.shape[1]
    step = pl.program_id(0)
    first, second = matching(place, down_0, down_1, down_2, down_3)

    @pl.when(step == 0)
    def _():
        acc[...] = start[...] + hidden(normed, [up_0, up_1], first(), u, act)

    @pl.when(step == 1)
    def _():
        acc[...] += hidden(normed, [up_2, up_3], second(), u, act)
        for i in range(BLOCKS):
            term = acc[i * rows : (i + 1) * rows]
            mlp_out[i] = term.astype(bf16)
            out[i] = (middle[i] + tab[i, 5:6] * term).astype(bf16)


def projection(w):
    return block_at(w, lambda j: 3)


def far_up(ref):
    return ref[...] if len(ref.shape) == 2 else block(ref)


def far_downs(downs):
    if len(downs[0].shape) == 2:
        return [down[...] for down in downs]
    wide = [
        jnp.concatenate([block(downs[index]), block(downs[index + 2])], axis=1) for index in range(2)
    ]
    return [wide[0][:HALF], wide[0][HALF:], wide[1][:HALF], wide[1][HALF:]]


def far_ins(ups, downs):
    if ups[0].ndim == 2:
        return [(part, None) for part in (*ups, *downs)]
    ins = []
    for index, part in enumerate((*ups, *downs)):
        pieces, _, rows, _ = part.shape
        at = pl.BlockSpec(
            (pieces, 1, rows, HALF),
            lambda *_, index=index: (0, 4 + index, 0, 0),
            pipeline_mode=pl.Buffered(1),
        )
        ins.append((part, at))
    return ins


def feed_near(mixed_n, mixed_r, proj_n, w_r, own, tab, up, down, deps=()):
    rows = own.shape[1]
    total = BLOCKS * rows
    tiles = ((2, total, TILE), bf16, pl.BlockSpec((1, total, TILE), lambda j: (j, 0, 0)))
    return run(
        mlp_near_body,
        (2,),
        [
            (mixed_n, None),
            (mixed_r, None),
            (proj_n, None),
            projection(w_r),
            (own, None),
            (tab, None),
            (up, pl.BlockSpec((D, TILE), lambda j: (0, j))),
            (down, pl.BlockSpec((TILE, D), lambda j: (j, 0))),
        ],
        [
            (own.shape, bf16, None),
            (own.shape, f32, None),
            (own.shape, bf16, None),
            tiles,
            tiles,
            ((total, D), f32, None),
        ],
        flops=2 * total * D * (D + 4 * D),
        deps=deps,
    )


def feed_far(place, normed, start, middle, tab, ups, downs, deps=()):
    total = BLOCKS * normed.shape[1]
    tiles = ((2, total, TILE), bf16, pl.BlockSpec((1, total, TILE), lambda j, *_: (j, 0, 0)))
    return run(
        mlp_far_body,
        (2,),
        [(normed, None), (start, None), (middle, None), (tab, None)]
        + far_ins(ups, downs),
        [tiles, tiles, (normed.shape, bf16, None), (normed.shape, bf16, None)],
        scratch=[pltpu.VMEM((total, D), f32)],
        scalars=(place,),
        flops=2 * total * D * (4 * D),
        deps=deps,
    )


def tile_of(j, place_ref):
    far = jnp.where(place_ref[0] // 2 % 2 == 0, j % 2, 1 - j % 2)
    return (j // 2, 0, jnp.where(j < 2, j % 2, far))


MLP_GRAD = ((2, HALF, 2 * TILE), bf16, pl.BlockSpec((1, HALF, TILE), tile_of))


def both_halves(near, far):
    size = near.shape[1]
    return [
        (near, pl.BlockSpec((1, size, TILE), lambda j, *_: (jnp.minimum(j, 1), 0, 0))),
        (far, pl.BlockSpec((1, size, TILE), lambda j, *_: (jnp.maximum(j - 2, 0), 0, 0))),
    ]


def store_grad(keep, away, at, size, value):
    there = pl.ds(at, size)
    keep[0, :, there] = value[:HALF]
    away[0, :, there] = value[HALF:]


def down_back_body(
    place, d_out, tab, mlp_out, order, act_n, act_r, g_keep, g_send, d_mlp, d_gate, d_mlp_t
):
    rows = d_out.shape[1]
    step = pl.program_id(0)
    core = place[0] % 2

    @pl.when(step == 0)
    def _():
        for i in range(BLOCKS):
            grad = d_out[i].astype(f32)
            d_mlp[i * rows : (i + 1) * rows] = (grad * tab[i, 5:6]).astype(bf16)
            d_gate[i] = col_sum(grad * mlp_out[i].astype(f32))
        d_mlp_t[...] = dot_cols(order[...], d_mlp[...]).astype(bf16)

    @pl.when(step < 2)
    def _():
        store_grad(g_keep, g_send, 0, TILE, dot(d_mlp_t[...], act_n[0]).astype(bf16))

    @pl.when(step >= 2)
    def _():
        for index in range(2):
            value = act_r[0, :, index * HALF : (index + 1) * HALF]
            at = pl.multiple_of((core if index == 0 else 1 - core) * HALF, 128)
            store_grad(g_keep, g_send, at, HALF, dot(d_mlp_t[...], value).astype(bf16))


def down_back(place, d_out, tab, mlp_out, order, act_n, act_r, deps=()):
    total = BLOCKS * d_out.shape[1]
    return run(
        down_back_body,
        (4,),
        [(d_out, None), (tab, None), (mlp_out, None), (order, None)] + both_halves(act_n, act_r),
        [MLP_GRAD, MLP_GRAD, ((total, D), bf16, None), ((BLOCKS, 1, D), f32, None)],
        scratch=[pltpu.VMEM((D, total), bf16)],
        scalars=(place,),
        flops=2 * total * D * 5 * D,
        deps=deps,
    )


def up_back_body(
    place, d_out, tab, d_mlp, normed, u_n, u_r,
    up_n, down_n, up_0, up_1, up_2, up_3, down_0, down_1, down_2, down_3,
    middle, attn_out, proj_n, proj_r, mixed_n, mixed_r, order,
    g_keep, g_send, p_keep, p_send, d_middle, d_mix_n, d_mix_r, d_mod,
    d_attn, turned, acc,
):
    rows = d_out.shape[1]
    step = pl.program_id(0)
    core = place[0] % 2

    @pl.when(step == 0)
    def _():
        turned[...] = dot_cols(order[...], flat(normed)).astype(bf16)

    def back(u, ups, downs, places):
        start = 0
        total = None
        ups = [far_up(up) for up in ups]
        for up, down, at in zip(ups, downs, places):
            size = up.shape[1]
            pre = u[0, :, start : start + size].astype(f32)
            start = start + size
            tanh, rate = gelu_parts(pre)
            slope = 0.5 * (1.0 + tanh) + (0.5 * rate) * pre * (1.0 - tanh * tanh) * (
                1.0 + (3.0 * 0.044715) * (pre * pre)
            )
            d_up = (slope * dot_cols(d_mlp[...], down[...])).astype(bf16)
            store_grad(g_keep, g_send, at, size, dot(turned[...], d_up).astype(bf16))
            term = dot_cols(d_up, up)
            total = term if total is None else total + term
        return total

    both = [pl.multiple_of(core * HALF, 128), pl.multiple_of((1 - core) * HALF, 128)]
    first, second = matching(place, down_0, down_1, down_2, down_3)

    @pl.when(step == 0)
    def _():
        acc[...] = back(u_n, [up_n], [down_n], [0])

    @pl.when(step == 1)
    def _():
        acc[...] += back(u_n, [up_n], [down_n], [0])

    @pl.when(step == 2)
    def _():
        acc[...] += back(u_r, [up_0, up_1], first(), both)

    @pl.when(step == 3)
    def _():
        acc[...] += back(u_r, [up_2, up_3], second(), both)
        for i in range(BLOCKS):
            at = slice(i * rows, (i + 1) * rows)
            d_normed = acc[at]
            unit, inverse = unit_rows(middle[i])
            grad = d_out[i].astype(f32) + norm_back(d_normed, unit, inverse, tab[i, 4:5])
            d_middle[i] = grad
            d_mod[i, 0:1] = col_sum(grad * attn_out[i].astype(f32))
            d_mod[i, 1:2] = col_sum(d_normed)
            d_mod[i, 2:3] = col_sum(d_normed * unit)
            d_attn[at] = (grad * tab[i, 2:3]).astype(bf16)
        turned[...] = dot_cols(order[...], d_attn[...]).astype(bf16)
        d_rows_n = dot_cols(d_attn[...], proj_n[...])
        far = block(proj_r)
        d_rows_r = dot_cols(d_attn[:, :HALF], far[:HALF]) + dot_cols(d_attn[:, HALF:], far[HALF:])
        for side, mixed, d_rows, d_mix in (
            (0, mixed_n, d_rows_n, d_mix_n),
            (1, mixed_r, d_rows_r, d_mix_r),
        ):
            d_mix[...] = d_rows.astype(bf16).reshape(d_mix.shape)
            g_proj = dot(turned[...], flat(mixed)).astype(bf16)
            p_keep[side] = g_proj[:HALF]
            p_send[side] = g_proj[HALF:]


def up_back(place, d_out, tab, d_mlp, saved, weights, proj_n, w_r, mixed_n, mixed_r, order, deps=()):
    attn_out, middle, normed, u_n, u_r = saved
    up, down, ups, downs = weights
    rows = d_out.shape[1]
    total = BLOCKS * rows
    here = lambda j: jnp.minimum(j, 1)
    return run(
        up_back_body,
        (4,),
        [(d_out, None), (tab, None), (d_mlp, None), (normed, None)]
        + both_halves(u_n, u_r)
        + [
            (up, pl.BlockSpec((D, TILE), lambda j, *_: (0, here(j)))),
            (down, pl.BlockSpec((TILE, D), lambda j, *_: (here(j), 0))),
        ]
        + far_ins(ups, downs)
        + [
            (middle, None),
            (attn_out, None),
            (proj_n, None),
            projection(w_r),
            (mixed_n, None),
            (mixed_r, None),
            (order, None),
        ],
        [
            MLP_GRAD,
            MLP_GRAD,
            ((2, HALF, HALF), bf16, None),
            ((2, HALF, HALF), bf16, None),
            (d_out.shape, f32, None),
            (mixed_n.shape, bf16, None),
            (mixed_n.shape, bf16, None),
            ((BLOCKS, 3, D), f32, None),
        ],
        scratch=[
            pltpu.VMEM((total, D), bf16),
            pltpu.VMEM((D, total), bf16),
            pltpu.VMEM((total, D), f32),
        ],
        scalars=(place,),
        flops=2 * total * D * (12 * D + 4 * D),
        deps=deps,
    )


def qkv_back_steps(step, grads, w, turned, p_keep, p_send, g_keep, g_send, acc, start):
    total = grads[0].shape[0] * grads[0].shape[1]

    for index, grad in enumerate(grads):

        @pl.when(step == index)
        def _(index=index, grad=grad):
            value = flat(grad)
            term = dot_cols(value, block(w))
            if index == 0:
                g_w = dot(turned[:, :total], value).astype(bf16)
                start(term)
            else:
                g_w = dot(turned[...], value).astype(bf16)
                acc[...] += term
            g_keep[...] = g_w[:HALF]
            g_send[...] = g_w[HALF:]

    @pl.when(step == 3)
    def _():
        g_keep[...] = p_keep[0]
        g_send[...] = p_send[0]


def qkv_back_body(
    dq, dk, dv, w, normed, order, p_keep, p_send, g_keep, g_send, turned, acc
):
    total = dq.shape[0] * dq.shape[1]
    step = pl.program_id(0)

    @pl.when(step == 0)
    def _():
        turned[...] = dot_cols(order[...], flat(normed)).astype(bf16)

    def start(term):
        acc[:total] = term
        acc[total:] = jnp.zeros((total, D), f32)

    qkv_back_steps(step, (dq, dk, dv), w, turned, p_keep, p_send, g_keep, g_send, acc, start)


def qkv_back_next_body(
    dq, dk, dv, w, turned, before, p_keep, p_send, g_keep, g_send, d_own, d_oth, acc
):
    total = dq.shape[0] * dq.shape[1]
    step = pl.program_id(0)

    def start(term):
        acc[...] = before[...]
        acc[:total] += term

    qkv_back_steps(step, (dq, dk, dv), w, turned, p_keep, p_send, g_keep, g_send, acc, start)

    @pl.when(step == 3)
    def _():
        d_own[...] = acc[:total]
        d_oth[...] = acc[total:].astype(bf16)


def qkv_back(first, side, grads, w, normed, order, turned, before, p_keep, p_send, deps=()):
    rows = normed.shape[2]
    total = BLOCKS * rows
    grad = ((HALF, 4 * HALF), bf16, pl.BlockSpec((HALF, HALF), lambda j: (0, j)))
    piece = pl.BlockSpec((1, HALF, HALF), lambda j: (side, 0, 0))
    ins = [(g, None) for g in grads]
    ins += [block_at(w, lambda j: jnp.minimum(j, 2))]
    ends = [(p_keep, piece), (p_send, piece)]
    flops = 2 * total * D * 10 * HALF
    if first:
        return run(
            qkv_back_body,
            (4,),
            ins + [(normed, None), (order, None)] + ends,
            [grad, grad, ((D, 2 * total), bf16, None), ((2 * total, D), f32, None)],
            flops=flops + 4 * total * D * D,
            deps=deps,
        )
    return run(
        qkv_back_next_body,
        (4,),
        ins + [(turned, None), (before, None)] + ends,
        [grad, grad, ((total, D), f32, None), ((total, D), bf16, None)],
        scratch=[pltpu.VMEM((2 * total, D), f32)],
        flops=flops,
        deps=deps,
    )


def finish_body(d_own, d_got, own, tab, d_middle, d_rows, d_mod):
    rows = own.shape[1]
    for i in range(BLOCKS):
        at = slice(i * rows, (i + 1) * rows)
        d_normed = d_own[at] + d_got[at].astype(f32)
        unit, inverse = unit_rows(own[i].astype(f32))
        grad = d_middle[i] + norm_back(d_normed, unit, inverse, tab[i, 1:2])
        d_rows[i] = grad.astype(bf16)
        d_mod[i, 0:1] = col_sum(d_normed)
        d_mod[i, 1:2] = col_sum(d_normed * unit)


def finish(d_own, d_got, own, tab, d_middle, deps=()):
    return run(
        finish_body,
        (1,),
        [(d_own, None), (d_got, None), (own, None), (tab, None), (d_middle, None)],
        [(own.shape, bf16, None), ((BLOCKS, 2, D), f32, None)],
        deps=deps,
    )


def pick_body(index, own, oth, out):
    spot = lax.broadcasted_iota(jnp.int32, (1, own.shape[0]), 1)
    here = (index[...] == spot).astype(bf16)
    there = (index[...] - own.shape[0] == spot).astype(bf16)
    out[...] = (dot(here, own[...]) + dot(there, oth[...])).astype(bf16)


def pick(index, own, oth, deps=()):
    count = index.shape[0]
    return run(
        pick_body,
        (1,),
        [(index, None), (own, None), (oth, None)],
        [((count, D), bf16, None)],
        flops=2 * count * GROUP * D,
        deps=deps,
    )[0]


def put_body(index_own, index_oth, own, oth, base, out):
    spot = lax.broadcasted_iota(jnp.int32, (base.shape[0], 1), 0)
    here = (index_own[...] == spot).astype(f32)
    there = (index_oth[...] == spot).astype(f32)
    hit = jnp.sum(here, axis=1, keepdims=True) + jnp.sum(there, axis=1, keepdims=True)
    put = dot(here.astype(bf16), own[...]) + dot(there.astype(bf16), oth[...])
    out[...] = jnp.where(hit > 0.5, put, base[...].astype(f32)).astype(bf16)


def put(index_own, index_oth, own, oth, base, deps=()):
    return run(
        put_body,
        (1,),
        [(index_own, None), (index_oth, None), (own, None), (oth, None), (base, None)],
        [(base.shape, bf16, None)],
        flops=2 * base.shape[0] * KEEP * D,
        deps=deps,
    )[0]


def on_device(
    n_dp,
    tokens,
    conditioning,
    segment_ids,
    kept_rows,
    cotangent,
    mod_first,
    qkv_first,
    proj_first,
    up_first,
    down_first,
    mod_second,
    qkv_second,
    proj_second,
    up_second,
    down_second,
):
    dp_pos = lax.axis_index("dp")
    side = lax.axis_index("tensor")
    core = dp_pos % 2
    bits = n_dp.bit_length() - 1

    def moves(where):
        pairs = []
        for dp in range(n_dp):
            for t in range(2):
                to_dp, to_t = where(dp, t)
                pairs.append((dp * 2 + t, to_dp * 2 + to_t))
        return pairs

    across = moves(lambda dp, t: (dp, 1 - t))
    core_swap = moves(lambda dp, t: (dp ^ 1, t))
    next_swap = moves(lambda dp, t: (dp ^ 2, t))
    turn = moves(lambda dp, t: (dp // 2 * 2 + t, dp % 2))
    deal = moves(lambda dp, t: (dp // 2 * 2 + 1 - t, dp % 2))
    undeal = moves(lambda dp, t: (dp // 2 * 2 + t, 1 - dp % 2))

    def send(value, pairs):
        return lax.ppermute(value, ALL, pairs)

    def after(value, *deps):
        return lax.optimization_barrier((value, *deps))[0]

    def to_owner(rows):
        tiles = rows.reshape(BLOCKS, SPAN // 2, D)
        return send(tiles[0::2], turn), send(tiles[1::2], deal)

    def owned(even, odd, *when):
        even, odd = after(even, *when), after(odd, *when)
        return jnp.where(core == 0, jnp.concatenate([even, odd]), jnp.concatenate([odd, even]))

    def from_owner(rows, begin=(), end=()):
        rows = after(rows.reshape(BLOCKS, SPAN // 2, D), *begin)
        even = after(send(lax.dynamic_slice_in_dim(rows, 2 * core, 3), turn), *end)
        odd = after(send(lax.dynamic_slice_in_dim(rows, 3 * (1 - core), 2), undeal), *end)
        shape = (3, 2, SPAN // 2, D)
        odd = jnp.pad(odd, ((0, 1), (0, 0), (0, 0)))
        even = jnp.broadcast_to(even[:, None], shape)
        odd = jnp.broadcast_to(odd[:, None], shape)
        second = lax.broadcasted_iota(jnp.int32, shape, 1) == 1
        both = jnp.where(second, odd, even).reshape(6 * SPAN // 2, D)
        return both[: BLOCKS * SPAN // 2]

    class Far:
        def __init__(self, near, bit, deps=()):
            self.swap = moves(lambda dp, t: (dp ^ 2**bit, t))
            self.first = send(after(near, *deps), across)

        def hop(self, *deps):
            first = after(self.first, *deps)
            self.third = send(first, self.swap)
            self.second = send(first, core_swap)

        def end(self, *deps):
            return self.first, self.second, self.third, send(after(self.third, *deps), core_swap)

    def part_of(value, axis, bit):
        size = value.shape[axis] // 4
        part = dp_pos // 2**bit % 2 * 2 + core
        return lax.dynamic_slice_in_dim(value, part * size, size, axis)

    numbers = send(jnp.concatenate([kept_rows, segment_ids[::SPAN]]), turn)
    cond = send(jax.nn.silu(conditioning.astype(f32)).astype(bf16), turn)
    wq_one = jnp.transpose(qkv_first, (1, 0, 2))
    wq_two = jnp.transpose(qkv_second, (1, 0, 2))
    place_ref = dp_pos.reshape(1).astype(jnp.int32)
    zero_ref = jnp.zeros((1,), jnp.int32)
    near_part = jnp.concatenate(
        [
            lax.dynamic_slice_in_dim(wq_one, core * HALF, HALF, 1),
            lax.dynamic_slice_in_dim(proj_first, core * HALF, HALF, 1)[None],
        ]
    )
    kept, segs = numbers[:KEEP], numbers[KEEP:]
    kind = jnp.where(segs[3] == segs[0], 0, jnp.where(segs[4] == segs[1], 1, 2)).reshape(1)
    slot_hot = segs[:, None] == jnp.arange(SLOTS, dtype=jnp.int32)[None, :]
    cond_rows = jnp.dot(slot_hot.astype(bf16), cond, preferred_element_type=f32).astype(bf16)

    def table(mod):
        return jnp.dot(cond_rows, mod, preferred_element_type=f32).reshape(BLOCKS, 6, D)

    arrived = to_owner(tokens)
    cond_rows = after(cond_rows, *arrived)
    tab_one, tab_two = table(mod_first), table(mod_second)

    block_of, inside = kept // SPAN, kept % SPAN
    spot = (
        jnp.where(inside // (SPAN // 2) == core, 0, GROUP // 2)
        + block_of * (SPAN // 2)
        + inside % (SPAN // 2)
    ).reshape(BLOCKS, 2, KEEP // (2 * BLOCKS))
    spot_own = lax.dynamic_slice_in_dim(spot, core, 1, 1).reshape(-1)
    spot_oth = lax.dynamic_slice_in_dim(spot, 1 - core, 1, 1).reshape(-1)
    spot_all = jnp.concatenate([spot_own, spot_oth])

    piece = D // n_dp
    row = jnp.arange(D, dtype=jnp.int32)
    turned = jnp.zeros_like(row)
    for bit in range(bits):
        turned = turned + (((row // piece) // 2 ** (bits - 1 - bit)) % 2) * 2**bit
    source = jnp.bitwise_xor(turned, dp_pos) * piece + row % piece
    order = (source[:, None] == row[None, :]).astype(bf16)
    pieces = min(n_dp, 16)
    deep = D // pieces
    which = dp_pos % pieces
    at = which * deep
    proj_piece = lax.dynamic_slice(
        proj_second, (at % HALF, at // HALF * HALF), (deep, HALF)
    )
    up_piece = lax.dynamic_slice_in_dim(up_second, at, deep).reshape(deep, 4, HALF)
    down_pieces = [
        lax.dynamic_slice_in_dim(down_second, row * D + at, deep).reshape(deep, 2, HALF)
        for row in range(2)
    ]
    pieces_two = jnp.concatenate(
        [
            lax.dynamic_slice_in_dim(wq_two, at, deep, 1),
            proj_piece[None],
            jnp.transpose(up_piece, (1, 0, 2)),
        ]
        + [down_pieces[row][None, :, column] for column in range(2) for row in range(2)]
    )
    piece_two = send(after(pieces_two, *arrived), across)
    w_near = send(after(near_part, *arrived), across)
    own = owned(*arrived, tab_one, tab_two, piece_two, order)
    oth = send(own, core_swap)

    def add(*terms):
        return functools.reduce(lambda p, q: p + q, [t.astype(f32) for t in terms])

    quarter = HALF // 2

    class Total:
        def cores(self, keep, away):
            got = send(away, core_swap)
            self.keep_n, self.keep_r, self.got_n, self.got_r = keep[0], keep[1], got[0], got[1]
            return self

        def cores_far(self, keep, away):
            self.keep_r, self.got_r = keep, send(away, core_swap)
            return self

        def cores_near(self, keep, away):
            self.keep_n, self.got_n = keep, send(away, core_swap)
            return self

        def far(self, *when):
            away = add(self.keep_r, after(self.got_r, *when)).astype(bf16)
            self.got = send(away, across)
            return (away,)

        def chips(self, *when):
            return add(self.keep_n, self.got_n, after(self.got, *when)).astype(bf16)

        def near(self, *when):
            terms = (self.keep_n, self.got_n, after(self.got, *when))
            away = add(*[t[quarter:] for t in terms]).astype(bf16)
            self.got = send(away, next_swap)
            self.terms = tuple(t[:quarter] for t in terms)
            return (away,)

        def sum(self, *when):
            return add(*self.terms, after(self.got, *when))

    class Rest:
        def __init__(self, acc, bit=2):
            self.acc, self.got, self.bit = acc, None, bit

        def next(self, *when):
            if self.bit == bits:
                return ()
            acc = self.acc
            if self.got is not None:
                acc = acc + after(self.got, *when).astype(f32)
            self.acc = acc
            size = self.acc.shape[0] // 2
            away = self.acc[size:].astype(bf16)
            bit = self.bit
            self.got = send(away, moves(lambda dp, t: (dp ^ 2**bit, t)))
            self.acc = self.acc[:size]
            self.bit = bit + 1
            return (away,)

        def sum(self, *when):
            return self.acc + after(self.got, *when).astype(f32)

        def end(self, *when):
            while self.bit < bits:
                self.next(*when)
            return self.acc + after(self.got, *when).astype(f32)

    normed_one, *near_one = project_first(own, oth, tab_one, wq_one)
    ups_one = Far(part_of(up_first, 1, 1), 1, (own,))
    downs_one = Far(part_of(down_first, 0, 2), 2, (own,))
    mixed_one_n, log_one_n = attend(kind, *near_one)
    w_parts = (w_near, send(after(w_near, mixed_one_n), core_swap))
    w_two_far = lax.all_gather(
        after(piece_two, own)[None],
        "dp",
        axis=0,
        tiled=True,
        axis_index_groups=[
            list(range(first, first + pieces)) for first in range(0, n_dp, pieces)
        ],
    )
    far_two_mlp = ([w_two_far] * 4, [w_two_far] * 4)
    w_one_far, *far_one = project_parts(
        place_ref, normed_one, w_parts, deps=(mixed_one_n,)
    )
    mixed_one_r, log_one_r = attend(kind, *far_one)
    ups_one.hop(mixed_one_r)
    downs_one.hop(mixed_one_r)
    attn_one, middle_one, normed_mlp_one, u_one_n, act_one_n, acc = feed_near(
        mixed_one_n, mixed_one_r, proj_first, w_one_far, own, tab_one, up_first, down_first
    )
    ups_one, downs_one = ups_one.end(normed_mlp_one), downs_one.end(normed_mlp_one)
    mlp_one = (up_first, down_first, ups_one, downs_one)
    cot_parts = to_owner(after(cotangent, normed_mlp_one))
    u_one_r, act_one_r, mlp_out_one, out_one = feed_far(
        place_ref, normed_mlp_one, acc, middle_one, tab_one, ups_one, downs_one
    )
    first_own = out_one.reshape(-1, D)
    first_oth = send(first_own, core_swap)

    routed = pick(spot_all[:, None], first_own, first_oth)
    routed_own, routed_oth = routed.reshape(2, BLOCKS, KEEP // (2 * BLOCKS), D)
    normed_two, *near_two = project_first(routed_own, routed_oth, tab_two, wq_two)
    mixed_two_n, log_two_n = attend(kind, *near_two)
    far_two = project_next(normed_two, w_two_far, deps=(mixed_two_n,))
    mixed_two_r, log_two_r = attend(kind, *far_two)
    cot_own = owned(*cot_parts, mixed_two_r)
    cot_oth = send(cot_own, core_swap)
    attn_two, middle_two, normed_mlp_two, u_two_n, act_two_n, acc = feed_near(
        mixed_two_n, mixed_two_r, proj_second, w_two_far, routed_own, tab_two, up_second,
        down_second,
    )
    first_out = from_owner(out_one, (mixed_two_r,), (normed_mlp_two,))
    mlp_two = (up_second, down_second, *far_two_mlp)
    u_two_r, act_two_r, mlp_out_two, out_two = feed_far(
        zero_ref, normed_mlp_two, acc, middle_two, tab_two, *mlp_two[2:], deps=(first_out,)
    )
    second_own = out_two.reshape(-1, D)
    second_oth = send(second_own, core_swap)
    cot_routed = pick(
        spot_own[:, None], cot_own.reshape(-1, D), cot_oth.reshape(-1, D), deps=(second_own,)
    ).reshape(routed_own.shape)

    g_keep, g_send, d_mlp, d_gate_two = down_back(
        zero_ref, cot_routed, tab_two, mlp_out_two, order, act_two_n, act_two_r
    )
    down_two = Total().cores(g_keep, g_send)
    saved = (attn_two, middle_two, normed_mlp_two, u_two_n, u_two_r)
    g_keep, g_send, p_keep, p_send, d_middle, d_mix_n, d_mix_r, d_mod_two = up_back(
        zero_ref, cot_routed, tab_two, d_mlp, saved, mlp_two, proj_second, w_two_far, mixed_two_n,
        mixed_two_r, order,
    )
    up_two = Total().cores(g_keep, g_send)
    sent = down_two.far(d_mix_r)
    grads_r = attend_back(kind, *far_two, d_mix_r, mixed_two_r, log_two_r, deps=sent)
    sent = up_two.far(grads_r[0])
    qr_keep, qr_send, normed_t, acc = qkv_back(
        True, 1, grads_r, w_two_far, normed_two, order, None, None, p_keep, p_send, deps=sent
    )
    qkv_two = Total().cores_far(qr_keep, qr_send)
    grads_n = attend_back(kind, *near_two, d_mix_n, mixed_two_n, log_two_n, deps=(acc, down_two.got))
    sent = qkv_two.far(grads_n[0])
    qn_keep, qn_send, d_own, d_oth = qkv_back(
        False, 0, grads_n, wq_two, normed_two, None, normed_t, acc, p_keep, p_send, deps=sent
    )
    d_got = send(d_oth, core_swap)
    qkv_two.cores_near(qn_keep, qn_send)
    d_two, d_mod_two_a = finish(
        d_own, d_got, routed_own, tab_two, d_middle
    )
    d_two_own = d_two.reshape(-1, D)
    d_two_oth = send(d_two_own, core_swap)

    def slot_sums(*parts):
        per_block = jnp.concatenate(parts, axis=1).reshape(BLOCKS, -1)
        return lax.dot_general(
            slot_hot.astype(f32),
            per_block,
            (((0,), (0,)), ((), ())),
            precision=lax.Precision.HIGHEST,
        ).astype(bf16)

    routed_rows = put(
        spot_own[None], spot_oth[None], second_own, second_oth, first_own, deps=(d_two_own,)
    )
    d_first = put(
        spot_own[None], spot_oth[None], d_two_own, d_two_oth, cot_own.reshape(-1, D),
        deps=(routed_rows,),
    ).reshape(own.shape)
    g_keep, g_send, d_mlp, d_gate = down_back(
        place_ref, d_first, tab_one, mlp_out_one, order, act_one_n, act_one_r, deps=(up_two.got,)
    )
    down_one = Total().cores(g_keep, g_send)
    mlp_rest_two = Rest(jnp.concatenate([t.chips(d_mlp) for t in (down_two, up_two)], axis=1), 1)
    sent = mlp_rest_two.next()
    saved = (attn_one, middle_one, normed_mlp_one, u_one_n, u_one_r)
    g_keep, g_send, p_keep, p_send, d_middle, d_mix_n, d_mix_r, d_mod = up_back(
        place_ref, d_first, tab_one, d_mlp, saved, mlp_one, proj_first, w_one_far, mixed_one_n,
        mixed_one_r, order, deps=sent,
    )
    up_one = Total().cores(g_keep, g_send)
    qkv_rest_two = Rest(qkv_two.chips(d_mix_r), 1)
    sent = (*down_one.far(d_mix_r), *qkv_rest_two.next())
    early = lax.all_gather(
        jnp.concatenate(
            [cond, slot_sums(d_mod_two_a, d_mod_two, d_gate_two), slot_sums(d_mod, d_gate)], axis=1
        ),
        ALL,
        axis=0,
        tiled=True,
    )
    grads_r = attend_back(kind, *far_one, d_mix_r, mixed_one_r, log_one_r, deps=sent)
    rest_two = Rest(
        jnp.concatenate([t.sum(grads_r[0]) for t in (mlp_rest_two, qkv_rest_two)], axis=1)
    )
    sent = (*up_one.far(grads_r[0]), *rest_two.next())
    qr_keep, qr_send, normed_t, acc = qkv_back(
        True, 1, grads_r, w_one_far, normed_one, order, None, None, p_keep, p_send,
        deps=sent,
    )
    qkv_one = Total().cores_far(qr_keep, qr_send)
    sent = down_one.near(acc)
    grads_n = attend_back(kind, *near_one, d_mix_n, mixed_one_n, log_one_n, deps=sent)
    done = grads_n[0]
    sent = (*qkv_one.far(done), *up_one.near(done), *rest_two.next(done))
    qn_keep, qn_send, d_own, d_oth = qkv_back(
        False, 0, grads_n, wq_one, normed_one, None, normed_t, acc, p_keep, p_send, deps=sent
    )
    d_got = send(d_oth, core_swap)
    qkv_one.cores_near(qn_keep, qn_send)
    routed_out = from_owner(routed_rows, (grads_r[0],), (d_own,))
    mlp_rest = Rest(jnp.concatenate([down_one.sum(d_own), up_one.sum(d_own)], axis=1))
    sent = (*mlp_rest.next(), routed_out)
    d_one, d_mod_a = finish(d_own, d_got, own, tab_one, d_middle, deps=(*sent, qkv_one.got_n))

    last = qkv_one.near(d_one)
    late = after(jnp.pad(slot_sums(d_mod_a), ((0, 8 - SLOTS), (0, 0))), *last)
    late = (late.astype(f32) + send(late, core_swap).astype(f32)).astype(bf16)[None]
    sources = jnp.array([dp_pos * 2 + side])

    def doubled(late, sources, mask):
        pairs = moves(lambda dp, t: ((dp * 2 + t ^ mask) // 2, (t ^ mask) % 2))
        late = jnp.concatenate([late, send(late, pairs)])
        return late, jnp.concatenate([sources, jnp.bitwise_xor(sources, mask)])

    late, sources = doubled(late, sources, 1)
    qkv_rest = Rest(qkv_one.sum(late))
    last = qkv_rest.next()
    mlp_rest.next(*last)
    for bit in range(2, bits):
        late, sources = doubled(after(late, *last), sources, 2**bit)
        last = qkv_rest.next(late) or last
    late, sources = doubled(after(late, *last), sources, 2**bits)
    input_grad = from_owner(d_one, (), last).astype(f32)
    early = after(early, *last)
    mlp_total = mlp_rest.end(*last)
    total_two = rest_two.end(*last)
    qkv_total = qkv_rest.end(late)

    mod_rows = D // (n_dp * 2)
    mine = lax.dynamic_slice_in_dim(early[:, :D], (dp_pos * 2 + side) * mod_rows, mod_rows, 1)
    mine_late = jnp.pad(
        mine.reshape(-1, SLOTS, mod_rows)[sources], ((0, 0), (0, 8 - SLOTS), (0, 0))
    ).reshape(-1, mod_rows)
    mod_two_end = 7 * D
    mod_one = jnp.concatenate(
        [
            dot_rows(mine_late, late.reshape(-1, 2 * D)),
            dot_rows(mine, early[:, mod_two_end:]),
        ],
        axis=1,
    )
    mod_two = dot_rows(mine, early[:, D:mod_two_end])
    wide = 2 * TILE

    def placed(attention, down, up):
        qkv = attention[:, : 3 * HALF].reshape(piece, 3, HALF)
        return qkv, attention[:, 3 * HALF :].T, up, down.T

    return (
        first_out,
        routed_out,
        input_grad,
        mod_one,
        *placed(qkv_total, mlp_total[:, :wide], mlp_total[:, wide:]),
        mod_two,
        *placed(
            total_two[:, 2 * wide :].astype(f32),
            total_two[:, :wide].astype(f32),
            total_two[:, wide : 2 * wide].astype(f32),
        ),
    )


def solution(mesh):
    n_dp = mesh.shape["dp"]
    return jax.shard_map(
        functools.partial(on_device, n_dp),
        mesh=mesh,
        in_specs=(
            P(("dp", "tensor"), None),
            P("dp", None),
            P("dp"),
            P("dp"),
            P(("dp", "tensor"), None),
            P(),
            P(None, None, "tensor"),
            P("tensor", None),
            P(None, "tensor"),
            P("tensor", None),
            P(),
            P(None, None, "tensor"),
            P("tensor", None),
            P(None, "tensor"),
            P("tensor", None),
        ),
        out_specs=(
            P(("dp", "tensor"), None),
            P(("dp", "tensor"), None),
            P(("dp", "tensor"), None),
            P(("dp", "tensor"), None),
            P("dp", None, "tensor"),
            P("tensor", "dp"),
            P("dp", "tensor"),
            P("tensor", "dp"),
            P(("dp", "tensor"), None),
            P("dp", None, "tensor"),
            P("tensor", "dp"),
            P("dp", "tensor"),
            P("tensor", "dp"),
        ),
        check_vma=False,
    )
```

```python
import functools

import jax
import jax.numpy as jnp
from jax import lax
from jax.experimental import pallas as pl
from jax.experimental.pallas import tpu as pltpu
from jax.sharding import PartitionSpec as P

D = 768
HEAD_DIM = 64
SLOTS = 5
GROUP = 1280
KEEP = 640
BLOCKS = 5
SPAN = GROUP // BLOCKS
HALF = D // 2
TILE = 768
NORM_EPS = 1e-06
f32 = jnp.float32
bf16 = jnp.bfloat16
ALL = ("dp", "tensor")
VMEM_BYTES = 24 * 1024 * 1024
LIGHT = 2000


def dot(left, right):
    return jnp.dot(left, right, preferred_element_type=f32)


def dot_cols(left, right):
    return lax.dot_general(left, right, (((1,), (1,)), ((), ())), preferred_element_type=f32)


def dot_rows(left, right):
    return lax.dot_general(left, right, (((0,), (0,)), ((), ())), preferred_element_type=f32)


def unit_rows(rows):
    centre = rows - jnp.mean(rows, axis=-1, keepdims=True)
    inverse = lax.rsqrt(jnp.mean(centre * centre, axis=-1, keepdims=True) + NORM_EPS)
    return centre * inverse, inverse


def norm_back(d_normed, unit, inverse, scale_row):
    e = d_normed * (1.0 + scale_row)
    return inverse * (
        e
        - jnp.mean(e, axis=-1, keepdims=True)
        - unit * jnp.mean(e * unit, axis=-1, keepdims=True)
    )


def col_sum(rows):
    return jnp.sum(rows, axis=0, keepdims=True)


def flat(ref):
    value = ref[...]
    return value.reshape(-1, value.shape[-1])


def whole(shape):
    return pl.BlockSpec(shape, lambda *_: (0,) * len(shape), pipeline_mode=pl.Buffered(1))


def run(body, grid, ins, outs, scratch=(), scalars=(), flops=0, deps=()):
    in_specs = [whole(a.shape) if s is None else s for a, s in ins]
    in_specs += [pl.BlockSpec(memory_space=pl.ANY)] * len(deps)
    first, past = len(scalars) + len(ins), len(scalars) + len(ins) + len(deps)

    def step(*refs):
        body(*refs[:first], *refs[past:])

    out_specs = [whole(sh) if s is None else s for sh, _, s in outs]
    moved = sum(a.size * a.dtype.itemsize for a, _ in ins)
    moved += sum(jnp.dtype(d).itemsize * functools.reduce(lambda p, q: p * q, sh, 1) for sh, d, _ in outs)
    return pl.pallas_call(
        step,
        grid_spec=pltpu.PrefetchScalarGridSpec(
            num_scalar_prefetch=len(scalars),
            grid=grid,
            in_specs=in_specs,
            out_specs=out_specs,
            scratch_shapes=list(scratch),
        ),
        out_shape=[jax.ShapeDtypeStruct(sh, d) for sh, d, _ in outs],
        compiler_params=pltpu.CompilerParams(
            vmem_limit_bytes=VMEM_BYTES, dimension_semantics=("arbitrary",) * len(grid)
        ),
        cost_estimate=pl.CostEstimate(
            flops=1 + int(flops) // LIGHT, bytes_accessed=1 + int(moved) // LIGHT, transcendentals=0
        ),
    )(*scalars, *[a for a, _ in ins], *deps)


def qkv_body(own, oth, tab, w, normed, q, k, v):
    rows = own.shape[1]
    step = pl.program_id(0)

    @pl.when(step == 0)
    def _():
        for side, src in ((0, own), (1, oth)):
            for i in range(BLOCKS):
                unit, _ = unit_rows(src[i].astype(f32))
                normed[side, i] = (unit * (1.0 + tab[i, 1:2]) + tab[i, 0:1]).astype(bf16)

    qkv_steps(step, normed, w, q, k, v)


def qkv_next_body(normed, w, q, k, v):
    qkv_steps(pl.program_id(0), normed, w, q, k, v)


def qkv_parts_body(place, normed, w_0, w_1, w, q, k, v):
    for index, part in enumerate((w_0, w_1)):
        at = pl.multiple_of((place[0] % 2 ^ index) * HALF, HALF)
        w[0, pl.ds(at, HALF)] = part[0]
    qkv_steps(pl.program_id(0), normed, w, q, k, v)


def block(w):
    return w[...].reshape(D, HALF)


def qkv_steps(step, normed, w, q, k, v):
    @pl.when(step == 0)
    def _():
        mine = normed[0].reshape(-1, D)
        q[...] = dot(mine, block(w)).astype(bf16).reshape(q.shape)

    for index, out in ((1, k), (2, v)):

        @pl.when(step == index)
        def _(out=out):
            out[...] = dot(flat(normed), block(w)).astype(bf16).reshape(out.shape)


def qkv_outs(rows):
    return [
        ((BLOCKS, rows, HALF), bf16, None),
        ((2, BLOCKS, rows, HALF), bf16, None),
        ((2, BLOCKS, rows, HALF), bf16, None),
    ]


BY_STEP = pl.BlockSpec((1, D, HALF), lambda j, *_: (j, 0, 0))


def block_at(w, index):
    if w.ndim == 3:
        return (w, pl.BlockSpec((1, D, HALF), lambda j, *_: (index(j), 0, 0)))
    pieces, _, rows, _ = w.shape
    return (w, pl.BlockSpec((pieces, 1, rows, HALF), lambda j, *_: (0, index(j), 0, 0)))


def project_first(own, oth, tab, w, deps=()):
    rows = own.shape[1]
    return run(
        qkv_body,
        (3,),
        [(own, None), (oth, None), (tab, None), (w, BY_STEP)],
        [((2, BLOCKS, rows, D), bf16, None)] + qkv_outs(rows),
        flops=2 * 25 * rows * D * HALF,
        deps=deps,
    )


def project_next(normed, w, deps=()):
    rows = normed.shape[2]
    ins = [(normed, None), block_at(w, lambda j: j)]
    return run(qkv_next_body, (3,), ins, qkv_outs(rows), flops=2 * 25 * rows * D * HALF, deps=deps)


def project_parts(place, normed, parts, deps=()):
    rows = normed.shape[2]
    by_step = pl.BlockSpec((1, HALF, HALF), lambda j, *_: (j, 0, 0))
    return run(
        qkv_parts_body,
        (4,),
        [(normed, None)] + [(part, by_step) for part in parts],
        [((4, D, HALF), bf16, BY_STEP)] + qkv_outs(rows),
        scalars=(place,),
        flops=2 * 25 * rows * D * HALF,
        deps=deps,
    )


def by_sequence(kind, one_sequence, long_tiles):
    @pl.when(kind < 2)
    def _():
        one_sequence(kind, 4, long_tiles)
        one_sequence(jnp.where(kind == 0, 4, 0), 1, 1)

    @pl.when(kind == 2)
    def _():
        def short(i, carry):
            one_sequence(i, 1, 1)
            return carry

        lax.fori_loop(0, BLOCKS, short, 0)


def two_heads(rows, low):
    zero = jnp.zeros_like(rows)
    return jnp.concatenate([jnp.where(low, rows, zero), jnp.where(low, zero, rows)], axis=0)


def attend_body(kind, q, k, v, out):
    rows = q.shape[1]
    low = lax.broadcasted_iota(jnp.int32, (1, 128), 1) < HEAD_DIM
    scaling = HEAD_DIM ** (-0.5)

    def one_sequence(start, count, tiles):
        keys = k[:, pl.ds(start, count)].reshape(2 * count * rows, 128)
        values = v[:, pl.ds(start, count)].reshape(2 * count * rows, 128)
        size = tiles * rows
        for part in range(count // tiles):
            at = pl.ds(start + part * tiles, tiles)
            pair = two_heads((q[at].reshape(size, 128) * scaling).astype(bf16), low)
            scores = dot_cols(pair, keys)
            shifted = jnp.exp(scores - jnp.max(scores, axis=-1, keepdims=True))
            total = jnp.sum(shifted, axis=-1, keepdims=True)
            mixed = dot(shifted.astype(bf16), values) * (1.0 / total)
            out[at] = jnp.where(low, mixed[:size], mixed[size:]).astype(bf16).reshape(tiles, rows, 128)

    by_sequence(kind[0], one_sequence, 128 // rows)


def attend(kind, q, k, v, deps=()):
    rows = q.shape[1]
    own = pl.BlockSpec((BLOCKS, rows, 128), lambda p, *_: (0, 0, p))
    every = pl.BlockSpec((2, BLOCKS, rows, 128), lambda p, *_: (0, 0, 0, p))
    return run(
        attend_body,
        (HALF // 128,),
        [(q, own), (k, every), (v, every)],
        [(q.shape, bf16, own)],
        scalars=(kind,),
        flops=16 * BLOCKS * rows * 8 * rows * HALF,
        deps=deps,
    )[0]


def attend_back_body(kind, q, k, v, d_out, dq, dk, dv, acc_k, acc_v):
    rows = q.shape[1]
    low = lax.broadcasted_iota(jnp.int32, (1, 128), 1) < HEAD_DIM
    scaling = HEAD_DIM ** (-0.5)

    def one_sequence(start, count, tiles):
        key_rows = 2 * count * rows
        keys = k[:, pl.ds(start, count)].reshape(key_rows, 128)
        values = v[:, pl.ds(start, count)].reshape(key_rows, 128)
        size = tiles * rows
        for part in range(count // tiles):
            at = pl.ds(start + part * tiles, tiles)
            pair = two_heads((q[at].reshape(size, 128) * scaling).astype(bf16), low)
            d_pair = two_heads(d_out[at].reshape(size, 128), low)
            scores = dot_cols(keys, pair)
            shifted = jnp.exp(scores - jnp.max(scores, axis=0, keepdims=True))
            probs = shifted * (1.0 / jnp.sum(shifted, axis=0, keepdims=True))
            d_probs = dot_cols(values, d_pair)
            row_sum = jnp.sum(probs * d_probs, axis=0, keepdims=True)
            d_scores = (probs * (d_probs - row_sum)).astype(bf16)
            add_v = dot(probs.astype(bf16), d_pair)
            add_k = dot(d_scores, pair)
            if part == 0:
                acc_v[:key_rows] = add_v
                acc_k[:key_rows] = add_k
            else:
                acc_v[:key_rows] += add_v
                acc_k[:key_rows] += add_k
            both = dot_rows(d_scores, keys) * scaling
            dq[at] = jnp.where(low, both[:size], both[size:]).astype(bf16).reshape(tiles, rows, 128)
        dk[:, pl.ds(start, count)] = acc_k[:key_rows].astype(bf16).reshape(2, count, rows, 128)
        dv[:, pl.ds(start, count)] = acc_v[:key_rows].astype(bf16).reshape(2, count, rows, 128)

    by_sequence(kind[0], one_sequence, 128 // rows)


def attend_back(kind, q, k, v, d_out, deps=()):
    rows = q.shape[1]
    own = pl.BlockSpec((BLOCKS, rows, 128), lambda p, *_: (0, 0, p))
    every = pl.BlockSpec((2, BLOCKS, rows, 128), lambda p, *_: (0, 0, 0, p))
    return run(
        attend_back_body,
        (HALF // 128,),
        [(q, own), (k, every), (v, every), (d_out, own)],
        [(q.shape, bf16, own), (k.shape, bf16, every), (v.shape, bf16, every)],
        scratch=[pltpu.VMEM((8 * rows, 128), f32), pltpu.VMEM((8 * rows, 128), f32)],
        scalars=(kind,),
        flops=40 * BLOCKS * rows * 8 * rows * HALF,
        deps=deps,
    )


def gelu_parts(u):
    rate = 0.7978845608028654
    inner = rate * (u + 0.044715 * (u * u * u))
    return jnp.tanh(inner), rate


def hidden(normed, ups, downs, u, act):
    start = 0
    total = None
    ups = [far_up(up) for up in ups]
    for up, down in zip(ups, downs):
        at = slice(start, start + up.shape[1])
        start = start + up.shape[1]
        pre = dot(flat(normed), up)
        u[0, :, at] = pre.astype(bf16)
        tanh, _ = gelu_parts(pre)
        value = (0.5 * pre * (1.0 + tanh)).astype(bf16)
        act[0, :, at] = value
        term = dot(value, down[...])
        total = term if total is None else total + term
    return total


def mlp_near_body(
    mixed_n, mixed_r, proj_n, proj_r, own, tab, up, down,
    attn_out, middle, normed, u, act, acc,
):
    rows = own.shape[1]
    step = pl.program_id(0)

    @pl.when(step == 0)
    def _():
        for at in (slice(0, HALF), slice(HALF, D)):
            acc[:, at] = dot(flat(mixed_n), proj_n[:, at]) + dot(flat(mixed_r), block(proj_r)[at])
        for i in range(BLOCKS):
            attn = acc[i * rows : (i + 1) * rows]
            attn_out[i] = attn.astype(bf16)
            mid = own[i].astype(f32) + tab[i, 2:3] * attn
            middle[i] = mid
            unit, _ = unit_rows(mid)
            normed[i] = (unit * (1.0 + tab[i, 4:5]) + tab[i, 3:4]).astype(bf16)
        acc[...] = hidden(normed, [up], [down], u, act)

    @pl.when(step == 1)
    def _():
        acc[...] += hidden(normed, [up], [down], u, act)


def matching(place, down_0, down_1, down_2, down_3):
    refs = (down_0, down_1, down_2, down_3)
    if len(down_0.shape) > 2:
        return (lambda: far_downs(refs)[:2]), (lambda: far_downs(refs)[2:])
    same = (place[0] // 2 + place[0] // 4) % 2 == 0

    def first():
        return [
            jnp.where(same, down_0[...], down_2[...]),
            jnp.where(same, down_1[...], down_3[...]),
        ]

    def second():
        return [
            jnp.where(same, down_2[...], down_0[...]),
            jnp.where(same, down_3[...], down_1[...]),
        ]

    return first, second


def mlp_far_body(
    place, normed, start, middle, tab, up_0, up_1, up_2, up_3, down_0, down_1, down_2, down_3,
    u, act, mlp_out, out, acc,
):
    rows = middle.shape[1]
    step = pl.program_id(0)
    first, second = matching(place, down_0, down_1, down_2, down_3)

    @pl.when(step == 0)
    def _():
        acc[...] = start[...] + hidden(normed, [up_0, up_1], first(), u, act)

    @pl.when(step == 1)
    def _():
        acc[...] += hidden(normed, [up_2, up_3], second(), u, act)
        for i in range(BLOCKS):
            term = acc[i * rows : (i + 1) * rows]
            mlp_out[i] = term.astype(bf16)
            out[i] = (middle[i] + tab[i, 5:6] * term).astype(bf16)


def projection(w):
    return block_at(w, lambda j: 3)


def far_up(ref):
    return ref[...] if len(ref.shape) == 2 else block(ref)


def far_downs(downs):
    if len(downs[0].shape) == 2:
        return [down[...] for down in downs]
    wide = [
        jnp.concatenate([block(downs[index]), block(downs[index + 2])], axis=1) for index in range(2)
    ]
    return [wide[0][:HALF], wide[0][HALF:], wide[1][:HALF], wide[1][HALF:]]


def far_ins(ups, downs):
    if ups[0].ndim == 2:
        return [(part, None) for part in (*ups, *downs)]
    ins = []
    for index, part in enumerate((*ups, *downs)):
        pieces, _, rows, _ = part.shape
        at = pl.BlockSpec(
            (pieces, 1, rows, HALF),
            lambda *_, index=index: (0, 4 + index, 0, 0),
            pipeline_mode=pl.Buffered(1),
        )
        ins.append((part, at))
    return ins


def feed_near(mixed_n, mixed_r, proj_n, w_r, own, tab, up, down, deps=()):
    rows = own.shape[1]
    total = BLOCKS * rows
    tiles = ((2, total, TILE), bf16, pl.BlockSpec((1, total, TILE), lambda j: (j, 0, 0)))
    return run(
        mlp_near_body,
        (2,),
        [
            (mixed_n, None),
            (mixed_r, None),
            (proj_n, None),
            projection(w_r),
            (own, None),
            (tab, None),
            (up, pl.BlockSpec((D, TILE), lambda j: (0, j))),
            (down, pl.BlockSpec((TILE, D), lambda j: (j, 0))),
        ],
        [
            (own.shape, bf16, None),
            (own.shape, f32, None),
            (own.shape, bf16, None),
            tiles,
            tiles,
            ((total, D), f32, None),
        ],
        flops=2 * total * D * (D + 4 * D),
        deps=deps,
    )


def feed_far(place, normed, start, middle, tab, ups, downs, deps=()):
    total = BLOCKS * normed.shape[1]
    tiles = ((2, total, TILE), bf16, pl.BlockSpec((1, total, TILE), lambda j, *_: (j, 0, 0)))
    return run(
        mlp_far_body,
        (2,),
        [(normed, None), (start, None), (middle, None), (tab, None)]
        + far_ins(ups, downs),
        [tiles, tiles, (normed.shape, bf16, None), (normed.shape, bf16, None)],
        scratch=[pltpu.VMEM((total, D), f32)],
        scalars=(place,),
        flops=2 * total * D * (4 * D),
        deps=deps,
    )


def tile_of(j, place_ref):
    far = jnp.where(place_ref[0] // 2 % 2 == 0, j % 2, 1 - j % 2)
    return (j // 2, 0, jnp.where(j < 2, j % 2, far))


MLP_GRAD = ((2, HALF, 2 * TILE), bf16, pl.BlockSpec((1, HALF, TILE), tile_of))


def both_halves(near, far):
    size = near.shape[1]
    return [
        (near, pl.BlockSpec((1, size, TILE), lambda j, *_: (jnp.minimum(j, 1), 0, 0))),
        (far, pl.BlockSpec((1, size, TILE), lambda j, *_: (jnp.maximum(j - 2, 0), 0, 0))),
    ]


def store_grad(keep, away, at, size, value):
    there = pl.ds(at, size)
    keep[0, :, there] = value[:HALF]
    away[0, :, there] = value[HALF:]


def down_back_body(
    place, d_out, tab, mlp_out, order, act_n, act_r, g_keep, g_send, d_mlp, d_gate, d_mlp_t
):
    rows = d_out.shape[1]
    step = pl.program_id(0)
    core = place[0] % 2

    @pl.when(step == 0)
    def _():
        for i in range(BLOCKS):
            grad = d_out[i].astype(f32)
            d_mlp[i * rows : (i + 1) * rows] = (grad * tab[i, 5:6]).astype(bf16)
            d_gate[i] = col_sum(grad * mlp_out[i].astype(f32))
        d_mlp_t[...] = dot_cols(order[...], d_mlp[...]).astype(bf16)

    @pl.when(step < 2)
    def _():
        store_grad(g_keep, g_send, 0, TILE, dot(d_mlp_t[...], act_n[0]).astype(bf16))

    @pl.when(step >= 2)
    def _():
        for index in range(2):
            value = act_r[0, :, index * HALF : (index + 1) * HALF]
            at = pl.multiple_of((core if index == 0 else 1 - core) * HALF, 128)
            store_grad(g_keep, g_send, at, HALF, dot(d_mlp_t[...], value).astype(bf16))


def down_back(place, d_out, tab, mlp_out, order, act_n, act_r, deps=()):
    total = BLOCKS * d_out.shape[1]
    return run(
        down_back_body,
        (4,),
        [(d_out, None), (tab, None), (mlp_out, None), (order, None)] + both_halves(act_n, act_r),
        [MLP_GRAD, MLP_GRAD, ((total, D), bf16, None), ((BLOCKS, 1, D), f32, None)],
        scratch=[pltpu.VMEM((D, total), bf16)],
        scalars=(place,),
        flops=2 * total * D * 5 * D,
        deps=deps,
    )


def up_back_body(
    place, d_out, tab, d_mlp, normed, u_n, u_r,
    up_n, down_n, up_0, up_1, up_2, up_3, down_0, down_1, down_2, down_3,
    middle, attn_out, proj_n, proj_r, mixed_n, mixed_r, order,
    g_keep, g_send, p_keep, p_send, d_middle, d_mix_n, d_mix_r, d_mod,
    d_attn, turned, acc,
):
    rows = d_out.shape[1]
    step = pl.program_id(0)
    core = place[0] % 2

    @pl.when(step == 0)
    def _():
        turned[...] = dot_cols(order[...], flat(normed)).astype(bf16)

    def back(u, ups, downs, places):
        start = 0
        total = None
        ups = [far_up(up) for up in ups]
        for up, down, at in zip(ups, downs, places):
            size = up.shape[1]
            pre = u[0, :, start : start + size].astype(f32)
            start = start + size
            tanh, rate = gelu_parts(pre)
            slope = 0.5 * (1.0 + tanh) + (0.5 * rate) * pre * (1.0 - tanh * tanh) * (
                1.0 + (3.0 * 0.044715) * (pre * pre)
            )
            d_up = (slope * dot_cols(d_mlp[...], down[...])).astype(bf16)
            store_grad(g_keep, g_send, at, size, dot(turned[...], d_up).astype(bf16))
            term = dot_cols(d_up, up)
            total = term if total is None else total + term
        return total

    both = [pl.multiple_of(core * HALF, 128), pl.multiple_of((1 - core) * HALF, 128)]
    first, second = matching(place, down_0, down_1, down_2, down_3)

    @pl.when(step == 0)
    def _():
        acc[...] = back(u_n, [up_n], [down_n], [0])

    @pl.when(step == 1)
    def _():
        acc[...] += back(u_n, [up_n], [down_n], [0])

    @pl.when(step == 2)
    def _():
        acc[...] += back(u_r, [up_0, up_1], first(), both)

    @pl.when(step == 3)
    def _():
        acc[...] += back(u_r, [up_2, up_3], second(), both)
        for i in range(BLOCKS):
            at = slice(i * rows, (i + 1) * rows)
            d_normed = acc[at]
            unit, inverse = unit_rows(middle[i])
            grad = d_out[i].astype(f32) + norm_back(d_normed, unit, inverse, tab[i, 4:5])
            d_middle[i] = grad
            d_mod[i, 0:1] = col_sum(grad * attn_out[i].astype(f32))
            d_mod[i, 1:2] = col_sum(d_normed)
            d_mod[i, 2:3] = col_sum(d_normed * unit)
            d_attn[at] = (grad * tab[i, 2:3]).astype(bf16)
        turned[...] = dot_cols(order[...], d_attn[...]).astype(bf16)
        d_rows_n = dot_cols(d_attn[...], proj_n[...])
        far = block(proj_r)
        d_rows_r = dot_cols(d_attn[:, :HALF], far[:HALF]) + dot_cols(d_attn[:, HALF:], far[HALF:])
        for side, mixed, d_rows, d_mix in (
            (0, mixed_n, d_rows_n, d_mix_n),
            (1, mixed_r, d_rows_r, d_mix_r),
        ):
            d_mix[...] = d_rows.astype(bf16).reshape(d_mix.shape)
            g_proj = dot(turned[...], flat(mixed)).astype(bf16)
            p_keep[side] = g_proj[:HALF]
            p_send[side] = g_proj[HALF:]


def up_back(place, d_out, tab, d_mlp, saved, weights, proj_n, w_r, mixed_n, mixed_r, order, deps=()):
    attn_out, middle, normed, u_n, u_r = saved
    up, down, ups, downs = weights
    rows = d_out.shape[1]
    total = BLOCKS * rows
    here = lambda j: jnp.minimum(j, 1)
    return run(
        up_back_body,
        (4,),
        [(d_out, None), (tab, None), (d_mlp, None), (normed, None)]
        + both_halves(u_n, u_r)
        + [
            (up, pl.BlockSpec((D, TILE), lambda j, *_: (0, here(j)))),
            (down, pl.BlockSpec((TILE, D), lambda j, *_: (here(j), 0))),
        ]
        + far_ins(ups, downs)
        + [
            (middle, None),
            (attn_out, None),
            (proj_n, None),
            projection(w_r),
            (mixed_n, None),
            (mixed_r, None),
            (order, None),
        ],
        [
            MLP_GRAD,
            MLP_GRAD,
            ((2, HALF, HALF), bf16, None),
            ((2, HALF, HALF), bf16, None),
            (d_out.shape, f32, None),
            (mixed_n.shape, bf16, None),
            (mixed_n.shape, bf16, None),
            ((BLOCKS, 3, D), f32, None),
        ],
        scratch=[
            pltpu.VMEM((total, D), bf16),
            pltpu.VMEM((D, total), bf16),
            pltpu.VMEM((total, D), f32),
        ],
        scalars=(place,),
        flops=2 * total * D * (12 * D + 4 * D),
        deps=deps,
    )


def qkv_back_steps(step, grads, w, turned, p_keep, p_send, g_keep, g_send, acc, start):
    total = grads[0].shape[0] * grads[0].shape[1]

    for index, grad in enumerate(grads):

        @pl.when(step == index)
        def _(index=index, grad=grad):
            value = flat(grad)
            term = dot_cols(value, block(w))
            if index == 0:
                g_w = dot(turned[:, :total], value).astype(bf16)
                start(term)
            else:
                g_w = dot(turned[...], value).astype(bf16)
                acc[...] += term
            g_keep[...] = g_w[:HALF]
            g_send[...] = g_w[HALF:]

    @pl.when(step == 3)
    def _():
        g_keep[...] = p_keep[0]
        g_send[...] = p_send[0]


def qkv_back_body(
    dq, dk, dv, w, normed, order, p_keep, p_send, g_keep, g_send, turned, acc
):
    total = dq.shape[0] * dq.shape[1]
    step = pl.program_id(0)

    @pl.when(step == 0)
    def _():
        turned[...] = dot_cols(order[...], flat(normed)).astype(bf16)

    def start(term):
        acc[:total] = term
        acc[total:] = jnp.zeros((total, D), f32)

    qkv_back_steps(step, (dq, dk, dv), w, turned, p_keep, p_send, g_keep, g_send, acc, start)


def qkv_back_next_body(
    dq, dk, dv, w, turned, before, p_keep, p_send, g_keep, g_send, d_own, d_oth, acc
):
    total = dq.shape[0] * dq.shape[1]
    step = pl.program_id(0)

    def start(term):
        acc[...] = before[...]
        acc[:total] += term

    qkv_back_steps(step, (dq, dk, dv), w, turned, p_keep, p_send, g_keep, g_send, acc, start)

    @pl.when(step == 3)
    def _():
        d_own[...] = acc[:total]
        d_oth[...] = acc[total:].astype(bf16)


def qkv_back(first, side, grads, w, normed, order, turned, before, p_keep, p_send, deps=()):
    rows = normed.shape[2]
    total = BLOCKS * rows
    grad = ((HALF, 4 * HALF), bf16, pl.BlockSpec((HALF, HALF), lambda j: (0, j)))
    piece = pl.BlockSpec((1, HALF, HALF), lambda j: (side, 0, 0))
    ins = [(g, None) for g in grads]
    ins += [block_at(w, lambda j: jnp.minimum(j, 2))]
    ends = [(p_keep, piece), (p_send, piece)]
    flops = 2 * total * D * 10 * HALF
    if first:
        return run(
            qkv_back_body,
            (4,),
            ins + [(normed, None), (order, None)] + ends,
            [grad, grad, ((D, 2 * total), bf16, None), ((2 * total, D), f32, None)],
            flops=flops + 4 * total * D * D,
            deps=deps,
        )
    return run(
        qkv_back_next_body,
        (4,),
        ins + [(turned, None), (before, None)] + ends,
        [grad, grad, ((total, D), f32, None), ((total, D), bf16, None)],
        scratch=[pltpu.VMEM((2 * total, D), f32)],
        flops=flops,
        deps=deps,
    )


def finish_body(d_own, d_got, own, tab, d_middle, d_rows, d_mod):
    rows = own.shape[1]
    for i in range(BLOCKS):
        at = slice(i * rows, (i + 1) * rows)
        d_normed = d_own[at] + d_got[at].astype(f32)
        unit, inverse = unit_rows(own[i].astype(f32))
        grad = d_middle[i] + norm_back(d_normed, unit, inverse, tab[i, 1:2])
        d_rows[i] = grad.astype(bf16)
        d_mod[i, 0:1] = col_sum(d_normed)
        d_mod[i, 1:2] = col_sum(d_normed * unit)


def finish(d_own, d_got, own, tab, d_middle, deps=()):
    return run(
        finish_body,
        (1,),
        [(d_own, None), (d_got, None), (own, None), (tab, None), (d_middle, None)],
        [(own.shape, bf16, None), ((BLOCKS, 2, D), f32, None)],
        deps=deps,
    )


def pick_body(index, own, oth, out):
    spot = lax.broadcasted_iota(jnp.int32, (1, own.shape[0]), 1)
    here = (index[...] == spot).astype(bf16)
    there = (index[...] - own.shape[0] == spot).astype(bf16)
    out[...] = (dot(here, own[...]) + dot(there, oth[...])).astype(bf16)


def pick(index, own, oth, deps=()):
    count = index.shape[0]
    return run(
        pick_body,
        (1,),
        [(index, None), (own, None), (oth, None)],
        [((count, D), bf16, None)],
        flops=2 * count * GROUP * D,
        deps=deps,
    )[0]


def put_body(index_own, index_oth, own, oth, base, out):
    spot = lax.broadcasted_iota(jnp.int32, (base.shape[0], 1), 0)
    here = (index_own[...] == spot).astype(f32)
    there = (index_oth[...] == spot).astype(f32)
    hit = jnp.sum(here, axis=1, keepdims=True) + jnp.sum(there, axis=1, keepdims=True)
    put = dot(here.astype(bf16), own[...]) + dot(there.astype(bf16), oth[...])
    out[...] = jnp.where(hit > 0.5, put, base[...].astype(f32)).astype(bf16)


def put(index_own, index_oth, own, oth, base, deps=()):
    return run(
        put_body,
        (1,),
        [(index_own, None), (index_oth, None), (own, None), (oth, None), (base, None)],
        [(base.shape, bf16, None)],
        flops=2 * base.shape[0] * KEEP * D,
        deps=deps,
    )[0]


def on_device(
    n_dp,
    tokens,
    conditioning,
    segment_ids,
    kept_rows,
    cotangent,
    mod_first,
    qkv_first,
    proj_first,
    up_first,
    down_first,
    mod_second,
    qkv_second,
    proj_second,
    up_second,
    down_second,
):
    dp_pos = lax.axis_index("dp")
    side = lax.axis_index("tensor")
    core = dp_pos % 2
    bits = n_dp.bit_length() - 1

    def moves(where):
        pairs = []
        for dp in range(n_dp):
            for t in range(2):
                to_dp, to_t = where(dp, t)
                pairs.append((dp * 2 + t, to_dp * 2 + to_t))
        return pairs

    across = moves(lambda dp, t: (dp, 1 - t))
    core_swap = moves(lambda dp, t: (dp ^ 1, t))
    next_swap = moves(lambda dp, t: (dp ^ 2, t))
    turn = moves(lambda dp, t: (dp // 2 * 2 + t, dp % 2))
    deal = moves(lambda dp, t: (dp // 2 * 2 + 1 - t, dp % 2))
    undeal = moves(lambda dp, t: (dp // 2 * 2 + t, 1 - dp % 2))

    def send(value, pairs):
        return lax.ppermute(value, ALL, pairs)

    def after(value, *deps):
        return lax.optimization_barrier((value, *deps))[0]

    def to_owner(rows):
        tiles = rows.reshape(BLOCKS, SPAN // 2, D)
        return send(tiles[0::2], turn), send(tiles[1::2], deal)

    def owned(even, odd, *when):
        even, odd = after(even, *when), after(odd, *when)
        return jnp.where(core == 0, jnp.concatenate([even, odd]), jnp.concatenate([odd, even]))

    def from_owner(rows, begin=(), end=()):
        rows = after(rows.reshape(BLOCKS, SPAN // 2, D), *begin)
        even = after(send(lax.dynamic_slice_in_dim(rows, 2 * core, 3), turn), *end)
        odd = after(send(lax.dynamic_slice_in_dim(rows, 3 * (1 - core), 2), undeal), *end)
        shape = (3, 2, SPAN // 2, D)
        odd = jnp.pad(odd, ((0, 1), (0, 0), (0, 0)))
        even = jnp.broadcast_to(even[:, None], shape)
        odd = jnp.broadcast_to(odd[:, None], shape)
        second = lax.broadcasted_iota(jnp.int32, shape, 1) == 1
        both = jnp.where(second, odd, even).reshape(6 * SPAN // 2, D)
        return both[: BLOCKS * SPAN // 2]

    class Far:
        def __init__(self, near, bit, deps=()):
            self.swap = moves(lambda dp, t: (dp ^ 2**bit, t))
            self.first = send(after(near, *deps), across)

        def hop(self, *deps):
            first = after(self.first, *deps)
            self.third = send(first, self.swap)
            self.second = send(first, core_swap)

        def end(self, *deps):
            return self.first, self.second, self.third, send(after(self.third, *deps), core_swap)

    def part_of(value, axis, bit):
        size = value.shape[axis] // 4
        part = dp_pos // 2**bit % 2 * 2 + core
        return lax.dynamic_slice_in_dim(value, part * size, size, axis)

    numbers = send(jnp.concatenate([kept_rows, segment_ids[::SPAN]]), turn)
    cond = send(jax.nn.silu(conditioning.astype(f32)).astype(bf16), turn)
    wq_one = jnp.transpose(qkv_first, (1, 0, 2))
    wq_two = jnp.transpose(qkv_second, (1, 0, 2))
    place_ref = dp_pos.reshape(1).astype(jnp.int32)
    zero_ref = jnp.zeros((1,), jnp.int32)
    near_part = jnp.concatenate(
        [
            lax.dynamic_slice_in_dim(wq_one, core * HALF, HALF, 1),
            lax.dynamic_slice_in_dim(proj_first, core * HALF, HALF, 1)[None],
        ]
    )
    kept, segs = numbers[:KEEP], numbers[KEEP:]
    kind = jnp.where(segs[3] == segs[0], 0, jnp.where(segs[4] == segs[1], 1, 2)).reshape(1)
    slot_hot = segs[:, None] == jnp.arange(SLOTS, dtype=jnp.int32)[None, :]
    cond_rows = jnp.dot(slot_hot.astype(bf16), cond, preferred_element_type=f32).astype(bf16)

    def table(mod):
        return jnp.dot(cond_rows, mod, preferred_element_type=f32).reshape(BLOCKS, 6, D)

    arrived = to_owner(tokens)
    cond_rows = after(cond_rows, *arrived)
    tab_one, tab_two = table(mod_first), table(mod_second)

    block_of, inside = kept // SPAN, kept % SPAN
    spot = (
        jnp.where(inside // (SPAN // 2) == core, 0, GROUP // 2)
        + block_of * (SPAN // 2)
        + inside % (SPAN // 2)
    ).reshape(BLOCKS, 2, KEEP // (2 * BLOCKS))
    spot_own = lax.dynamic_slice_in_dim(spot, core, 1, 1).reshape(-1)
    spot_oth = lax.dynamic_slice_in_dim(spot, 1 - core, 1, 1).reshape(-1)
    spot_all = jnp.concatenate([spot_own, spot_oth])

    piece = D // n_dp
    row = jnp.arange(D, dtype=jnp.int32)
    turned = jnp.zeros_like(row)
    for bit in range(bits):
        turned = turned + (((row // piece) // 2 ** (bits - 1 - bit)) % 2) * 2**bit
    source = jnp.bitwise_xor(turned, dp_pos) * piece + row % piece
    order = (source[:, None] == row[None, :]).astype(bf16)
    pieces = min(n_dp, 16)
    deep = D // pieces
    which = dp_pos % pieces
    at = which * deep
    proj_piece = lax.dynamic_slice(
        proj_second, (at % HALF, at // HALF * HALF), (deep, HALF)
    )
    up_piece = lax.dynamic_slice_in_dim(up_second, at, deep).reshape(deep, 4, HALF)
    down_pieces = [
        lax.dynamic_slice_in_dim(down_second, row * D + at, deep).reshape(deep, 2, HALF)
        for row in range(2)
    ]
    pieces_two = jnp.concatenate(
        [
            lax.dynamic_slice_in_dim(wq_two, at, deep, 1),
            proj_piece[None],
            jnp.transpose(up_piece, (1, 0, 2)),
        ]
        + [down_pieces[row][None, :, column] for column in range(2) for row in range(2)]
    )
    piece_two = send(after(pieces_two, *arrived), across)
    w_near = send(after(near_part, *arrived), across)
    own = owned(*arrived, tab_one, tab_two, piece_two, order)
    oth = send(own, core_swap)

    def add(*terms):
        return functools.reduce(lambda p, q: p + q, [t.astype(f32) for t in terms])

    quarter = HALF // 2

    class Total:
        def cores(self, keep, away):
            got = send(away, core_swap)
            self.keep_n, self.keep_r, self.got_n, self.got_r = keep[0], keep[1], got[0], got[1]
            return self

        def cores_far(self, keep, away):
            self.keep_r, self.got_r = keep, send(away, core_swap)
            return self

        def cores_near(self, keep, away):
            self.keep_n, self.got_n = keep, send(away, core_swap)
            return self

        def far(self, *when):
            away = add(self.keep_r, after(self.got_r, *when)).astype(bf16)
            self.got = send(away, across)
            return (away,)

        def chips(self, *when):
            return add(self.keep_n, self.got_n, after(self.got, *when)).astype(bf16)

        def near(self, *when):
            terms = (self.keep_n, self.got_n, after(self.got, *when))
            away = add(*[t[quarter:] for t in terms]).astype(bf16)
            self.got = send(away, next_swap)
            self.terms = tuple(t[:quarter] for t in terms)
            return (away,)

        def sum(self, *when):
            return add(*self.terms, after(self.got, *when))

    class Rest:
        def __init__(self, acc, bit=2):
            self.acc, self.got, self.bit = acc, None, bit

        def next(self, *when):
            if self.bit == bits:
                return ()
            acc = self.acc
            if self.got is not None:
                acc = acc + after(self.got, *when).astype(f32)
            self.acc = acc
            size = self.acc.shape[0] // 2
            away = self.acc[size:].astype(bf16)
            bit = self.bit
            self.got = send(away, moves(lambda dp, t: (dp ^ 2**bit, t)))
            self.acc = self.acc[:size]
            self.bit = bit + 1
            return (away,)

        def sum(self, *when):
            return self.acc + after(self.got, *when).astype(f32)

        def end(self, *when):
            while self.bit < bits:
                self.next(*when)
            return self.acc + after(self.got, *when).astype(f32)

    normed_one, *near_one = project_first(own, oth, tab_one, wq_one)
    ups_one = Far(part_of(up_first, 1, 1), 1, (own,))
    downs_one = Far(part_of(down_first, 0, 2), 2, (own,))
    mixed_one_n = attend(kind, *near_one)
    w_parts = (w_near, send(after(w_near, mixed_one_n), core_swap))
    w_two_far = lax.all_gather(
        after(piece_two, own)[None],
        "dp",
        axis=0,
        tiled=True,
        axis_index_groups=[
            list(range(first, first + pieces)) for first in range(0, n_dp, pieces)
        ],
    )
    far_two_mlp = ([w_two_far] * 4, [w_two_far] * 4)
    w_one_far, *far_one = project_parts(
        place_ref, normed_one, w_parts, deps=(mixed_one_n,)
    )
    mixed_one_r = attend(kind, *far_one)
    ups_one.hop(mixed_one_r)
    downs_one.hop(mixed_one_r)
    attn_one, middle_one, normed_mlp_one, u_one_n, act_one_n, acc = feed_near(
        mixed_one_n, mixed_one_r, proj_first, w_one_far, own, tab_one, up_first, down_first
    )
    ups_one, downs_one = ups_one.end(normed_mlp_one), downs_one.end(normed_mlp_one)
    mlp_one = (up_first, down_first, ups_one, downs_one)
    cot_parts = to_owner(after(cotangent, normed_mlp_one))
    u_one_r, act_one_r, mlp_out_one, out_one = feed_far(
        place_ref, normed_mlp_one, acc, middle_one, tab_one, ups_one, downs_one
    )
    first_own = out_one.reshape(-1, D)
    first_oth = send(first_own, core_swap)

    routed = pick(spot_all[:, None], first_own, first_oth)
    routed_own, routed_oth = routed.reshape(2, BLOCKS, KEEP // (2 * BLOCKS), D)
    normed_two, *near_two = project_first(routed_own, routed_oth, tab_two, wq_two)
    mixed_two_n = attend(kind, *near_two)
    far_two = project_next(normed_two, w_two_far, deps=(mixed_two_n,))
    mixed_two_r = attend(kind, *far_two)
    cot_own = owned(*cot_parts, mixed_two_r)
    cot_oth = send(cot_own, core_swap)
    attn_two, middle_two, normed_mlp_two, u_two_n, act_two_n, acc = feed_near(
        mixed_two_n, mixed_two_r, proj_second, w_two_far, routed_own, tab_two, up_second,
        down_second,
    )
    first_out = from_owner(out_one, (mixed_two_r,), (normed_mlp_two,))
    mlp_two = (up_second, down_second, *far_two_mlp)
    u_two_r, act_two_r, mlp_out_two, out_two = feed_far(
        zero_ref, normed_mlp_two, acc, middle_two, tab_two, *mlp_two[2:], deps=(first_out,)
    )
    second_own = out_two.reshape(-1, D)
    second_oth = send(second_own, core_swap)
    cot_routed = pick(
        spot_own[:, None], cot_own.reshape(-1, D), cot_oth.reshape(-1, D), deps=(second_own,)
    ).reshape(routed_own.shape)

    g_keep, g_send, d_mlp, d_gate_two = down_back(
        zero_ref, cot_routed, tab_two, mlp_out_two, order, act_two_n, act_two_r
    )
    down_two = Total().cores(g_keep, g_send)
    saved = (attn_two, middle_two, normed_mlp_two, u_two_n, u_two_r)
    g_keep, g_send, p_keep, p_send, d_middle, d_mix_n, d_mix_r, d_mod_two = up_back(
        zero_ref, cot_routed, tab_two, d_mlp, saved, mlp_two, proj_second, w_two_far, mixed_two_n,
        mixed_two_r, order,
    )
    up_two = Total().cores(g_keep, g_send)
    sent = down_two.far(d_mix_r)
    grads_r = attend_back(kind, *far_two, d_mix_r, deps=sent)
    sent = up_two.far(grads_r[0])
    qr_keep, qr_send, normed_t, acc = qkv_back(
        True, 1, grads_r, w_two_far, normed_two, order, None, None, p_keep, p_send, deps=sent
    )
    qkv_two = Total().cores_far(qr_keep, qr_send)
    grads_n = attend_back(kind, *near_two, d_mix_n, deps=(acc, down_two.got))
    sent = qkv_two.far(grads_n[0])
    qn_keep, qn_send, d_own, d_oth = qkv_back(
        False, 0, grads_n, wq_two, normed_two, None, normed_t, acc, p_keep, p_send, deps=sent
    )
    d_got = send(d_oth, core_swap)
    qkv_two.cores_near(qn_keep, qn_send)
    d_two, d_mod_two_a = finish(
        d_own, d_got, routed_own, tab_two, d_middle
    )
    d_two_own = d_two.reshape(-1, D)
    d_two_oth = send(d_two_own, core_swap)

    def slot_sums(*parts):
        per_block = jnp.concatenate(parts, axis=1).reshape(BLOCKS, -1)
        return lax.dot_general(
            slot_hot.astype(f32),
            per_block,
            (((0,), (0,)), ((), ())),
            precision=lax.Precision.HIGHEST,
        ).astype(bf16)

    routed_rows = put(
        spot_own[None], spot_oth[None], second_own, second_oth, first_own, deps=(d_two_own,)
    )
    d_first = put(
        spot_own[None], spot_oth[None], d_two_own, d_two_oth, cot_own.reshape(-1, D),
        deps=(routed_rows,),
    ).reshape(own.shape)
    g_keep, g_send, d_mlp, d_gate = down_back(
        place_ref, d_first, tab_one, mlp_out_one, order, act_one_n, act_one_r, deps=(up_two.got,)
    )
    down_one = Total().cores(g_keep, g_send)
    mlp_rest_two = Rest(jnp.concatenate([t.chips(d_mlp) for t in (down_two, up_two)], axis=1), 1)
    sent = mlp_rest_two.next()
    saved = (attn_one, middle_one, normed_mlp_one, u_one_n, u_one_r)
    g_keep, g_send, p_keep, p_send, d_middle, d_mix_n, d_mix_r, d_mod = up_back(
        place_ref, d_first, tab_one, d_mlp, saved, mlp_one, proj_first, w_one_far, mixed_one_n,
        mixed_one_r, order, deps=sent,
    )
    up_one = Total().cores(g_keep, g_send)
    qkv_rest_two = Rest(qkv_two.chips(d_mix_r), 1)
    sent = (*down_one.far(d_mix_r), *qkv_rest_two.next())
    early = lax.all_gather(
        jnp.concatenate(
            [cond, slot_sums(d_mod_two_a, d_mod_two, d_gate_two), slot_sums(d_mod, d_gate)], axis=1
        ),
        ALL,
        axis=0,
        tiled=True,
    )
    grads_r = attend_back(kind, *far_one, d_mix_r, deps=sent)
    rest_two = Rest(
        jnp.concatenate([t.sum(grads_r[0]) for t in (mlp_rest_two, qkv_rest_two)], axis=1)
    )
    sent = (*up_one.far(grads_r[0]), *rest_two.next())
    qr_keep, qr_send, normed_t, acc = qkv_back(
        True, 1, grads_r, w_one_far, normed_one, order, None, None, p_keep, p_send,
        deps=sent,
    )
    qkv_one = Total().cores_far(qr_keep, qr_send)
    sent = down_one.near(acc)
    grads_n = attend_back(kind, *near_one, d_mix_n, deps=sent)
    done = grads_n[0]
    sent = (*qkv_one.far(done), *up_one.near(done), *rest_two.next(done))
    qn_keep, qn_send, d_own, d_oth = qkv_back(
        False, 0, grads_n, wq_one, normed_one, None, normed_t, acc, p_keep, p_send, deps=sent
    )
    d_got = send(d_oth, core_swap)
    qkv_one.cores_near(qn_keep, qn_send)
    routed_out = from_owner(routed_rows, (grads_r[0],), (d_own,))
    mlp_rest = Rest(jnp.concatenate([down_one.sum(d_own), up_one.sum(d_own)], axis=1))
    sent = (*mlp_rest.next(), routed_out)
    d_one, d_mod_a = finish(d_own, d_got, own, tab_one, d_middle, deps=(*sent, qkv_one.got_n))

    last = qkv_one.near(d_one)
    late = after(jnp.pad(slot_sums(d_mod_a), ((0, 8 - SLOTS), (0, 0))), *last)
    late = (late.astype(f32) + send(late, core_swap).astype(f32)).astype(bf16)[None]
    sources = jnp.array([dp_pos * 2 + side])

    def doubled(late, sources, mask):
        pairs = moves(lambda dp, t: ((dp * 2 + t ^ mask) // 2, (t ^ mask) % 2))
        late = jnp.concatenate([late, send(late, pairs)])
        return late, jnp.concatenate([sources, jnp.bitwise_xor(sources, mask)])

    late, sources = doubled(late, sources, 1)
    qkv_rest = Rest(qkv_one.sum(late))
    last = qkv_rest.next()
    mlp_rest.next(*last)
    for bit in range(2, bits):
        late, sources = doubled(after(late, *last), sources, 2**bit)
        last = qkv_rest.next(late) or last
    late, sources = doubled(after(late, *last), sources, 2**bits)
    input_grad = from_owner(d_one, (), last).astype(f32)
    early = after(early, *last)
    mlp_total = mlp_rest.end(*last)
    total_two = rest_two.end(*last)
    qkv_total = qkv_rest.end(late)

    mod_rows = D // (n_dp * 2)
    mine = lax.dynamic_slice_in_dim(early[:, :D], (dp_pos * 2 + side) * mod_rows, mod_rows, 1)
    mine_late = jnp.pad(
        mine.reshape(-1, SLOTS, mod_rows)[sources], ((0, 0), (0, 8 - SLOTS), (0, 0))
    ).reshape(-1, mod_rows)
    mod_two_end = 7 * D
    mod_one = jnp.concatenate(
        [
            dot_rows(mine_late, late.reshape(-1, 2 * D)),
            dot_rows(mine, early[:, mod_two_end:]),
        ],
        axis=1,
    )
    mod_two = dot_rows(mine, early[:, D:mod_two_end])
    wide = 2 * TILE

    def placed(attention, down, up):
        qkv = attention[:, : 3 * HALF].reshape(piece, 3, HALF)
        return qkv, attention[:, 3 * HALF :].T, up, down.T

    return (
        first_out,
        routed_out,
        input_grad,
        mod_one,
        *placed(qkv_total, mlp_total[:, :wide], mlp_total[:, wide:]),
        mod_two,
        *placed(
            total_two[:, 2 * wide :].astype(f32),
            total_two[:, :wide].astype(f32),
            total_two[:, wide : 2 * wide].astype(f32),
        ),
    )


def solution(mesh):
    n_dp = mesh.shape["dp"]
    return jax.shard_map(
        functools.partial(on_device, n_dp),
        mesh=mesh,
        in_specs=(
            P(("dp", "tensor"), None),
            P("dp", None),
            P("dp"),
            P("dp"),
            P(("dp", "tensor"), None),
            P(),
            P(None, None, "tensor"),
            P("tensor", None),
            P(None, "tensor"),
            P("tensor", None),
            P(),
            P(None, None, "tensor"),
            P("tensor", None),
            P(None, "tensor"),
            P("tensor", None),
        ),
        out_specs=(
            P(("dp", "tensor"), None),
            P(("dp", "tensor"), None),
            P(("dp", "tensor"), None),
            P(("dp", "tensor"), None),
            P("dp", None, "tensor"),
            P("tensor", "dp"),
            P("dp", "tensor"),
            P("tensor", "dp"),
            P(("dp", "tensor"), None),
            P("dp", None, "tensor"),
            P("tensor", "dp"),
            P("dp", "tensor"),
            P("tensor", "dp"),
        ),
        check_vma=False,
    )
```
